32 devices in a mesh: ctx: 16 (over z, x, core), fsdp: 2 (over y).
Axes of the slice: x: 2, y: 2, z: 4, core: 2. Of those that a mesh axis runs over, the one named last changes fastest.
Arguments:
- tokens: bfloat16 [2, 4096, 1024], P('fsdp', 'ctx'), may hold values from -6 to 6
- cotangent: bfloat16 [2, 4096, 1024], P('fsdp', 'ctx'), may hold values from -6 to 6
- first_gain: bfloat16 [1024], P('fsdp'), may hold values from 0.5 to 1.5
- first_shift: bfloat16 [1024], P('fsdp'), may hold values from -1.5 to 1.5
- second_gain: bfloat16 [1024], P('fsdp'), may hold values from 0.5 to 1.5
- second_shift: bfloat16 [1024], P('fsdp'), may hold values from -1.5 to 1.5
- joint_weight: bfloat16 [1024, 3072], P('fsdp'), may hold values from -0.1875 to 0.1875
- joint_bias: bfloat16 [3072], P('fsdp'), may hold values from -1.5 to 1.5
- dense_weight: bfloat16 [1024, 1024], P('fsdp'), may hold values from -6 to 6
- dense_bias: bfloat16 [1024], P('fsdp'), may hold values from -1.5 to 1.5
- expand_weight: bfloat16 [1024, 4096], P('fsdp'), may hold values from -0.1875 to 0.1875
- expand_bias: bfloat16 [4096], P('fsdp'), may hold values from -1.5 to 1.5
- shrink_weight: bfloat16 [4096, 1024], P('fsdp'), may hold values from -0.09375 to 0.09375
- shrink_bias: bfloat16 [1024], P('fsdp'), may hold values from -1.5 to 1.5
- block_order: int32 [32], replicated, may hold values from 0 to 31, as said below
Outputs:
- layer_output: bfloat16 [2, 4096, 1024], P('fsdp', 'ctx')
- tokens_grad: bfloat16 [2, 4096, 1024], P('fsdp', 'ctx')
- first_gain_grad: float32 [1024], P('fsdp')
- first_shift_grad: float32 [1024], P('fsdp')
- second_gain_grad: float32 [1024], P('fsdp')
- second_shift_grad: float32 [1024], P('fsdp')
- joint_weight_grad: float32 [1024, 3072], P('fsdp')
- joint_bias_grad: float32 [3072], P('fsdp')
- dense_weight_grad: float32 [1024, 1024], P('fsdp')
- dense_bias_grad: float32 [1024], P('fsdp')
- expand_weight_grad: float32 [1024, 4096], P('fsdp')
- expand_bias_grad: float32 [4096], P('fsdp')
- shrink_weight_grad: float32 [4096, 1024], P('fsdp')
- shrink_bias_grad: float32 [1024], P('fsdp')
The draws below stay inside these ranges and needn't reach their ends.
Inputs may be any that keep to these rules, and one draw needn't show every extreme that they name: `block_order`: slots 2i and 2i + 1 hold two blocks b and 31 - b in either order; every block of 0 to 31 is held once.
All inputs are finite; a program needn't handle non-finite values.
Results may differ from the reference program's by a relative error of at most 0.018.
Values may be sent and summed in bfloat16 or wider, within the bound.
No kernel may reach another device: no remote copies, remote signals or barrier semaphores. Data moves between devices by JAX's collectives and lax.ppermute only.
A program may use at most 256 MiB of HBM per device.

```python
import jax
import jax.numpy as jnp
from jax import lax

D = 1024
HEADS = 16
HEAD_DIM = 64
ROT = 16
FF = 4096
TOK_DEV = 256
BLK = 128
SEQ = 4096
SEQS = 2
N_CTX = 16


def draw_block_order(key, part):
    key = jax.random.fold_in(key, 7)
    first, second = jax.random.split(key)
    order = jax.random.permutation(first, N_CTX).astype(jnp.int32)
    flips = jax.random.randint(second, (N_CTX,), 0, 2, dtype=jnp.int32)
    mirror = 2 * N_CTX - 1 - order
    leading = jnp.where(flips == 1, mirror, order)
    trailing = jnp.where(flips == 1, order, mirror)
    return jnp.stack([leading, trailing], 1).reshape(2 * N_CTX).astype(jnp.int32)


def levels(rng, dims, cuts, least, high):
    factor_of = 1.0
    for dim, parts in cuts:
        heights = jax.random.uniform(jax.random.fold_in(jax.random.fold_in(rng, 6), dim), (parts,), jnp.float32, least / len(cuts), high / len(cuts))
        factor_of = factor_of * jnp.repeat(jnp.exp(heights), dims[dim] // parts).reshape((-1,) + (1,) * (len(dims) - 1 - dim))
    return factor_of


def normal_values(key, shape, width, most, cuts=(), kind=jnp.bfloat16):
    level = levels(key, shape, cuts, -0.22, 0.18) if cuts else 1.0
    values = jax.random.normal(key, shape, jnp.float32) * width * level
    return jnp.minimum(jnp.maximum(values, -most), most).astype(kind)


def setup_inputs(seed: int = 0) -> dict:
    streams_of = jax.random.split(jax.random.key(seed), 16)
    return {
        "tokens": normal_values(streams_of[0], (SEQS, SEQ, D), 1.0, 6.0, ((0, 2), (1, 16))),
        "cotangent": normal_values(streams_of[1], (SEQS, SEQ, D), 1.0, 6.0, ((0, 2), (1, 16))),
        "first_gain": jnp.clip(1.0 + 0.1 * jax.random.normal(streams_of[2], (D,), jnp.float32), 0.5, 1.5).astype(jnp.bfloat16),
        "first_shift": normal_values(streams_of[3], (D,), 0.3, 1.5, ((0, 2),)),
        "second_gain": jnp.clip(1.0 + 0.1 * jax.random.normal(streams_of[4], (D,), jnp.float32), 0.5, 1.5).astype(jnp.bfloat16),
        "second_shift": normal_values(streams_of[5], (D,), 0.3, 1.5, ((0, 2),)),
        "joint_weight": normal_values(streams_of[6], (D, 3 * D), D ** -0.5, 0.1875, ((0, 2),)),
        "joint_bias": normal_values(streams_of[7], (3 * D,), 0.3, 1.5, ((0, 2),)),
        "dense_weight": normal_values(streams_of[8], (D, D), (max(1, 2 * D // (TOK_DEV * N_CTX))) ** -0.5, 6.0, ((0, 2),)),
        "dense_bias": normal_values(streams_of[9], (D,), 0.3, 1.5, ((0, 2),)),
        "expand_weight": normal_values(streams_of[10], (D, FF), D ** -0.5, 0.1875, ((0, 2),)),
        "expand_bias": normal_values(streams_of[11], (FF,), 0.3, 1.5, ((0, 2),)),
        "shrink_weight": normal_values(streams_of[12], (FF, D), FF ** -0.5, 0.09375, ((0, 2),)),
        "shrink_bias": normal_values(streams_of[13], (D,), 0.3, 1.5, ((0, 2),)),
        "block_order": draw_block_order(jax.random.fold_in(streams_of[15], 71), 0),
    }


@jax.custom_vjp
def low(v):
    return lax.optimization_barrier(v.astype(jnp.bfloat16)).astype(jnp.float32)

@jax.custom_vjp
def low_back(v):
    return v

def low_keep(v):
    return (low(v), None)

def low_pass(kept, grad):
    return (grad,)

def back_keep(v):
    return (v, None)

def back_low(kept, grad):
    return (low(grad),)
low.defvjp(low_keep, low_pass)
low_back.defvjp(back_keep, back_low)
epsilon = 1e-05
negative = -1e+30

def normalize(values, gain, shift):
    center = values - lax.optimization_barrier(jnp.mean(values, -1, keepdims=True))
    spread = lax.optimization_barrier(jnp.mean(center * center, -1, keepdims=True))
    return center * lax.rsqrt(spread + epsilon) * gain + shift

def turn_tables(positions):
    inverse = jnp.power(10000.0, -2.0 * jnp.arange(ROT // 2, dtype=jnp.float32) / ROT)
    angles = positions.astype(jnp.float32)[:, None] * inverse[None, :]
    angles = jnp.concatenate([angles, angles], -1)[:, None, :]
    return (jnp.cos(angles), jnp.sin(angles))

def rotate(values, cosine, sine):
    half = ROT // 2
    front = values[..., :ROT]
    turned = jnp.concatenate([-front[..., half:], front[..., :half]], -1)
    return jnp.concatenate([front * cosine + turned * sine, values[..., ROT:]], -1)

def attend(queries, keys, values, positions):
    length = queries.shape[0]
    span = min(512, length)
    scale = HEAD_DIM ** (-0.5)

    def block(items):
        rows, spots = items
        scores = jnp.einsum('qhd,khd->hqk', rows, keys, precision=lax.Precision.HIGHEST) * scale
        scores = low_back(scores)
        visible = (spots[:, None] >= positions[None, :])[None]
        scores = jnp.where(visible, scores, negative)
        weights = low(jax.nn.softmax(scores, -1))
        return jnp.einsum('hqk,khd->qhd', weights, values, precision=lax.Precision.HIGHEST)
    mixed = lax.map(jax.checkpoint(block), (queries.reshape(length // span, span, HEADS, HEAD_DIM), positions.reshape(length // span, span)))
    return mixed.reshape(length, HEADS * HEAD_DIM)

def forward(inputs, first_gain, first_shift, second_gain, second_shift, joint_weight, joint_bias, dense_weight, dense_bias, expand_weight, expand_bias, shrink_weight, shrink_bias, positions):
    count = inputs.shape[0]
    highest = lax.Precision.HIGHEST
    normed_one = low(normalize(inputs, first_gain, first_shift))
    normed_two = low(normalize(inputs, second_gain, second_shift))
    joint = low_back(jnp.dot(normed_one, joint_weight, precision=highest) + joint_bias)
    cosine, sine = turn_tables(positions)
    shape = (count, SEQ, HEADS, HEAD_DIM)
    queries = low(rotate(joint[..., :D].reshape(shape), cosine, sine))
    keys = low(rotate(joint[..., D:2 * D].reshape(shape), cosine, sine))
    values = low(joint[..., 2 * D:].reshape(shape))
    mixed = lax.map(lambda items: attend(items[0], items[1], items[2], positions), (queries, keys, values))
    mixed = low_back(low(mixed))
    attention = jnp.dot(mixed, dense_weight, precision=highest) + dense_bias
    expanded = low_back(jnp.dot(normed_two, expand_weight, precision=highest) + expand_bias)
    activated = low(jax.nn.gelu(expanded, approximate=False))
    branch = jnp.dot(activated, shrink_weight, precision=highest) + shrink_bias
    return inputs + attention + branch

def reference(tokens, cotangent, first_gain, first_shift, second_gain, second_shift, joint_weight, joint_bias, dense_weight, dense_bias, expand_weight, expand_bias, shrink_weight, shrink_bias, block_order):
    slots = jnp.arange(SEQ, dtype=jnp.int32)
    positions = block_order[slots // BLK] * BLK + slots % BLK
    params = (first_gain.astype(jnp.float32), first_shift.astype(jnp.float32), second_gain.astype(jnp.float32), second_shift.astype(jnp.float32), joint_weight.astype(jnp.float32), joint_bias.astype(jnp.float32), dense_weight.astype(jnp.float32), dense_bias.astype(jnp.float32), expand_weight.astype(jnp.float32), expand_bias.astype(jnp.float32), shrink_weight.astype(jnp.float32), shrink_bias.astype(jnp.float32))

    def layer(inputs, *weights):
        return forward(inputs, *weights, positions)
    output, pull = jax.vjp(layer, tokens.astype(jnp.float32), *params)
    grads = pull(cotangent.astype(jnp.float32))
    return (output.astype(jnp.bfloat16), grads[0].astype(jnp.bfloat16), grads[1], grads[2], grads[3], grads[4], grads[5], grads[6], grads[7], grads[8], grads[9], grads[10], grads[11], grads[12])
```

```python
import functools

import jax
import jax.numpy as jnp
from jax import lax
from jax.experimental import pallas as pl
from jax.experimental.pallas import tpu as pltpu
from jax.sharding import PartitionSpec as P

HEADS = 16
ROT = 16


epsilon = 1e-05
negative = -1e30


def normalize(values, gain, shift):
    center = values - jnp.mean(values, -1, keepdims=True)
    spread = jnp.mean(center * center, -1, keepdims=True)
    return center * lax.rsqrt(spread + epsilon) * gain + shift


def turn_tables(positions):
    inverse = jnp.power(10000.0, -2.0 * jnp.arange(ROT // 2, dtype=jnp.float32) / ROT)
    angles = positions.astype(jnp.float32)[:, None] * inverse[None, :]
    angles = jnp.concatenate([angles, angles], -1)[:, None, :]
    return (jnp.cos(angles), jnp.sin(angles))


def rotate(values, cosine, sine):
    half = ROT // 2
    front = values[..., :ROT]
    turned = jnp.concatenate([-front[..., half:], front[..., :half]], -1)
    return jnp.concatenate([front * cosine + turned * sine, values[..., ROT:]], -1)


def contract(left, right, left_dim, right_dim):
    return lax.dot_general(
        left, right, (((left_dim,), (right_dim,)), ((), ())), preferred_element_type=jnp.float32
    )


def shards(
    tokens,
    cotangent,
    first_gain,
    first_shift,
    second_gain,
    second_shift,
    joint_weight,
    joint_bias,
    dense_weight,
    dense_bias,
    expand_weight,
    expand_bias,
    shrink_weight,
    shrink_bias,
    block_order,
):
    rows = tokens.shape[1]
    width = tokens.shape[2]
    head_dim = width // HEADS
    scale = head_dim ** (-0.5)
    groups = lax.axis_size("ctx")
    half_rows = rows // 2
    (
        gain_one,
        shift_one,
        gain_two,
        shift_two,
        joint_full,
        joint_shift,
        dense_full,
        dense_shift,
        expand_full,
        expand_shift,
        shrink_full,
        shrink_shift,
    ) = (
        lax.all_gather(first_gain, "fsdp", axis=0, tiled=True),
        lax.all_gather(first_shift, "fsdp", axis=0, tiled=True),
        lax.all_gather(second_gain, "fsdp", axis=0, tiled=True),
        lax.all_gather(second_shift, "fsdp", axis=0, tiled=True),
        lax.all_gather(joint_weight, "fsdp", axis=0, tiled=True),
        lax.all_gather(joint_bias, "fsdp", axis=0, tiled=True),
        lax.all_gather(dense_weight, "fsdp", axis=0, tiled=True),
        lax.all_gather(dense_bias, "fsdp", axis=0, tiled=True),
        lax.all_gather(expand_weight, "fsdp", axis=0, tiled=True),
        lax.all_gather(expand_bias, "fsdp", axis=0, tiled=True),
        lax.all_gather(shrink_weight, "fsdp", axis=0, tiled=True),
        lax.all_gather(shrink_bias, "fsdp", axis=0, tiled=True),
    )
    gain_one = gain_one.astype(jnp.float32)
    shift_one = shift_one.astype(jnp.float32)
    gain_two = gain_two.astype(jnp.float32)
    shift_two = shift_two.astype(jnp.float32)
    all_positions = (
        block_order[:, None] * half_rows + jnp.arange(half_rows, dtype=jnp.int32)[None, :]
    ).reshape(rows * groups)
    positions = lax.dynamic_slice_in_dim(all_positions, lax.axis_index("ctx") * rows, rows)
    cosine, sine = turn_tables(positions)
    visible = positions[:, None] >= all_positions[None, :]
    inputs = tokens[0].astype(jnp.float32)
    normed_one = normalize(inputs, gain_one, shift_one).astype(jnp.bfloat16)
    normed_two = normalize(inputs, gain_two, shift_two).astype(jnp.bfloat16)
    joint = jnp.dot(
        normed_one, joint_full, preferred_element_type=jnp.float32
    ) + joint_shift.astype(jnp.float32)
    queries = (
        rotate(joint[:, :width].reshape(rows, HEADS, head_dim), cosine, sine)
        .reshape(rows, width)
        .astype(jnp.bfloat16)
    )
    key_rows = (
        rotate(joint[:, width : 2 * width].reshape(rows, HEADS, head_dim), cosine, sine)
        .reshape(rows, width)
        .astype(jnp.bfloat16)
    )
    value_rows = joint[:, 2 * width :].astype(jnp.bfloat16)
    all_keys, all_values = (
        lax.all_gather(key_rows, "ctx", axis=0, tiled=True),
        lax.all_gather(value_rows, "ctx", axis=0, tiled=True),
    )

    def head_scores(head, key_source):
        query = lax.dynamic_slice_in_dim(queries, head * head_dim, head_dim, 1)
        key_cols = lax.dynamic_slice_in_dim(key_source, head * head_dim, head_dim, 1)
        scores = contract(query, key_cols, 1, 1) * scale
        return (query, key_cols, jnp.where(visible, scores, negative))

    def head_forward(head):
        query, key_cols, scores = head_scores(head, all_keys)
        top = jnp.max(scores, -1, keepdims=True)
        total = jnp.sum(jnp.exp(scores - top), -1, keepdims=True)
        log_total = top + jnp.log(total)
        weights = jnp.exp(scores - log_total).astype(jnp.bfloat16)
        value_cols = lax.dynamic_slice_in_dim(all_values, head * head_dim, head_dim, 1)
        return (jnp.dot(weights, value_cols, preferred_element_type=jnp.float32), log_total[:, 0])

    mixed, log_totals = lax.map(head_forward, jnp.arange(HEADS))
    attended = jnp.transpose(mixed, (1, 0, 2)).reshape(rows, width).astype(jnp.bfloat16)
    expanded = jnp.dot(
        normed_two, expand_full, preferred_element_type=jnp.float32
    ) + expand_shift.astype(jnp.float32)
    activated = jax.nn.gelu(expanded, approximate=False).astype(jnp.bfloat16)
    output = (
        inputs
        + jnp.dot(attended, dense_full, preferred_element_type=jnp.float32)
        + dense_shift.astype(jnp.float32)
    )
    output = (
        output
        + jnp.dot(activated, shrink_full, preferred_element_type=jnp.float32)
        + shrink_shift.astype(jnp.float32)
    )
    upstream = cotangent[0]
    upstream_float = upstream.astype(jnp.float32)
    column_sum = jnp.sum(upstream_float, 0)
    dense_grad = contract(attended, upstream, 0, 0)
    shrink_grad = contract(activated, upstream, 0, 0)
    act_grad = contract(upstream, shrink_full, 1, 1)
    _, gelu_pull = jax.vjp(lambda value: jax.nn.gelu(value, approximate=False), expanded)
    expand_delta = gelu_pull(act_grad)[0].astype(jnp.bfloat16)
    expand_grad = contract(normed_two, expand_delta, 0, 0)
    expand_bias_grad = jnp.sum(expand_delta.astype(jnp.float32), 0)
    normed_two_grad = contract(expand_delta, expand_full, 1, 1)
    _, pull_two = jax.vjp(normalize, inputs, gain_two, shift_two)
    input_two, gain_two_grad, shift_two_grad = pull_two(normed_two_grad)
    attended_grad = contract(upstream, dense_full, 1, 1).astype(jnp.bfloat16)
    key_source, value_source = (all_keys, all_values)

    def head_backward(items):
        head, log_total = items
        query, key_cols, scores = head_scores(head, key_source)
        probs = jnp.exp(scores - log_total[:, None])
        value_cols = lax.dynamic_slice_in_dim(value_source, head * head_dim, head_dim, 1)
        out_grad = lax.dynamic_slice_in_dim(attended_grad, head * head_dim, head_dim, 1)
        prob_grad = contract(out_grad, value_cols, 1, 1)
        inner = jnp.sum(probs * prob_grad, -1, keepdims=True)
        score_grad = (probs * (prob_grad - inner)).astype(jnp.bfloat16)
        query_grad = jnp.dot(score_grad, key_cols, preferred_element_type=jnp.float32) * scale
        key_grad = contract(score_grad, query, 0, 0) * scale
        value_grad = contract(probs.astype(jnp.bfloat16), out_grad, 0, 0)
        return (query_grad, key_grad, value_grad)

    query_grads, key_grads, value_grads = lax.map(head_backward, (jnp.arange(HEADS), log_totals))
    key_sums, value_sums = (
        lax.psum_scatter(
            key_grads.astype(jnp.bfloat16), "ctx", scatter_dimension=1, tiled=True
        ).astype(jnp.float32),
        lax.psum_scatter(
            value_grads.astype(jnp.bfloat16), "ctx", scatter_dimension=1, tiled=True
        ).astype(jnp.float32),
    )
    query_back = rotate(jnp.transpose(query_grads, (1, 0, 2)), cosine, -sine).reshape(rows, width)
    key_back = rotate(jnp.transpose(key_sums, (1, 0, 2)), cosine, -sine).reshape(rows, width)
    value_back = jnp.transpose(value_sums, (1, 0, 2)).reshape(rows, width)
    joint_delta = jnp.concatenate([query_back, key_back, value_back], 1).astype(jnp.bfloat16)
    joint_grad = contract(normed_one, joint_delta, 0, 0)
    joint_bias_grad = jnp.sum(joint_delta.astype(jnp.float32), 0)
    normed_one_grad = contract(joint_delta, joint_full, 1, 1)
    _, pull_one = jax.vjp(normalize, inputs, gain_one, shift_one)
    input_one, gain_one_grad, shift_one_grad = pull_one(normed_one_grad)
    tokens_grad = (upstream_float + input_one + input_two).astype(jnp.bfloat16)
    (
        gain_one_part,
        shift_one_part,
        gain_two_part,
        shift_two_part,
        joint_part,
        joint_bias_part,
        dense_part,
        column_part,
        expand_part,
        expand_bias_part,
        shrink_part,
    ) = (
        lax.psum_scatter(
            gain_one_grad.astype(jnp.bfloat16), "fsdp", scatter_dimension=0, tiled=True
        ).astype(jnp.float32),
        lax.psum_scatter(
            shift_one_grad.astype(jnp.bfloat16), "fsdp", scatter_dimension=0, tiled=True
        ).astype(jnp.float32),
        lax.psum_scatter(
            gain_two_grad.astype(jnp.bfloat16), "fsdp", scatter_dimension=0, tiled=True
        ).astype(jnp.float32),
        lax.psum_scatter(
            shift_two_grad.astype(jnp.bfloat16), "fsdp", scatter_dimension=0, tiled=True
        ).astype(jnp.float32),
        lax.psum_scatter(
            joint_grad.astype(jnp.bfloat16), "fsdp", scatter_dimension=0, tiled=True
        ).astype(jnp.float32),
        lax.psum_scatter(
            joint_bias_grad.astype(jnp.bfloat16), "fsdp", scatter_dimension=0, tiled=True
        ).astype(jnp.float32),
        lax.psum_scatter(
            dense_grad.astype(jnp.bfloat16), "fsdp", scatter_dimension=0, tiled=True
        ).astype(jnp.float32),
        lax.psum_scatter(
            column_sum.astype(jnp.bfloat16), "fsdp", scatter_dimension=0, tiled=True
        ).astype(jnp.float32),
        lax.psum_scatter(
            expand_grad.astype(jnp.bfloat16), "fsdp", scatter_dimension=0, tiled=True
        ).astype(jnp.float32),
        lax.psum_scatter(
            expand_bias_grad.astype(jnp.bfloat16), "fsdp", scatter_dimension=0, tiled=True
        ).astype(jnp.float32),
        lax.psum_scatter(
            shrink_grad.astype(jnp.bfloat16), "fsdp", scatter_dimension=0, tiled=True
        ).astype(jnp.float32),
    )
    (
        gain_one_total,
        shift_one_total,
        gain_two_total,
        shift_two_total,
        joint_total,
        joint_bias_total,
        dense_total,
        column_total,
        expand_total,
        expand_bias_total,
        shrink_total,
    ) = (
        lax.psum(gain_one_part.astype(jnp.bfloat16), "ctx").astype(jnp.float32),
        lax.psum(shift_one_part.astype(jnp.bfloat16), "ctx").astype(jnp.float32),
        lax.psum(gain_two_part.astype(jnp.bfloat16), "ctx").astype(jnp.float32),
        lax.psum(shift_two_part.astype(jnp.bfloat16), "ctx").astype(jnp.float32),
        lax.psum(joint_part.astype(jnp.bfloat16), "ctx").astype(jnp.float32),
        lax.psum(joint_bias_part.astype(jnp.bfloat16), "ctx").astype(jnp.float32),
        lax.psum(dense_part.astype(jnp.bfloat16), "ctx").astype(jnp.float32),
        lax.psum(column_part.astype(jnp.bfloat16), "ctx").astype(jnp.float32),
        lax.psum(expand_part.astype(jnp.bfloat16), "ctx").astype(jnp.float32),
        lax.psum(expand_bias_part.astype(jnp.bfloat16), "ctx").astype(jnp.float32),
        lax.psum(shrink_part.astype(jnp.bfloat16), "ctx").astype(jnp.float32),
    )
    return (
        output.astype(jnp.bfloat16)[None],
        tokens_grad[None],
        gain_one_total,
        shift_one_total,
        gain_two_total,
        shift_two_total,
        joint_total,
        joint_bias_total,
        dense_total,
        column_total,
        expand_total,
        expand_bias_total,
        shrink_total,
        column_total,
    )

CYCLE = (0, 2, 4, 6, 7, 5, 3, 1)
RIGHT = tuple(
    (2 * CYCLE[i] + core, 2 * CYCLE[(i + 1) % 8] + core) for i in range(8) for core in range(2)
)
LEFT = tuple((b, a) for a, b in RIGHT)
SWAP = tuple((i, i ^ 1) for i in range(16))
OFFSETS = (0, -1, 1, -2, 2, -3, 3, 4)
TILE = 512
BLOCK = 128


def right(values):
    return lax.ppermute(values, "ctx", RIGHT)


def left(values):
    return lax.ppermute(values, "ctx", LEFT)


def swap(values):
    return lax.ppermute(values, "ctx", SWAP)


def other(values):
    return lax.ppermute(values, "fsdp", ((0, 1), (1, 0)))


def after(values, *others):
    return lax.optimization_barrier((values, *others))[0]


def ring_gather(own):
    half = own.shape[0] // 2
    rights, lefts = [own], [own]
    for _ in range(3):
        rights.append(right(rights[-1]))
        lefts.append(left(lefts[-1]))
    far = jnp.concatenate([right(rights[3][:half]), left(lefts[3][half:])], 0)
    pieces = [own]
    for step in (1, 2, 3):
        pieces += [rights[step], lefts[step]]
    return pieces + [far]


def ring_scatter(parts):
    table = dict(zip(OFFSETS, parts))
    half = parts[0].shape[0] // 2
    add = lambda a, b: (a.astype(jnp.float32) + b.astype(jnp.float32)).astype(jnp.bfloat16)
    ahead = right(table[4][:half])
    behind = left(table[4][half:])
    ahead = jnp.concatenate([add(ahead, table[3][:half]), table[3][half:]], 0)
    behind = jnp.concatenate([table[-3][:half], add(behind, table[-3][half:])], 0)
    for step in (2, 1):
        ahead = add(right(ahead), table[step])
        behind = add(left(behind), table[-step])
    return right(ahead).astype(jnp.float32) + left(behind).astype(jnp.float32)


def turn_back(values, lanes):
    ahead = pltpu.roll(values, 128 - ROT // 2, 1)
    behind = pltpu.roll(values, ROT // 2, 1)
    return jnp.where(lanes % 64 < ROT // 2, -ahead, behind)


def nt(left_side, right_side):
    return lax.dot_general(
        left_side, right_side, (((1,), (1,)), ((), ())), preferred_element_type=jnp.float32
    )


def nn(left_side, right_side):
    return jnp.dot(left_side, right_side, preferred_element_type=jnp.float32)


def forward_kernel(slots, joint, cosine, sine, mixed, q_out, k_out, v_out, o_out, lse_out):
    rows = joint.shape[0]
    tiles = rows // TILE
    lanes = lax.broadcasted_iota(jnp.int32, (BLOCK, 128), 1)

    def sort(p, _):
        source = pl.ds(pl.multiple_of(slots[p] * BLOCK, BLOCK), BLOCK)
        target = pl.ds(pl.multiple_of(p * BLOCK, BLOCK), BLOCK)
        pair = joint[source, 0:128]
        pair = pair * cosine[target, :] + turn_back(pair, lanes) * sine[target, :]
        q_out[target, :] = pair[:, 0:64].astype(jnp.bfloat16)
        k_out[target, :] = pair[:, 64:128].astype(jnp.bfloat16)
        v_out[target, :] = joint[source, 128:192].astype(jnp.bfloat16)
        return 0

    lax.fori_loop(0, rows // BLOCK, sort, 0)
    below = lax.broadcasted_iota(jnp.int32, (TILE, TILE), 0) <= lax.broadcasted_iota(
        jnp.int32, (TILE, TILE), 1
    )

    def query_tile(i, _):
        here = pl.ds(pl.multiple_of(i * TILE, TILE), TILE)
        query = q_out[here, :] * jnp.bfloat16(0.125)

        def step(j, carry, masked):
            top, total, acc = carry
            there = pl.ds(pl.multiple_of(j * TILE, TILE), TILE)
            scores = nt(k_out[there, :], query)
            if masked:
                scores = jnp.where(below, scores, negative)
            new_top = jnp.maximum(top, jnp.max(scores, 0, keepdims=True))
            weights = jnp.exp(scores - new_top)
            keep = jnp.exp(top - new_top)
            total = total * keep + jnp.sum(weights, 0, keepdims=True)
            term = lax.dot_general(
                v_out[there, :],
                weights.astype(jnp.bfloat16),
                (((0,), (0,)), ((), ())),
                preferred_element_type=jnp.float32,
            )
            return new_top, total, acc * keep + term

        carry = (
            jnp.full((1, TILE), negative, jnp.float32),
            jnp.zeros((1, TILE), jnp.float32),
            jnp.zeros((64, TILE), jnp.float32),
        )
        carry = lax.fori_loop(0, i, lambda j, c: step(j, c, False), carry)
        top, total, acc = step(i, carry, True)
        acc = acc / total
        o_out[:, here] = acc
        lse_out[:, here] = top + jnp.log(total)
        out = acc.T.astype(jnp.bfloat16)
        for part in range(TILE // BLOCK):
            slot = slots[i * (TILE // BLOCK) + part]
            mixed[pl.ds(pl.multiple_of(slot * BLOCK, BLOCK), BLOCK), :] = out[
                part * BLOCK : (part + 1) * BLOCK
            ]
        return 0

    lax.fori_loop(0, tiles, query_tile, 0)


def backward_kernel(
    slots, q_in, k_in, v_in, o_in, lse_in, mixed_grad, cosine, sine, delta_out, grad_sorted, inner, dq, dk, dv
):
    rows = q_in.shape[0]
    tiles = rows // TILE
    lanes = lax.broadcasted_iota(jnp.int32, (BLOCK, 128), 1)

    def sort(p, _):
        source = pl.ds(pl.multiple_of(slots[p] * BLOCK, BLOCK), BLOCK)
        target = pl.ds(pl.multiple_of(p * BLOCK, BLOCK), BLOCK)
        piece = mixed_grad[source, :]
        grad_sorted[target, :] = piece
        flat = piece.astype(jnp.float32).T
        inner[:, target] = jnp.sum(flat * o_in[:, target], 0, keepdims=True)
        return 0

    lax.fori_loop(0, rows // BLOCK, sort, 0)
    dq[...] = jnp.zeros_like(dq)
    below = lax.broadcasted_iota(jnp.int32, (TILE, TILE), 0) <= lax.broadcasted_iota(
        jnp.int32, (TILE, TILE), 1
    )

    def key_tile(j, _):
        there = pl.ds(pl.multiple_of(j * TILE, TILE), TILE)
        key = k_in[there, :]
        value = v_in[there, :]

        def step(i, carry, masked):
            key_grad, value_grad = carry
            here = pl.ds(pl.multiple_of(i * TILE, TILE), TILE)
            query = q_in[here, :] * jnp.bfloat16(0.125)
            grad = grad_sorted[here, :]
            scores = nt(key, query)
            probs = jnp.exp(scores - lse_in[:, here])
            if masked:
                probs = jnp.where(below, probs, 0.0)
            prob_grad = nt(value, grad)
            score_grad = (probs * (prob_grad - inner[:, here])).astype(jnp.bfloat16)
            value_grad = value_grad + nn(probs.astype(jnp.bfloat16), grad)
            key_grad = key_grad + nn(score_grad, query)
            dq[:, here] += lax.dot_general(
                key, score_grad, (((0,), (0,)), ((), ())), preferred_element_type=jnp.float32
            )
            return key_grad, value_grad

        zero = jnp.zeros((TILE, 64), jnp.float32)
        carry = step(j, (zero, zero), True)
        key_grad, value_grad = lax.fori_loop(
            j + 1, tiles, lambda i, c: step(i, c, False), carry
        )
        dk[there, :] = key_grad
        dv[there, :] = value_grad
        return 0

    lax.fori_loop(0, tiles, key_tile, 0)

    def finish(p, _):
        target = pl.ds(pl.multiple_of(slots[p] * BLOCK, BLOCK), BLOCK)
        source = pl.ds(pl.multiple_of(p * BLOCK, BLOCK), BLOCK)
        pair = jnp.concatenate([dq[:, source].T * 0.125, dk[source, :]], 1)
        pair = pair * cosine[source, :] - turn_back(pair, lanes) * sine[source, :]
        delta_out[target, 0:128] = pair.astype(jnp.bfloat16)
        value = dv[source, :]
        delta_out[target, 128:256] = jnp.concatenate(
            [value, jnp.zeros_like(value)], 1
        ).astype(jnp.bfloat16)
        return 0

    lax.fori_loop(0, rows // BLOCK, finish, 0)


def whole(count):
    return [pl.BlockSpec(memory_space=pltpu.VMEM)] * count


def attention_forward(slots, joint, cosine, sine):
    rows = joint.shape[0]
    head = jax.ShapeDtypeStruct((rows, 64), jnp.bfloat16)
    return pl.pallas_call(
        forward_kernel,
        in_specs=[pl.BlockSpec(memory_space=pltpu.SMEM)] + whole(3),
        out_specs=whole(6),
        out_shape=[
            head,
            head,
            head,
            head,
            jax.ShapeDtypeStruct((64, rows), jnp.float32),
            jax.ShapeDtypeStruct((1, rows), jnp.float32),
        ],
        compiler_params=pltpu.CompilerParams(vmem_limit_bytes=48 * 1024 * 1024),
        cost_estimate=pl.CostEstimate(
            flops=rows * rows * 512, bytes_accessed=rows * 4096, transcendentals=rows * rows // 2
        ),
        name="attention_forward",
    )(slots, joint, cosine, sine)


def attention_backward(slots, query, key, value, out, lse, mixed_grad, cosine, sine):
    rows = query.shape[0]
    return pl.pallas_call(
        backward_kernel,
        in_specs=[pl.BlockSpec(memory_space=pltpu.SMEM)] + whole(8),
        out_specs=pl.BlockSpec(memory_space=pltpu.VMEM),
        out_shape=jax.ShapeDtypeStruct((rows, 256), jnp.bfloat16),
        scratch_shapes=[
            pltpu.VMEM((rows, 64), jnp.bfloat16),
            pltpu.VMEM((1, rows), jnp.float32),
            pltpu.VMEM((64, rows), jnp.float32),
            pltpu.VMEM((rows, 64), jnp.float32),
            pltpu.VMEM((rows, 64), jnp.float32),
        ],
        compiler_params=pltpu.CompilerParams(vmem_limit_bytes=48 * 1024 * 1024),
        cost_estimate=pl.CostEstimate(
            flops=rows * rows * 1280, bytes_accessed=rows * 4096, transcendentals=rows * rows // 2
        ),
        name="attention_backward",
    )(slots, query, key, value, out, lse, mixed_grad, cosine, sine)


def assemble_kernel(count, owners, *refs):
    blobs = refs[:count]
    shrink, dense, expand = refs[count + 3 : count + 6]
    wide, tall, sems = refs[count + 6 :]
    group = owners[count]
    hidden = expand.shape[1] // 2

    def dense_copy(n, owner):
        return pltpu.make_async_copy(
            wide.at[n, pl.ds(128, 64)],
            dense.at[pl.ds(pl.multiple_of(lax.rem(owner, 8) * 64, 64), 64)],
            sems.at[n, 3],
        )

    copies = []
    for n in range(count):
        owner = owners[n]
        blob = blobs[n]
        wide[n] = blob[0:192, :].astype(jnp.float32)
        for quarter in range(4):
            tall[n, quarter * 128 : (quarter + 1) * 128, :] = blob[
                192:320, quarter * 256 : (quarter + 1) * 256
            ].astype(jnp.float32)
        start = pl.multiple_of(owner * 128, 128)
        copies.append(
            pltpu.make_async_copy(
                wide.at[n, pl.ds(0, 128)], shrink.at[pl.ds(start, 128)], sems.at[n, 0]
            )
        )
        copies.append(
            pltpu.make_async_copy(
                tall.at[n, :, pl.ds(0, 128)], expand.at[:, pl.ds(start, 128)], sems.at[n, 1]
            )
        )
        copies.append(
            pltpu.make_async_copy(
                tall.at[n, :, pl.ds(128, 128)],
                expand.at[:, pl.ds(pl.multiple_of(hidden + start, 128), 128)],
                sems.at[n, 2],
            )
        )
        for copy in copies[-3:]:
            copy.start()

        @pl.when(owner // 8 == group)
        def _(n=n, owner=owner):
            dense_copy(n, owner).start()

    for copy in copies:
        copy.wait()
    for n in range(count):
        owner = owners[n]

        @pl.when(owner // 8 == group)
        def _(n=n, owner=owner):
            dense_copy(n, owner).wait()


def assemble(owners, blobs, outs):
    count = len(blobs)
    anywhere = [pl.BlockSpec(memory_space=pl.ANY)] * 3
    return pl.pallas_call(
        functools.partial(assemble_kernel, count),
        in_specs=[pl.BlockSpec(memory_space=pltpu.SMEM)] + whole(count) + anywhere,
        out_specs=anywhere,
        out_shape=[jax.ShapeDtypeStruct(o.shape, o.dtype) for o in outs],
        scratch_shapes=[
            pltpu.VMEM((count, 192, 1024), jnp.float32),
            pltpu.VMEM((count, 512, 256), jnp.float32),
            pltpu.SemaphoreType.DMA((count, 4)),
        ],
        input_output_aliases={1 + count + i: i for i in range(3)},
        compiler_params=pltpu.CompilerParams(vmem_limit_bytes=48 * 1024 * 1024),
        cost_estimate=pl.CostEstimate(
            flops=0, bytes_accessed=count * 320 * 1024 * 6, transcendentals=0
        ),
        name="assemble_blobs",
    )(owners, *blobs, *outs)


def assemble_joint_kernel(count, owners, *refs):
    blobs = refs[:count]
    joint = refs[count + 1]
    buffer, sems = refs[count + 2 :]
    width = joint.shape[1] // 3
    copies = []
    for n in range(count):
        owner = owners[n]
        buffer[n] = blobs[n][...].astype(jnp.float32)
        for part in range(3):
            start = pl.multiple_of(part * width + (owner // 2) * 128, 128)
            top = pl.multiple_of(lax.rem(owner, 2) * 256, 256)
            copies.append(
                pltpu.make_async_copy(
                    buffer.at[n, :, pl.ds(part * 128, 128)],
                    joint.at[pl.ds(top, 256), pl.ds(start, 128)],
                    sems.at[n, part],
                )
            )
            copies[-1].start()
    for copy in copies:
        copy.wait()


def assemble_joint(owners, blobs, out):
    count = len(blobs)
    return pl.pallas_call(
        functools.partial(assemble_joint_kernel, count),
        in_specs=[pl.BlockSpec(memory_space=pltpu.SMEM)]
        + whole(count)
        + [pl.BlockSpec(memory_space=pl.ANY)],
        out_specs=pl.BlockSpec(memory_space=pl.ANY),
        out_shape=jax.ShapeDtypeStruct(out.shape, out.dtype),
        scratch_shapes=[
            pltpu.VMEM((count, 256, 384), jnp.float32),
            pltpu.SemaphoreType.DMA((count, 3)),
        ],
        input_output_aliases={1 + count: 0},
        compiler_params=pltpu.CompilerParams(vmem_limit_bytes=48 * 1024 * 1024),
        cost_estimate=pl.CostEstimate(
            flops=0, bytes_accessed=count * 256 * 384 * 6, transcendentals=0
        ),
        name="assemble_joint",
    )(owners, *blobs, out)


def split_heads(
    tokens,
    cotangent,
    first_gain,
    first_shift,
    second_gain,
    second_shift,
    joint_weight,
    joint_bias,
    dense_weight,
    dense_bias,
    expand_weight,
    expand_bias,
    shrink_weight,
    shrink_bias,
    block_order,
):
    f32, bf16 = jnp.float32, jnp.bfloat16
    me = lax.axis_index("ctx")
    group = lax.axis_index("fsdp")
    rows, width = tokens.shape[1:]
    total_rows = rows * 16
    hidden = expand_weight.shape[1] // 2
    own_tokens, own_upstream = tokens[0], cotangent[0]

    def cut(values, start, size, axis):
        return lax.dynamic_slice_in_dim(values, start, size, axis)

    def both(values, axis):
        received = other(values)
        lower = jnp.where(group == 0, values, received)
        upper = jnp.where(group == 0, received, values)
        return jnp.concatenate([lower, upper], axis)

    cycle = jnp.array(CYCLE, jnp.int32)
    place = jnp.array([CYCLE.index(i) for i in range(8)], jnp.int32)[me // 2]
    chips = cycle[(place + jnp.array(OFFSETS, jnp.int32)) % 8]
    owners = jnp.concatenate([2 * chips + me % 2, 2 * chips + 1 - me % 2])
    blocks = block_order.reshape(16, 2)[owners].reshape(32)
    slots = jnp.zeros((32,), jnp.int32).at[blocks].set(jnp.arange(32, dtype=jnp.int32))

    vectors = both(
        jnp.concatenate(
            [
                v.reshape(-1, 512)
                for v in (
                    first_gain,
                    first_shift,
                    second_gain,
                    second_shift,
                    dense_bias,
                    shrink_bias,
                    joint_bias,
                    expand_bias,
                )
            ],
            0,
        )[None],
        0,
    )
    gain_one, shift_one, gain_two, shift_two, dense_shift, shrink_shift = (
        vectors[:, i, :].reshape(-1).astype(f32) for i in range(6)
    )
    joint_shift = vectors[:, 6:9, :].reshape(3, 16, 64)
    expand_shift = vectors[:, 9:13, :].reshape(2, 16, 128)
    joint_part = cut(joint_weight.reshape(-1, 3, 16, 64), me, 1, 2).reshape(-1, 192)
    joint_c = both(jnp.pad(joint_part, ((0, 0), (0, 64))), 0)
    joint_b = jnp.pad(cut(joint_shift, me, 1, 1).reshape(192), (0, 64)).astype(f32)
    expand_part = jnp.concatenate(
        [cut(expand_weight, me * 128, 128, 1), cut(expand_weight, hidden + me * 128, 128, 1)], 1
    )
    expand_c = both(expand_part, 0)
    expand_b = cut(expand_shift, me, 1, 1).reshape(256).astype(f32)
    shrink_c = both(cut(shrink_weight, me * 128, 128, 0), 0)
    dense_part = cut(dense_weight, (me % 8) * 64, 64, 0)
    dense_c = jnp.where(group == me // 8, dense_part, other(dense_part))

    token_own = ring_gather(own_tokens)
    token_all = token_own + [swap(v) for v in token_own]
    inputs = jnp.concatenate(token_all, 0)
    upstream_own = ring_gather(after(own_upstream, token_own[-2], token_own[-3]))
    upstream = jnp.concatenate(upstream_own + [swap(v) for v in upstream_own], 0)

    wide = inputs.astype(f32)
    center = wide - jnp.mean(wide, -1, keepdims=True)
    spread = jnp.mean(center * center, -1, keepdims=True)
    unit = center * lax.rsqrt(spread + epsilon)
    normed_one = (unit * gain_one + shift_one).astype(bf16)
    normed_two = (unit * gain_two + shift_two).astype(bf16)
    joint = nn(normed_one, joint_c) + joint_b
    expanded = nn(normed_two, expand_c) + expand_b
    activated = jax.nn.gelu(expanded, approximate=False).astype(bf16)

    inverse = jnp.power(10000.0, -2.0 * jnp.arange(ROT // 2, dtype=f32) / ROT)
    angles = jnp.arange(total_rows, dtype=f32)[:, None] * inverse[None, :]
    rest = jnp.zeros((total_rows, 64 - ROT), f32)
    cosine = jnp.concatenate([jnp.cos(angles), jnp.cos(angles), rest + 1.0] * 2, 1)
    sine = jnp.concatenate([jnp.sin(angles), jnp.sin(angles), rest] * 2, 1)

    mixed, query, key, value, out, lse = attention_forward(slots, joint, cosine, sine)

    branch = jnp.concatenate([activated, mixed], 1)
    back = jnp.concatenate([shrink_c, dense_c], 0)
    out_parts = core_sums(branch, back)
    out_sum = out_parts[0].astype(f32) + ring_scatter(out_parts)
    output = own_tokens.astype(f32) + out_sum + dense_shift + shrink_shift

    column_sum = jnp.sum(upstream.astype(f32), 0)
    back_grad = contract(branch, upstream, 0, 0)
    act_grad = nt(upstream, shrink_c)
    mixed_grad = nt(upstream, dense_c).astype(bf16)
    _, gelu_pull = jax.vjp(lambda v: jax.nn.gelu(v, approximate=False), expanded)
    expand_delta = gelu_pull(act_grad)[0].astype(bf16)
    expand_grad = contract(normed_two, expand_delta, 0, 0)
    expand_sum = jnp.sum(expand_delta.astype(f32), 0)

    def half_of(values, which, axis):
        size = values.shape[axis] // 2
        return cut(values, which * size, size, axis)

    def sum_halves(values, axis):
        sent = half_of(values, 1 - group, axis).astype(bf16)
        return half_of(values, group, axis) + other(sent).astype(f32)

    shrink_half = sum_halves(back_grad[:256], 0).astype(bf16)
    dense_half = (back_grad[256:] + other(back_grad[256:].astype(bf16)).astype(f32)).astype(bf16)
    expand_half = sum_halves(expand_grad, 0).astype(bf16)
    blob = jnp.concatenate(
        [
            shrink_half,
            dense_half,
            jnp.concatenate([expand_half[i * 128 : (i + 1) * 128] for i in range(4)], 1),
        ],
        0,
    )
    blob_own = ring_gather(blob)
    blob_all = blob_own + [swap(v) for v in blob_own]
    outs = tuple(
        jnp.zeros(shape, f32) for shape in ((hidden, width), (width // 2, width), (width // 2, 2 * hidden))
    )
    for start in (0, 4, 8, 12):
        some = owners[start : start + 4]
        outs = assemble(jnp.concatenate([some, group[None]]), blob_all[start : start + 4], outs)
    shrink_total, dense_total, expand_total = outs

    joint_delta = attention_backward(
        slots, query, key, value, out, lse, mixed_grad, cosine, sine
    )
    joint_grad = contract(normed_one, joint_delta, 0, 0)
    joint_sum = jnp.sum(joint_delta.astype(f32), 0)

    delta = jnp.concatenate([joint_delta, expand_delta], 1)
    scaled = jnp.concatenate(
        [
            (joint_c.astype(f32) * gain_one[:, None]).astype(bf16),
            (expand_c.astype(f32) * gain_two[:, None]).astype(bf16),
        ],
        1,
    ).T
    in_parts = core_sums(delta, scaled)
    in_sum = in_parts[0].astype(f32) + ring_scatter(in_parts)
    mine = own_tokens.astype(f32)
    mine = mine - jnp.mean(mine, -1, keepdims=True)
    scale = lax.rsqrt(jnp.mean(mine * mine, -1, keepdims=True) + epsilon)
    mine = mine * scale
    term = scale * (
        in_sum
        - jnp.mean(in_sum, -1, keepdims=True)
        - mine * jnp.mean(in_sum * mine, -1, keepdims=True)
    )
    tokens_grad = (own_upstream.astype(f32) + term).astype(bf16)

    joint_half = sum_halves(joint_grad, 0)[:, :192].astype(bf16)
    core = me % 2
    kept = half_of(joint_half, core, 0)
    received = swap(half_of(joint_half, 1 - core, 0))
    low = jnp.where(core == 0, kept, received).reshape(-1, 3, 1, 64)
    high = jnp.where(core == 0, received, kept).reshape(-1, 3, 1, 64)
    joint_blob = jnp.concatenate([low, high], 2).reshape(-1, 384)
    joint_own = ring_gather(joint_blob)
    joint_all = joint_own + [swap(v) for v in joint_own]
    joint_total = jnp.zeros((width // 2, 3 * width), f32)
    joint_total = assemble_joint(owners, joint_all, joint_total)

    def norm_grads(weight, grad, total, gain, shift):
        weight = weight.astype(f32)
        shift_grad = jnp.sum(weight * total[None, :], 1)
        return (jnp.sum(weight * grad, 1) - shift * shift_grad) / gain, shift_grad

    gain_one_grad, shift_one_grad = norm_grads(joint_c, joint_grad, joint_sum, gain_one, shift_one)
    gain_two_grad, shift_two_grad = norm_grads(expand_c, expand_grad, expand_sum, gain_two, shift_two)
    mark = (jnp.arange(16) == me).astype(f32)[None, :, None]
    expand_bias = (mark * expand_sum.reshape(2, 1, 128)).reshape(-1)
    joint_bias_all = (mark * joint_sum[:192].reshape(3, 1, 64)).reshape(-1)
    early = lax.psum(
        jnp.concatenate([expand_bias, gain_two_grad, shift_two_grad, column_sum / 16]),
        ("ctx", "fsdp"),
    )
    late = lax.psum(
        jnp.concatenate([joint_bias_all, gain_one_grad, shift_one_grad]), ("ctx", "fsdp")
    )

    def shard(values, start, size):
        return cut(values, start + group * (size // 2), size // 2, 0)

    full = 2 * hidden
    column_total = shard(early, full + 2 * width, width)
    return (
        output.astype(bf16)[None],
        tokens_grad[None],
        shard(late, 3 * width, width),
        shard(late, 4 * width, width),
        shard(early, full, width),
        shard(early, full + width, width),
        joint_total,
        shard(late, 0, 3 * width),
        dense_total,
        column_total,
        expand_total,
        shard(early, 0, full),
        shrink_total,
        column_total,
    )


def core_sums(values, weight):
    rows = values.shape[0] // 16
    parts = []
    for first, last in ((7, 8), (5, 7), (3, 5), (1, 3), (0, 1)):
        theirs = nn(values[(8 + first) * rows : (8 + last) * rows], weight).astype(jnp.bfloat16)
        mine = nn(values[first * rows : last * rows], weight)
        both = (mine + swap(theirs).astype(jnp.float32)).astype(jnp.bfloat16)
        parts = [both[i * rows : (i + 1) * rows] for i in range(last - first)] + parts
    return parts


def solution(mesh):
    fits = mesh.shape["ctx"] == HEADS and mesh.shape["fsdp"] == 2
    return jax.shard_map(
        split_heads if fits else shards,
        mesh=mesh,
        in_specs=(
            P("fsdp", "ctx", None),
            P("fsdp", "ctx", None),
            P("fsdp"),
            P("fsdp"),
            P("fsdp"),
            P("fsdp"),
            P("fsdp", None),
            P("fsdp"),
            P("fsdp", None),
            P("fsdp"),
            P("fsdp", None),
            P("fsdp"),
            P("fsdp", None),
            P("fsdp"),
            P(),
        ),
        out_specs=(
            P("fsdp", "ctx", None),
            P("fsdp", "ctx", None),
            P("fsdp"),
            P("fsdp"),
            P("fsdp"),
            P("fsdp"),
            P("fsdp", None),
            P("fsdp"),
            P("fsdp", None),
            P("fsdp"),
            P("fsdp", None),
            P("fsdp"),
            P("fsdp", None),
            P("fsdp"),
        ),
        check_vma=False,
    )
```

```python
import functools

import jax
import jax.numpy as jnp
from jax import lax
from jax.experimental import pallas as pl
from jax.experimental.pallas import tpu as pltpu
from jax.sharding import PartitionSpec as P

HEADS = 16
ROT = 16


epsilon = 1e-05
negative = -1e30


def normalize(values, gain, shift):
    center = values - jnp.mean(values, -1, keepdims=True)
    spread = jnp.mean(center * center, -1, keepdims=True)
    return center * lax.rsqrt(spread + epsilon) * gain + shift


def turn_tables(positions):
    inverse = jnp.power(10000.0, -2.0 * jnp.arange(ROT // 2, dtype=jnp.float32) / ROT)
    angles = positions.astype(jnp.float32)[:, None] * inverse[None, :]
    angles = jnp.concatenate([angles, angles], -1)[:, None, :]
    return (jnp.cos(angles), jnp.sin(angles))


def rotate(values, cosine, sine):
    half = ROT // 2
    front = values[..., :ROT]
    turned = jnp.concatenate([-front[..., half:], front[..., :half]], -1)
    return jnp.concatenate([front * cosine + turned * sine, values[..., ROT:]], -1)


def contract(left, right, left_dim, right_dim):
    return lax.dot_general(
        left, right, (((left_dim,), (right_dim,)), ((), ())), preferred_element_type=jnp.float32
    )


def shards(
    tokens,
    cotangent,
    first_gain,
    first_shift,
    second_gain,
    second_shift,
    joint_weight,
    joint_bias,
    dense_weight,
    dense_bias,
    expand_weight,
    expand_bias,
    shrink_weight,
    shrink_bias,
    block_order,
):
    rows = tokens.shape[1]
    width = tokens.shape[2]
    head_dim = width // HEADS
    scale = head_dim ** (-0.5)
    groups = lax.axis_size("ctx")
    half_rows = rows // 2
    (
        gain_one,
        shift_one,
        gain_two,
        shift_two,
        joint_full,
        joint_shift,
        dense_full,
        dense_shift,
        expand_full,
        expand_shift,
        shrink_full,
        shrink_shift,
    ) = (
        lax.all_gather(first_gain, "fsdp", axis=0, tiled=True),
        lax.all_gather(first_shift, "fsdp", axis=0, tiled=True),
        lax.all_gather(second_gain, "fsdp", axis=0, tiled=True),
        lax.all_gather(second_shift, "fsdp", axis=0, tiled=True),
        lax.all_gather(joint_weight, "fsdp", axis=0, tiled=True),
        lax.all_gather(joint_bias, "fsdp", axis=0, tiled=True),
        lax.all_gather(dense_weight, "fsdp", axis=0, tiled=True),
        lax.all_gather(dense_bias, "fsdp", axis=0, tiled=True),
        lax.all_gather(expand_weight, "fsdp", axis=0, tiled=True),
        lax.all_gather(expand_bias, "fsdp", axis=0, tiled=True),
        lax.all_gather(shrink_weight, "fsdp", axis=0, tiled=True),
        lax.all_gather(shrink_bias, "fsdp", axis=0, tiled=True),
    )
    gain_one = gain_one.astype(jnp.float32)
    shift_one = shift_one.astype(jnp.float32)
    gain_two = gain_two.astype(jnp.float32)
    shift_two = shift_two.astype(jnp.float32)
    all_positions = (
        block_order[:, None] * half_rows + jnp.arange(half_rows, dtype=jnp.int32)[None, :]
    ).reshape(rows * groups)
    positions = lax.dynamic_slice_in_dim(all_positions, lax.axis_index("ctx") * rows, rows)
    cosine, sine = turn_tables(positions)
    visible = positions[:, None] >= all_positions[None, :]
    inputs = tokens[0].astype(jnp.float32)
    normed_one = normalize(inputs, gain_one, shift_one).astype(jnp.bfloat16)
    normed_two = normalize(inputs, gain_two, shift_two).astype(jnp.bfloat16)
    joint = jnp.dot(
        normed_one, joint_full, preferred_element_type=jnp.float32
    ) + joint_shift.astype(jnp.float32)
    queries = (
        rotate(joint[:, :width].reshape(rows, HEADS, head_dim), cosine, sine)
        .reshape(rows, width)
        .astype(jnp.bfloat16)
    )
    key_rows = (
        rotate(joint[:, width : 2 * width].reshape(rows, HEADS, head_dim), cosine, sine)
        .reshape(rows, width)
        .astype(jnp.bfloat16)
    )
    value_rows = joint[:, 2 * width :].astype(jnp.bfloat16)
    all_keys, all_values = (
        lax.all_gather(key_rows, "ctx", axis=0, tiled=True),
        lax.all_gather(value_rows, "ctx", axis=0, tiled=True),
    )

    def head_scores(head, key_source):
        query = lax.dynamic_slice_in_dim(queries, head * head_dim, head_dim, 1)
        key_cols = lax.dynamic_slice_in_dim(key_source, head * head_dim, head_dim, 1)
        scores = contract(query, key_cols, 1, 1) * scale
        return (query, key_cols, jnp.where(visible, scores, negative))

    def head_forward(head):
        query, key_cols, scores = head_scores(head, all_keys)
        top = jnp.max(scores, -1, keepdims=True)
        total = jnp.sum(jnp.exp(scores - top), -1, keepdims=True)
        log_total = top + jnp.log(total)
        weights = jnp.exp(scores - log_total).astype(jnp.bfloat16)
        value_cols = lax.dynamic_slice_in_dim(all_values, head * head_dim, head_dim, 1)
        return (jnp.dot(weights, value_cols, preferred_element_type=jnp.float32), log_total[:, 0])

    mixed, log_totals = lax.map(head_forward, jnp.arange(HEADS))
    attended = jnp.transpose(mixed, (1, 0, 2)).reshape(rows, width).astype(jnp.bfloat16)
    expanded = jnp.dot(
        normed_two, expand_full, preferred_element_type=jnp.float32
    ) + expand_shift.astype(jnp.float32)
    activated = jax.nn.gelu(expanded, approximate=False).astype(jnp.bfloat16)
    output = (
        inputs
        + jnp.dot(attended, dense_full, preferred_element_type=jnp.float32)
        + dense_shift.astype(jnp.float32)
    )
    output = (
        output
        + jnp.dot(activated, shrink_full, preferred_element_type=jnp.float32)
        + shrink_shift.astype(jnp.float32)
    )
    upstream = cotangent[0]
    upstream_float = upstream.astype(jnp.float32)
    column_sum = jnp.sum(upstream_float, 0)
    dense_grad = contract(attended, upstream, 0, 0)
    shrink_grad = contract(activated, upstream, 0, 0)
    act_grad = contract(upstream, shrink_full, 1, 1)
    _, gelu_pull = jax.vjp(lambda value: jax.nn.gelu(value, approximate=False), expanded)
    expand_delta = gelu_pull(act_grad)[0].astype(jnp.bfloat16)
    expand_grad = contract(normed_two, expand_delta, 0, 0)
    expand_bias_grad = jnp.sum(expand_delta.astype(jnp.float32), 0)
    normed_two_grad = contract(expand_delta, expand_full, 1, 1)
    _, pull_two = jax.vjp(normalize, inputs, gain_two, shift_two)
    input_two, gain_two_grad, shift_two_grad = pull_two(normed_two_grad)
    attended_grad = contract(upstream, dense_full, 1, 1).astype(jnp.bfloat16)
    key_source, value_source = (all_keys, all_values)

    def head_backward(items):
        head, log_total = items
        query, key_cols, scores = head_scores(head, key_source)
        probs = jnp.exp(scores - log_total[:, None])
        value_cols = lax.dynamic_slice_in_dim(value_source, head * head_dim, head_dim, 1)
        out_grad = lax.dynamic_slice_in_dim(attended_grad, head * head_dim, head_dim, 1)
        prob_grad = contract(out_grad, value_cols, 1, 1)
        inner = jnp.sum(probs * prob_grad, -1, keepdims=True)
        score_grad = (probs * (prob_grad - inner)).astype(jnp.bfloat16)
        query_grad = jnp.dot(score_grad, key_cols, preferred_element_type=jnp.float32) * scale
        key_grad = contract(score_grad, query, 0, 0) * scale
        value_grad = contract(probs.astype(jnp.bfloat16), out_grad, 0, 0)
        return (query_grad, key_grad, value_grad)

    query_grads, key_grads, value_grads = lax.map(head_backward, (jnp.arange(HEADS), log_totals))
    key_sums, value_sums = (
        lax.psum_scatter(
            key_grads.astype(jnp.bfloat16), "ctx", scatter_dimension=1, tiled=True
        ).astype(jnp.float32),
        lax.psum_scatter(
            value_grads.astype(jnp.bfloat16), "ctx", scatter_dimension=1, tiled=True
        ).astype(jnp.float32),
    )
    query_back = rotate(jnp.transpose(query_grads, (1, 0, 2)), cosine, -sine).reshape(rows, width)
    key_back = rotate(jnp.transpose(key_sums, (1, 0, 2)), cosine, -sine).reshape(rows, width)
    value_back = jnp.transpose(value_sums, (1, 0, 2)).reshape(rows, width)
    joint_delta = jnp.concatenate([query_back, key_back, value_back], 1).astype(jnp.bfloat16)
    joint_grad = contract(normed_one, joint_delta, 0, 0)
    joint_bias_grad = jnp.sum(joint_delta.astype(jnp.float32), 0)
    normed_one_grad = contract(joint_delta, joint_full, 1, 1)
    _, pull_one = jax.vjp(normalize, inputs, gain_one, shift_one)
    input_one, gain_one_grad, shift_one_grad = pull_one(normed_one_grad)
    tokens_grad = (upstream_float + input_one + input_two).astype(jnp.bfloat16)
    (
        gain_one_part,
        shift_one_part,
        gain_two_part,
        shift_two_part,
        joint_part,
        joint_bias_part,
        dense_part,
        column_part,
        expand_part,
        expand_bias_part,
        shrink_part,
    ) = (
        lax.psum_scatter(
            gain_one_grad.astype(jnp.bfloat16), "fsdp", scatter_dimension=0, tiled=True
        ).astype(jnp.float32),
        lax.psum_scatter(
            shift_one_grad.astype(jnp.bfloat16), "fsdp", scatter_dimension=0, tiled=True
        ).astype(jnp.float32),
        lax.psum_scatter(
            gain_two_grad.astype(jnp.bfloat16), "fsdp", scatter_dimension=0, tiled=True
        ).astype(jnp.float32),
        lax.psum_scatter(
            shift_two_grad.astype(jnp.bfloat16), "fsdp", scatter_dimension=0, tiled=True
        ).astype(jnp.float32),
        lax.psum_scatter(
            joint_grad.astype(jnp.bfloat16), "fsdp", scatter_dimension=0, tiled=True
        ).astype(jnp.float32),
        lax.psum_scatter(
            joint_bias_grad.astype(jnp.bfloat16), "fsdp", scatter_dimension=0, tiled=True
        ).astype(jnp.float32),
        lax.psum_scatter(
            dense_grad.astype(jnp.bfloat16), "fsdp", scatter_dimension=0, tiled=True
        ).astype(jnp.float32),
        lax.psum_scatter(
            column_sum.astype(jnp.bfloat16), "fsdp", scatter_dimension=0, tiled=True
        ).astype(jnp.float32),
        lax.psum_scatter(
            expand_grad.astype(jnp.bfloat16), "fsdp", scatter_dimension=0, tiled=True
        ).astype(jnp.float32),
        lax.psum_scatter(
            expand_bias_grad.astype(jnp.bfloat16), "fsdp", scatter_dimension=0, tiled=True
        ).astype(jnp.float32),
        lax.psum_scatter(
            shrink_grad.astype(jnp.bfloat16), "fsdp", scatter_dimension=0, tiled=True
        ).astype(jnp.float32),
    )
    (
        gain_one_total,
        shift_one_total,
        gain_two_total,
        shift_two_total,
        joint_total,
        joint_bias_total,
        dense_total,
        column_total,
        expand_total,
        expand_bias_total,
        shrink_total,
    ) = (
        lax.psum(gain_one_part.astype(jnp.bfloat16), "ctx").astype(jnp.float32),
        lax.psum(shift_one_part.astype(jnp.bfloat16), "ctx").astype(jnp.float32),
        lax.psum(gain_two_part.astype(jnp.bfloat16), "ctx").astype(jnp.float32),
        lax.psum(shift_two_part.astype(jnp.bfloat16), "ctx").astype(jnp.float32),
        lax.psum(joint_part.astype(jnp.bfloat16), "ctx").astype(jnp.float32),
        lax.psum(joint_bias_part.astype(jnp.bfloat16), "ctx").astype(jnp.float32),
        lax.psum(dense_part.astype(jnp.bfloat16), "ctx").astype(jnp.float32),
        lax.psum(column_part.astype(jnp.bfloat16), "ctx").astype(jnp.float32),
        lax.psum(expand_part.astype(jnp.bfloat16), "ctx").astype(jnp.float32),
        lax.psum(expand_bias_part.astype(jnp.bfloat16), "ctx").astype(jnp.float32),
        lax.psum(shrink_part.astype(jnp.bfloat16), "ctx").astype(jnp.float32),
    )
    return (
        output.astype(jnp.bfloat16)[None],
        tokens_grad[None],
        gain_one_total,
        shift_one_total,
        gain_two_total,
        shift_two_total,
        joint_total,
        joint_bias_total,
        dense_total,
        column_total,
        expand_total,
        expand_bias_total,
        shrink_total,
        column_total,
    )

CYCLE = (0, 2, 4, 6, 7, 5, 3, 1)
RING = tuple((2 * CYCLE[i], 2 * CYCLE[(i + 1) % 8]) for i in range(8)) + tuple(
    (2 * CYCLE[i] + 1, 2 * CYCLE[i - 1] + 1) for i in range(8)
)
SWAP = tuple((i, i ^ 1) for i in range(16))
TILE = 512
BLOCK = 128
MIB = 1024 * 1024


def hop(values):
    return lax.ppermute(values, "ctx", RING)


def swap(values):
    return lax.ppermute(values, "ctx", SWAP)


def other(values):
    return lax.ppermute(values, "fsdp", ((0, 1), (1, 0)))


def after(values, *others):
    return lax.optimization_barrier((values, *others))[0]


def cut(values, start, size, axis):
    return lax.dynamic_slice_in_dim(values, start, size, axis)


def ring_gather(own, core, gates=(None, None, None, None)):
    size = own.shape[0]
    partner = swap(own)
    pair = jnp.where(
        core == 0, jnp.concatenate([own, partner], 0), jnp.concatenate([partner, own], 0)
    )
    blocks, hops = [pair], []
    held = pair
    for step in range(3):
        if gates[step] is not None:
            held = after(held, gates[step])
        held = hop(held)
        hops.append(held)
        blocks += [held, swap(held)]
    far = cut(held, core * size, size, 0)
    if gates[3] is not None:
        far = after(far, gates[3])
    far = hop(far)
    hops.append(far)
    blocks.append(jnp.concatenate([far, swap(far)], 0))
    return blocks, hops


def piece_owners(me):
    core = me % 2
    cycle = jnp.array(CYCLE, jnp.int32)
    place = jnp.array([CYCLE.index(i) for i in range(8)], jnp.int32)[me // 2]
    toward = 2 * core - 1
    steps = jnp.array([0, 1, -1, 2, -2, 3, -3], jnp.int32) * toward
    chips = cycle[(place + steps) % 8]
    pairs = (2 * chips[:, None] + jnp.arange(2, dtype=jnp.int32)[None, :]).reshape(-1)
    far = cycle[(place + 4) % 8]
    return jnp.concatenate([pairs, jnp.stack([2 * far + core, 2 * far + 1 - core])]).astype(
        jnp.int32
    )


def ring_scatter(values, weight, core, gates=(None, None, None, None)):
    rows = values.shape[0] // 16
    f32, bf16 = jnp.float32, jnp.bfloat16

    def term(first, count):
        return nn(values[first * rows : (first + count) * rows], weight)

    def gated(held, step):
        return held if gates[step] is None else after(held, gates[step])

    far = (term(14, 1) + swap(term(15, 1).astype(bf16)).astype(f32)).astype(bf16)
    held = hop(gated(far, 0))
    hops = [held]
    for step in (3, 2, 1):
        theirs = swap(term(4 * step - 2, 2).astype(bf16))
        mine = term(4 * step, 2) + theirs.astype(f32)
        if step == 3:
            blank = jnp.zeros_like(held)
            held = jnp.where(
                core == 0,
                jnp.concatenate([held, blank], 0),
                jnp.concatenate([blank, held], 0),
            )
        held = hop(gated((mine + held.astype(f32)).astype(bf16), 4 - step))
        hops.append(held)
    total = term(0, 2) + held.astype(f32)
    sent = cut(total, (1 - core) * rows, rows, 0).astype(bf16)
    return cut(total, core * rows, rows, 0) + swap(sent).astype(f32), hops


def turn_back(values, lanes):
    ahead = pltpu.roll(values, 128 - ROT // 2, 1)
    behind = pltpu.roll(values, ROT // 2, 1)
    return jnp.where(lanes % 64 < ROT // 2, -ahead, behind)


def nt(left_side, right_side):
    return lax.dot_general(
        left_side, right_side, (((1,), (1,)), ((), ())), preferred_element_type=jnp.float32
    )


def nn(left_side, right_side):
    return jnp.dot(left_side, right_side, preferred_element_type=jnp.float32)


def tn(left_side, right_side):
    return lax.dot_general(
        left_side, right_side, (((0,), (0,)), ((), ())), preferred_element_type=jnp.float32
    )


VMEM = pl.BlockSpec(memory_space=pltpu.VMEM)
SMEM = pl.BlockSpec(memory_space=pltpu.SMEM)
ANY = pl.BlockSpec(memory_space=pl.ANY)


def shaped(shape, dtype):
    return jax.ShapeDtypeStruct(shape, dtype)


def pre_kernel(x, norms, joint_w, joint_b, expand_w, expand_b, *refs):
    one, two, joint, active, slope = refs[-5:]
    wide = x[...].astype(jnp.float32)
    center = wide - jnp.mean(wide, -1, keepdims=True)
    spread = jnp.mean(center * center, -1, keepdims=True)
    unit = center * lax.rsqrt(spread + epsilon)
    normed_one = (unit * norms[0:1, :] + norms[1:2, :]).astype(jnp.bfloat16)
    normed_two = (unit * norms[2:3, :] + norms[3:4, :]).astype(jnp.bfloat16)
    one[...] = normed_one
    two[...] = normed_two
    joint[...] = nn(normed_one, joint_w[...]) + joint_b[...]
    expanded = nn(normed_two, expand_w[...]) + expand_b[...]
    share = 0.5 + 0.5 * lax.erf(expanded * (0.5**0.5))
    active[...] = (expanded * share).astype(jnp.bfloat16)
    slope[...] = share + expanded * (jnp.exp(-0.5 * expanded * expanded) * 0.3989422804014327)


def pre(index, x, norms, joint_w, joint_b, expand_w, expand_b, outs, count):
    rows, width = x.shape
    step = rows // 2
    fixed = lambda shape: pl.BlockSpec(shape, lambda i: (0, 0))
    place = lambda cols: pl.BlockSpec((step, cols), lambda i: (2 * index + i, 0))
    total = rows * count
    bf16, f32 = jnp.bfloat16, jnp.float32
    aliases = {} if outs is None else {6 + i: i for i in range(5)}
    return pl.pallas_call(
        pre_kernel,
        grid=(2,),
        in_specs=[pl.BlockSpec((step, width), lambda i: (i, 0))]
        + [fixed(v.shape) for v in (norms, joint_w, joint_b, expand_w, expand_b)]
        + [ANY] * len(aliases),
        out_specs=[place(width), place(width), place(256), place(256), place(256)],
        out_shape=[
            shaped((total, width), bf16),
            shaped((total, width), bf16),
            shaped((total, 256), f32),
            shaped((total, 256), bf16),
            shaped((total, 256), f32),
        ],
        input_output_aliases=aliases,
        compiler_params=pltpu.CompilerParams(vmem_limit_bytes=40 * MIB),
        cost_estimate=pl.CostEstimate(
            flops=rows * width * 1024, bytes_accessed=rows * width * 10, transcendentals=rows * 512
        ),
        name="norms_joint_hidden",
    )(x, norms, joint_w, joint_b, expand_w, expand_b, *(outs or ()))


def tables(angle_rows):
    lanes = jnp.arange(128) % 64
    inverse = jnp.power(10000.0, -2.0 * (lanes % (ROT // 2)).astype(jnp.float32) / ROT)
    angles = angle_rows.astype(jnp.float32)[:, None] * jnp.where(lanes < ROT, inverse, 0.0)[None, :]
    return jnp.cos(angles), jnp.sin(angles)


def turn_kernel(blocks, joint, cos_far, sin_far, cos_near, sin_near, q_out, k_out, v_out):
    rows = joint.shape[0]
    lanes = lax.broadcasted_iota(jnp.int32, (BLOCK, 128), 1)

    def sort(s, _):
        p = blocks[s]
        source = pl.ds(pl.multiple_of(s * BLOCK, BLOCK), BLOCK)
        target = pl.ds(pl.multiple_of(p * BLOCK, BLOCK), BLOCK)
        far = pl.ds(p, 1)
        cosine = cos_far[far, :] * cos_near[...] - sin_far[far, :] * sin_near[...]
        sine = sin_far[far, :] * cos_near[...] + cos_far[far, :] * sin_near[...]
        pair = joint[source, 0:128]
        pair = pair * cosine + turn_back(pair, lanes) * sine
        q_out[target, :] = pair[:, 0:64].astype(jnp.bfloat16)
        k_out[target, :] = pair[:, 64:128].astype(jnp.bfloat16)
        v_out[target, :] = joint[source, 128:192].astype(jnp.bfloat16)
        return 0

    lax.fori_loop(0, rows // BLOCK, sort, 0)


def turn(blocks, joint, angles):
    rows = joint.shape[0]
    head = shaped((rows, 64), jnp.bfloat16)
    return pl.pallas_call(
        turn_kernel,
        in_specs=[SMEM] + [VMEM] * 5,
        out_specs=[VMEM] * 3,
        out_shape=[head] * 3,
        compiler_params=pltpu.CompilerParams(vmem_limit_bytes=40 * MIB),
        cost_estimate=pl.CostEstimate(flops=0, bytes_accessed=rows * 2048, transcendentals=0),
        name="rotary_and_sort",
    )(blocks, joint, *angles)


def below_diagonal():
    return lax.broadcasted_iota(jnp.int32, (TILE, TILE), 0) <= lax.broadcasted_iota(
        jnp.int32, (TILE, TILE), 1
    )


def forward_kernel(index, slots, q, k, v, *refs):
    mixed_out, out, lse = refs[-5:-2]
    buffer, sems = refs[-2:]
    tiles = q.shape[0] // TILE
    below = below_diagonal()
    parts = TILE // BLOCK
    copies = []
    for which, i in enumerate((index, tiles - 1 - index)):
        query = q[i * TILE : (i + 1) * TILE, :] * jnp.bfloat16(0.125)

        def step(j, carry, masked):
            top, total, acc = carry
            there = pl.ds(pl.multiple_of(j * TILE, TILE), TILE)
            scores = nt(k[there, :], query)
            if masked:
                scores = jnp.where(below, scores, negative)
            new_top = jnp.maximum(top, jnp.max(scores, 0, keepdims=True))
            weights = jnp.exp(scores - new_top)
            keep = jnp.exp(top - new_top)
            total = total * keep + jnp.sum(weights, 0, keepdims=True)
            return new_top, total, acc * keep + tn(v[there, :], weights.astype(jnp.bfloat16))

        carry = (
            jnp.full((1, TILE), negative, jnp.float32),
            jnp.zeros((1, TILE), jnp.float32),
            jnp.zeros((64, TILE), jnp.float32),
        )
        carry = lax.fori_loop(0, i, lambda j, c: step(j, c, False), carry)
        top, total, acc = step(i, carry, True)
        acc = acc / total
        here = slice(which * TILE, (which + 1) * TILE)
        out[:, here] = acc
        lse[:, here] = top + jnp.log(total)
        buffer[here, :] = acc.T.astype(jnp.bfloat16)
        for part in range(parts):
            slot = slots[i * parts + part]
            copies.append(
                pltpu.make_async_copy(
                    buffer.at[pl.ds(which * TILE + part * BLOCK, BLOCK)],
                    mixed_out.at[pl.ds(pl.multiple_of(slot * BLOCK, BLOCK), BLOCK)],
                    sems.at[which * parts + part],
                )
            )
            copies[-1].start()
    for copy in copies:
        copy.wait()


def attention_forward(index, slots, q, k, v, mixed, gate):
    rows = q.shape[0]
    extra = ([] if mixed is None else [mixed]) + ([] if gate is None else [gate])
    return pl.pallas_call(
        functools.partial(forward_kernel, index),
        in_specs=[SMEM] + [VMEM] * 3 + [ANY] * len(extra),
        out_specs=[ANY, VMEM, VMEM],
        out_shape=[
            shaped((rows, 64), jnp.bfloat16),
            shaped((64, 2 * TILE), jnp.float32),
            shaped((1, 2 * TILE), jnp.float32),
        ],
        scratch_shapes=[
            pltpu.VMEM((2 * TILE, 64), jnp.bfloat16),
            pltpu.SemaphoreType.DMA((2 * TILE // BLOCK,)),
        ],
        input_output_aliases={} if mixed is None else {4: 0},
        compiler_params=pltpu.CompilerParams(vmem_limit_bytes=40 * MIB),
        cost_estimate=pl.CostEstimate(
            flops=rows * rows * 256, bytes_accessed=rows * 1024, transcendentals=rows * rows // 8
        ),
        name="attention_forward",
    )(slots, q, k, v, *extra)


def post_kernel(pieces, *refs):
    blocks = refs[:pieces]
    slope, active, mixed, shrink, dense = refs[pieces : pieces + 5]
    delta, mixed_grad, shrink_grad, dense_grad, column, delta_sum, held = refs[pieces + 5 :]
    step = pl.program_id(0)
    for n in range(pieces):

        @pl.when(step == n)
        def _(n=n):
            held[...] = blocks[n][...]

    @pl.when(step == 0)
    def _():
        shrink_grad[...] = jnp.zeros_like(shrink_grad)
        dense_grad[...] = jnp.zeros_like(dense_grad)
        column[...] = jnp.zeros_like(column)
        delta_sum[...] = jnp.zeros_like(delta_sum)

    grad = held[...]
    column[...] += jnp.sum(grad.astype(jnp.float32), 0, keepdims=True)
    rounded = (nt(grad, shrink[...]) * slope[...]).astype(jnp.bfloat16)
    delta[...] = rounded
    delta_sum[...] += jnp.sum(rounded.astype(jnp.float32), 0, keepdims=True)
    mixed_grad[...] = nt(grad, dense[...]).astype(jnp.bfloat16)
    shrink_grad[...] += tn(active[...], grad)
    dense_grad[...] += tn(mixed[...], grad)


def post(blocks, slope, active, mixed, shrink, dense):
    count = len(blocks)
    rows, width = blocks[0].shape
    total = rows * count
    row = lambda cols: pl.BlockSpec((rows, cols), lambda i: (i, 0))
    fixed = lambda shape: pl.BlockSpec(shape, lambda i: (0, 0))
    f32, bf16 = jnp.float32, jnp.bfloat16
    return pl.pallas_call(
        functools.partial(post_kernel, count),
        grid=(count,),
        in_specs=[VMEM] * count
        + [row(256), row(256), row(64), fixed(shrink.shape), fixed(dense.shape)],
        out_specs=[
            row(256),
            row(64),
            fixed((256, width)),
            fixed((64, width)),
            fixed((1, width)),
            fixed((1, 256)),
        ],
        out_shape=[
            shaped((total, 256), bf16),
            shaped((total, 64), bf16),
            shaped((256, width), f32),
            shaped((64, width), f32),
            shaped((1, width), f32),
            shaped((1, 256), f32),
        ],
        scratch_shapes=[pltpu.VMEM((rows, width), bf16)],
        compiler_params=pltpu.CompilerParams(vmem_limit_bytes=44 * MIB),
        cost_estimate=pl.CostEstimate(
            flops=total * width * 1280, bytes_accessed=total * width * 4, transcendentals=0
        ),
        name="cotangent_products",
    )(*blocks, slope, active, mixed, shrink, dense)


def sort_grad_kernel(tiles, slots, mixed_grad, *refs):
    outs = refs[:tiles]
    grad, inner = refs[-2:]
    per_tile = TILE // BLOCK

    for p in range(slots.shape[0]):
        tile, part = divmod(p, per_tile)
        column = part * BLOCK
        if tile >= tiles:
            tile, column = 2 * tiles - 1 - tile, column + TILE
        source = pl.ds(pl.multiple_of(slots[p] * BLOCK, BLOCK), BLOCK)
        piece = mixed_grad[source, :]
        here = slice(p * BLOCK, (p + 1) * BLOCK)
        grad[here, :] = piece
        flat = piece.astype(jnp.float32).T
        inner[:, here] = jnp.sum(
            flat * outs[tile][:, column : column + BLOCK], 0, keepdims=True
        )


def sort_grad(slots, mixed_grad, outs):
    rows = mixed_grad.shape[0]
    return pl.pallas_call(
        functools.partial(sort_grad_kernel, len(outs)),
        in_specs=[SMEM] + [VMEM] * (1 + len(outs)),
        out_specs=[VMEM] * 2,
        out_shape=[shaped((rows, 64), jnp.bfloat16), shaped((1, rows), jnp.float32)],
        compiler_params=pltpu.CompilerParams(vmem_limit_bytes=40 * MIB),
        cost_estimate=pl.CostEstimate(flops=0, bytes_accessed=rows * 1024, transcendentals=0),
        name="sort_gradient",
    )(slots, mixed_grad, *outs)


def backward_kernel(index, first, q, k, v, grad, inner, lse, *refs):
    dq, dk, dv = refs[-3:]
    tiles = q.shape[0] // TILE
    below = below_diagonal()
    if first:
        dq[...] = jnp.zeros_like(dq)
    else:
        dq[...] = refs[0][...]
    for which, j in enumerate((index, tiles - 1 - index)):
        key = k[j * TILE : (j + 1) * TILE, :]
        value = v[j * TILE : (j + 1) * TILE, :]

        def step(i, carry, masked):
            key_grad, value_grad = carry
            here = pl.ds(pl.multiple_of(i * TILE, TILE), TILE)
            query = q[here, :] * jnp.bfloat16(0.125)
            out_grad = grad[here, :]
            probs = jnp.exp(nt(key, query) - lse[:, here])
            if masked:
                probs = jnp.where(below, probs, 0.0)
            score_grad = (probs * (nt(value, out_grad) - inner[:, here])).astype(jnp.bfloat16)
            value_grad = value_grad + nn(probs.astype(jnp.bfloat16), out_grad)
            key_grad = key_grad + nn(score_grad, query)
            dq[:, here] += tn(key, score_grad)
            return key_grad, value_grad

        zero = jnp.zeros((TILE, 64), jnp.float32)
        carry = step(j, (zero, zero), True)
        key_grad, value_grad = lax.fori_loop(
            j + 1, tiles, lambda i, c: step(i, c, False), carry
        )
        here = slice(which * TILE, (which + 1) * TILE)
        dk[here, :] = key_grad
        dv[here, :] = value_grad


def attention_backward(index, q, k, v, grad, inner, lse, dq, gate):
    rows = q.shape[0]
    extra = ([] if dq is None else [dq]) + ([] if gate is None else [gate])
    specs = ([] if dq is None else [VMEM]) + ([] if gate is None else [ANY])
    return pl.pallas_call(
        functools.partial(backward_kernel, index, dq is None),
        in_specs=[VMEM] * 6 + specs,
        out_specs=[VMEM] * 3,
        out_shape=[
            shaped((64, rows), jnp.float32),
            shaped((2 * TILE, 64), jnp.float32),
            shaped((2 * TILE, 64), jnp.float32),
        ],
        compiler_params=pltpu.CompilerParams(vmem_limit_bytes=40 * MIB),
        cost_estimate=pl.CostEstimate(
            flops=rows * rows * 640, bytes_accessed=rows * 2048, transcendentals=rows * rows // 8
        ),
        name="attention_backward",
    )(q, k, v, grad, inner, lse, *extra)


def finish_kernel(tiles, slots, dq, cos_far, sin_far, cos_near, sin_near, *refs):
    key_grads, value_grads = refs[:tiles], refs[tiles : 2 * tiles]
    delta, total = refs[-2:]
    lanes = lax.broadcasted_iota(jnp.int32, (BLOCK, 128), 1)
    per_tile = TILE // BLOCK
    total[...] = jnp.zeros_like(total)
    for p in range(slots.shape[0]):
        tile, part = divmod(p, per_tile)
        row = part * BLOCK
        if tile >= tiles:
            tile, row = 2 * tiles - 1 - tile, row + TILE
        target = pl.ds(pl.multiple_of(slots[p] * BLOCK, BLOCK), BLOCK)
        cosine = cos_far[p : p + 1, :] * cos_near[...] - sin_far[p : p + 1, :] * sin_near[...]
        sine = sin_far[p : p + 1, :] * cos_near[...] + cos_far[p : p + 1, :] * sin_near[...]
        query = dq[:, p * BLOCK : (p + 1) * BLOCK].T * 0.125
        pair = jnp.concatenate([query, key_grads[tile][row : row + BLOCK, :]], 1)
        pair = (pair * cosine - turn_back(pair, lanes) * sine).astype(jnp.bfloat16)
        value = value_grads[tile][row : row + BLOCK, :]
        last = jnp.concatenate([value, jnp.zeros_like(value)], 1).astype(jnp.bfloat16)
        delta[target, 0:128] = pair
        delta[target, 128:256] = last
        total[:, 0:128] += jnp.sum(pair.astype(jnp.float32), 0, keepdims=True)
        total[:, 128:256] += jnp.sum(last.astype(jnp.float32), 0, keepdims=True)


def finish(slots, dq, angles, key_grads, value_grads):
    rows = dq.shape[1]
    return pl.pallas_call(
        functools.partial(finish_kernel, len(key_grads)),
        in_specs=[SMEM] + [VMEM] * (5 + 2 * len(key_grads)),
        out_specs=[VMEM] * 2,
        out_shape=[shaped((rows, 256), jnp.bfloat16), shaped((1, 256), jnp.float32)],
        compiler_params=pltpu.CompilerParams(vmem_limit_bytes=40 * MIB),
        cost_estimate=pl.CostEstimate(flops=0, bytes_accessed=rows * 2048, transcendentals=0),
        name="joint_delta",
    )(slots, dq, *angles, *key_grads, *value_grads)


def assemble_kernel(owners, blob, *refs):
    shrink, dense, expand = refs[-6:-3]
    wide, tall, sems = refs[-3:]
    group = owners[2]
    hidden = expand.shape[1] // 2
    size = blob.shape[0] // 2

    def dense_copy(n):
        return pltpu.make_async_copy(
            wide.at[n, pl.ds(128, 64)],
            dense.at[pl.ds(pl.multiple_of(lax.rem(owners[n], 8) * 64, 64), 64)],
            sems.at[n, 3],
        )

    copies = []
    for n in range(2):
        wide[n] = blob[n * size : n * size + 192, :].astype(jnp.float32)
        for quarter in range(4):
            tall[n, quarter * 128 : (quarter + 1) * 128, :] = blob[
                n * size + 192 : n * size + 320, quarter * 256 : (quarter + 1) * 256
            ].astype(jnp.float32)
        start = pl.multiple_of(owners[n] * 128, 128)
        copies += [
            pltpu.make_async_copy(
                wide.at[n, pl.ds(0, 128)], shrink.at[pl.ds(start, 128)], sems.at[n, 0]
            ),
            pltpu.make_async_copy(
                tall.at[n, :, pl.ds(0, 128)], expand.at[:, pl.ds(start, 128)], sems.at[n, 1]
            ),
            pltpu.make_async_copy(
                tall.at[n, :, pl.ds(128, 128)],
                expand.at[:, pl.ds(pl.multiple_of(hidden + start, 128), 128)],
                sems.at[n, 2],
            ),
        ]
        for copy in copies[-3:]:
            copy.start()

        @pl.when(owners[n] // 8 == group)
        def _(n=n):
            dense_copy(n).start()

    for copy in copies:
        copy.wait()
    for n in range(2):

        @pl.when(owners[n] // 8 == group)
        def _(n=n):
            dense_copy(n).wait()


def assemble(owners, blob, shapes, outs):
    return pl.pallas_call(
        assemble_kernel,
        in_specs=[SMEM, VMEM] + [ANY] * (0 if outs is None else 3),
        out_specs=[ANY] * 3,
        out_shape=[shaped(s, jnp.float32) for s in shapes],
        scratch_shapes=[
            pltpu.VMEM((2, 192, 1024), jnp.float32),
            pltpu.VMEM((2, 512, 256), jnp.float32),
            pltpu.SemaphoreType.DMA((2, 4)),
        ],
        input_output_aliases={} if outs is None else {2 + i: i for i in range(3)},
        compiler_params=pltpu.CompilerParams(vmem_limit_bytes=40 * MIB),
        cost_estimate=pl.CostEstimate(flops=0, bytes_accessed=640 * 6144, transcendentals=0),
        name="place_gradients",
    )(owners, blob, *(outs or ()))


def assemble_joint_kernel(count, owners, *refs):
    blobs = refs[:count]
    joint, buffer, sems = refs[count:]
    width = joint.shape[1] // 3
    size = blobs[0].shape[0] // 2
    copies = []
    for n in range(2 * count):
        owner = owners[n]
        first = (n % 2) * size
        buffer[n] = blobs[n // 2][first : first + 256, :].astype(jnp.float32)
        top = pl.multiple_of(lax.rem(owner, 2) * 256, 256)
        for part in range(3):
            start = pl.multiple_of(part * width + (owner // 2) * 128, 128)
            copies.append(
                pltpu.make_async_copy(
                    buffer.at[n, :, pl.ds(part * 128, 128)],
                    joint.at[pl.ds(top, 256), pl.ds(start, 128)],
                    sems.at[n, part],
                )
            )
            copies[-1].start()
    for copy in copies:
        copy.wait()


def assemble_joint(owners, blobs, shape):
    count = len(blobs)
    return pl.pallas_call(
        functools.partial(assemble_joint_kernel, count),
        in_specs=[SMEM] + [VMEM] * count,
        out_specs=ANY,
        out_shape=shaped(shape, jnp.float32),
        scratch_shapes=[
            pltpu.VMEM((2 * count, 256, 384), jnp.float32),
            pltpu.SemaphoreType.DMA((2 * count, 3)),
        ],
        compiler_params=pltpu.CompilerParams(vmem_limit_bytes=40 * MIB),
        cost_estimate=pl.CostEstimate(
            flops=0, bytes_accessed=count * 512 * 384 * 6, transcendentals=0
        ),
        name="place_joint_gradient",
    )(owners, *blobs)


def split_heads(
    tokens,
    cotangent,
    first_gain,
    first_shift,
    second_gain,
    second_shift,
    joint_weight,
    joint_bias,
    dense_weight,
    dense_bias,
    expand_weight,
    expand_bias,
    shrink_weight,
    shrink_bias,
    block_order,
):
    f32, bf16 = jnp.float32, jnp.bfloat16
    me = lax.axis_index("ctx")
    group = lax.axis_index("fsdp")
    core = me % 2
    rows, width = tokens.shape[1:]
    total_rows = rows * 16
    hidden = expand_weight.shape[1] // 2
    own_tokens, own_upstream = tokens[0], cotangent[0]

    token_blocks, token_hops = ring_gather(own_tokens, core)
    upstream_blocks, upstream_hops = ring_gather(
        own_upstream, core, (token_hops[2], token_hops[3], None, None)
    )

    owners = piece_owners(me)
    blocks = block_order.reshape(16, 2)[owners].reshape(32)
    slots = jnp.sum(
        jnp.where(
            blocks[None, :] == jnp.arange(32, dtype=jnp.int32)[:, None],
            jnp.arange(32, dtype=jnp.int32)[None, :],
            0,
        ),
        1,
    )

    def both(mine, received, axis):
        return jnp.concatenate(
            [jnp.where(group == 0, mine, received), jnp.where(group == 0, received, mine)], axis
        )

    heads = [cut(joint_weight, i * width + (me // 2) * 128, 128, 1) for i in range(3)]
    tall = jnp.concatenate(
        [jnp.where(core == 0, h[:, :64], h[:, 64:]) for h in heads]
        + [jnp.zeros((width // 2, 64), bf16)]
        + [cut(expand_weight, i * hidden + me * 128, 128, 1) for i in range(2)],
        1,
    )
    vector = jnp.concatenate(
        [
            first_gain,
            first_shift,
            second_gain,
            second_shift,
            dense_bias,
            shrink_bias,
            joint_bias,
            expand_bias,
            jnp.zeros((16 * 1024 - 13 * 512,), bf16),
        ]
    ).reshape(16, 1024)
    flat = jnp.concatenate(
        [cut(shrink_weight, me * 128, 128, 0), cut(dense_weight, (me % 8) * 64, 64, 0), vector], 0
    )
    tall_other, flat_other = other(tall), other(flat)
    tall = both(tall, tall_other, 0)
    joint_c, expand_c = tall[:, :256], tall[:, 256:]
    shrink_c = both(flat[:128], flat_other[:128], 0)
    dense_c = jnp.where(group == me // 8, flat[128:192], flat_other[128:192])
    vectors = both(
        vector.reshape(-1, 512)[None, :13], flat_other[192:].reshape(-1, 512)[None, :13], 0
    ).astype(f32)
    gain_one, shift_one, gain_two, shift_two, dense_shift, shrink_shift = (
        vectors[:, i, :].reshape(-1) for i in range(6)
    )
    joint_b = jnp.pad(
        cut(vectors[:, 6:9, :].reshape(3, 16, 64), me, 1, 1).reshape(1, 192), ((0, 0), (0, 64))
    )
    expand_b = cut(vectors[:, 9:13, :].reshape(2, 16, 128), me, 1, 1).reshape(1, 256)
    norms = jnp.concatenate(
        [jnp.stack([gain_one, shift_one, gain_two, shift_two]), jnp.zeros((4, width), f32)], 0
    )

    outs = None
    for index, block in enumerate(token_blocks):
        outs = pre(index, block, norms, joint_c, joint_b, expand_c, expand_b, outs, 8)
    normed_one, normed_two, joint, activated, slope = outs

    angles = tables(jnp.arange(total_rows // BLOCK) * BLOCK) + tables(jnp.arange(BLOCK))
    query, key, value = turn(blocks, joint, angles)
    mixed, outs, sums = None, [], []
    for index in range(4):
        gate = upstream_hops[index - 1] if index else None
        mixed, out, lse = attention_forward(index, slots, query, key, value, mixed, gate)
        outs.append(out)
        sums.append(lse)
    lse = jnp.concatenate(
        [s[:, :TILE] for s in sums] + [s[:, TILE:] for s in sums[::-1]], 1
    )

    branch = jnp.concatenate([activated, mixed], 1)
    back = jnp.concatenate([shrink_c, dense_c], 0)
    out_sum, out_hops = ring_scatter(branch, back, core, (upstream_hops[3], None, None, None))
    output = own_tokens.astype(f32) + out_sum + dense_shift + shrink_shift

    expand_delta, mixed_grad, shrink_grad, dense_grad, column_sum, expand_sum = post(
        upstream_blocks, slope, activated, mixed, shrink_c, dense_c
    )
    expand_grad = tn(normed_two, expand_delta)

    def half_of(values, which, axis):
        size = values.shape[axis] // 2
        return cut(values, which * size, size, axis)

    def sum_halves(values, axis):
        sent = half_of(values, 1 - group, axis).astype(bf16)
        return half_of(values, group, axis) + other(sent).astype(f32)

    shrink_half = sum_halves(shrink_grad, 0).astype(bf16)
    dense_half = (dense_grad + other(dense_grad.astype(bf16)).astype(f32)).astype(bf16)
    expand_half = sum_halves(expand_grad, 0).astype(bf16)
    blob = jnp.concatenate(
        [
            shrink_half,
            dense_half,
            jnp.concatenate([expand_half[i * 128 : (i + 1) * 128] for i in range(4)], 1),
        ],
        0,
    )
    blob_blocks, blob_hops = ring_gather(blob, core, (out_hops[2], out_hops[3], None, None))
    placed = None
    shapes = ((hidden, width), (width // 2, width), (width // 2, 2 * hidden))
    for index, block in enumerate(blob_blocks):
        some = jnp.concatenate([owners[2 * index : 2 * index + 2], group[None]]).astype(jnp.int32)
        placed = assemble(some, block, shapes, placed)
    shrink_total, dense_total, expand_total = placed

    out_grad, inner = sort_grad(slots, mixed_grad, outs)
    dq, key_grads, value_grads = None, [], []
    for index in range(4):
        gate = out_hops[index - 1] if index else None
        dq, dk, dv = attention_backward(
            index, query, key, value, out_grad, inner, lse, dq, gate
        )
        key_grads.append(dk)
        value_grads.append(dv)
    joint_delta, joint_sum = finish(slots, dq, angles, key_grads, value_grads)
    joint_grad = tn(normed_one, joint_delta)

    delta = jnp.concatenate([joint_delta, expand_delta], 1)
    scaled = jnp.concatenate(
        [
            (joint_c.astype(f32) * gain_one[:, None]).astype(bf16),
            (expand_c.astype(f32) * gain_two[:, None]).astype(bf16),
        ],
        1,
    ).T
    in_sum, in_hops = ring_scatter(delta, scaled, core, (blob_hops[2], blob_hops[3], None, None))
    mine = own_tokens.astype(f32)
    mine = mine - jnp.mean(mine, -1, keepdims=True)
    scale = lax.rsqrt(jnp.mean(mine * mine, -1, keepdims=True) + epsilon)
    mine = mine * scale
    term = scale * (
        in_sum
        - jnp.mean(in_sum, -1, keepdims=True)
        - mine * jnp.mean(in_sum * mine, -1, keepdims=True)
    )
    tokens_grad = (own_upstream.astype(f32) + term).astype(bf16)

    def norm_grads(weight, grad, total, gain, shift):
        weight = weight.astype(f32)
        shift_grad = jnp.sum(weight * total, 1)
        return (jnp.sum(weight * grad, 1) - shift * shift_grad) / gain, shift_grad

    gain_one_grad, shift_one_grad = norm_grads(joint_c, joint_grad, joint_sum, gain_one, shift_one)
    gain_two_grad, shift_two_grad = norm_grads(
        expand_c, expand_grad, expand_sum, gain_two, shift_two
    )
    norm_part = jnp.stack([gain_one_grad, shift_one_grad, gain_two_grad, shift_two_grad]).reshape(
        4, 2, width // 2
    )
    column_part = column_sum.reshape(2, width // 2)
    bias_part = jnp.concatenate([joint_sum[0, :192], expand_sum[0]])

    def pack(which):
        return jnp.concatenate(
            [
                cut(norm_part, which, 1, 1).reshape(-1),
                cut(column_part, which, 1, 0).reshape(-1),
                bias_part,
                jnp.zeros((32 * 384 - 5 * (width // 2) - 448,), f32),
            ]
        ).reshape(32, 384)

    packed = pack(group) + other(pack(1 - group).astype(bf16)).astype(f32)

    joint_half = sum_halves(joint_grad, 0)[:, :192].astype(bf16)
    kept = half_of(joint_half, core, 0)
    received = swap(half_of(joint_half, 1 - core, 0))
    low = jnp.where(core == 0, kept, received).reshape(-1, 3, 1, 64)
    high = jnp.where(core == 0, received, kept).reshape(-1, 3, 1, 64)
    joint_blob = jnp.concatenate([low, high], 2).reshape(-1, 384)
    joint_blob = jnp.concatenate([joint_blob, packed.astype(bf16)], 0)
    joint_blocks, _ = ring_gather(joint_blob, core)
    joint_total = assemble_joint(owners, joint_blocks, (width // 2, 3 * width))

    parts = jnp.concatenate(
        [
            jnp.stack([b[256:288], b[544:576]]).reshape(2, -1).astype(f32)
            for b in joint_blocks
        ],
        0,
    )
    small = width // 2
    totals = jnp.sum(parts[:, : 4 * small], 0)
    order = jnp.zeros((16, 16), f32).at[owners, jnp.arange(16)].set(1.0)
    biases = jnp.sum(order[:, :, None] * parts[None, :, 5 * small : 5 * small + 448], 1)
    joint_bias_total = jnp.transpose(biases[:, :192].reshape(16, 3, 64), (1, 0, 2)).reshape(-1)
    expand_bias_total = jnp.transpose(biases[:, 192:].reshape(16, 2, 128), (1, 0, 2)).reshape(-1)
    column_total = packed.reshape(-1)[4 * small : 5 * small]

    return (
        output.astype(bf16)[None],
        tokens_grad[None],
        totals[:small],
        totals[small : 2 * small],
        totals[2 * small : 3 * small],
        totals[3 * small :],
        joint_total,
        half_of(joint_bias_total, group, 0),
        dense_total,
        column_total,
        expand_total,
        half_of(expand_bias_total, group, 0),
        shrink_total,
        column_total,
    )


def solution(mesh):
    fits = mesh.shape["ctx"] == HEADS and mesh.shape["fsdp"] == 2
    return jax.shard_map(
        split_heads if fits else shards,
        mesh=mesh,
        in_specs=(
            P("fsdp", "ctx", None),
            P("fsdp", "ctx", None),
            P("fsdp"),
            P("fsdp"),
            P("fsdp"),
            P("fsdp"),
            P("fsdp", None),
            P("fsdp"),
            P("fsdp", None),
            P("fsdp"),
            P("fsdp", None),
            P("fsdp"),
            P("fsdp", None),
            P("fsdp"),
            P(),
        ),
        out_specs=(
            P("fsdp", "ctx", None),
            P("fsdp", "ctx", None),
            P("fsdp"),
            P("fsdp"),
            P("fsdp"),
            P("fsdp"),
            P("fsdp", None),
            P("fsdp"),
            P("fsdp", None),
            P("fsdp"),
            P("fsdp", None),
            P("fsdp"),
            P("fsdp", None),
            P("fsdp"),
        ),
        check_vma=False,
    )
```

```python
import functools

import jax
import jax.numpy as jnp
from jax import lax
from jax.experimental import pallas as pl
from jax.experimental.pallas import tpu as pltpu
from jax.sharding import PartitionSpec as P

HEADS = 16
ROT = 16


epsilon = 1e-05
negative = -1e30


def normalize(values, gain, shift):
    center = values - jnp.mean(values, -1, keepdims=True)
    spread = jnp.mean(center * center, -1, keepdims=True)
    return center * lax.rsqrt(spread + epsilon) * gain + shift


def turn_tables(positions):
    inverse = jnp.power(10000.0, -2.0 * jnp.arange(ROT // 2, dtype=jnp.float32) / ROT)
    angles = positions.astype(jnp.float32)[:, None] * inverse[None, :]
    angles = jnp.concatenate([angles, angles], -1)[:, None, :]
    return (jnp.cos(angles), jnp.sin(angles))


def rotate(values, cosine, sine):
    half = ROT // 2
    front = values[..., :ROT]
    turned = jnp.concatenate([-front[..., half:], front[..., :half]], -1)
    return jnp.concatenate([front * cosine + turned * sine, values[..., ROT:]], -1)


def contract(left, right, left_dim, right_dim):
    return lax.dot_general(
        left, right, (((left_dim,), (right_dim,)), ((), ())), preferred_element_type=jnp.float32
    )


def shards(
    tokens,
    cotangent,
    first_gain,
    first_shift,
    second_gain,
    second_shift,
    joint_weight,
    joint_bias,
    dense_weight,
    dense_bias,
    expand_weight,
    expand_bias,
    shrink_weight,
    shrink_bias,
    block_order,
):
    rows = tokens.shape[1]
    width = tokens.shape[2]
    head_dim = width // HEADS
    scale = head_dim ** (-0.5)
    groups = lax.axis_size("ctx")
    half_rows = rows // 2
    (
        gain_one,
        shift_one,
        gain_two,
        shift_two,
        joint_full,
        joint_shift,
        dense_full,
        dense_shift,
        expand_full,
        expand_shift,
        shrink_full,
        shrink_shift,
    ) = (
        lax.all_gather(first_gain, "fsdp", axis=0, tiled=True),
        lax.all_gather(first_shift, "fsdp", axis=0, tiled=True),
        lax.all_gather(second_gain, "fsdp", axis=0, tiled=True),
        lax.all_gather(second_shift, "fsdp", axis=0, tiled=True),
        lax.all_gather(joint_weight, "fsdp", axis=0, tiled=True),
        lax.all_gather(joint_bias, "fsdp", axis=0, tiled=True),
        lax.all_gather(dense_weight, "fsdp", axis=0, tiled=True),
        lax.all_gather(dense_bias, "fsdp", axis=0, tiled=True),
        lax.all_gather(expand_weight, "fsdp", axis=0, tiled=True),
        lax.all_gather(expand_bias, "fsdp", axis=0, tiled=True),
        lax.all_gather(shrink_weight, "fsdp", axis=0, tiled=True),
        lax.all_gather(shrink_bias, "fsdp", axis=0, tiled=True),
    )
    gain_one = gain_one.astype(jnp.float32)
    shift_one = shift_one.astype(jnp.float32)
    gain_two = gain_two.astype(jnp.float32)
    shift_two = shift_two.astype(jnp.float32)
    all_positions = (
        block_order[:, None] * half_rows + jnp.arange(half_rows, dtype=jnp.int32)[None, :]
    ).reshape(rows * groups)
    positions = lax.dynamic_slice_in_dim(all_positions, lax.axis_index("ctx") * rows, rows)
    cosine, sine = turn_tables(positions)
    visible = positions[:, None] >= all_positions[None, :]
    inputs = tokens[0].astype(jnp.float32)
    normed_one = normalize(inputs, gain_one, shift_one).astype(jnp.bfloat16)
    normed_two = normalize(inputs, gain_two, shift_two).astype(jnp.bfloat16)
    joint = jnp.dot(
        normed_one, joint_full, preferred_element_type=jnp.float32
    ) + joint_shift.astype(jnp.float32)
    queries = (
        rotate(joint[:, :width].reshape(rows, HEADS, head_dim), cosine, sine)
        .reshape(rows, width)
        .astype(jnp.bfloat16)
    )
    key_rows = (
        rotate(joint[:, width : 2 * width].reshape(rows, HEADS, head_dim), cosine, sine)
        .reshape(rows, width)
        .astype(jnp.bfloat16)
    )
    value_rows = joint[:, 2 * width :].astype(jnp.bfloat16)
    all_keys, all_values = (
        lax.all_gather(key_rows, "ctx", axis=0, tiled=True),
        lax.all_gather(value_rows, "ctx", axis=0, tiled=True),
    )

    def head_scores(head, key_source):
        query = lax.dynamic_slice_in_dim(queries, head * head_dim, head_dim, 1)
        key_cols = lax.dynamic_slice_in_dim(key_source, head * head_dim, head_dim, 1)
        scores = contract(query, key_cols, 1, 1) * scale
        return (query, key_cols, jnp.where(visible, scores, negative))

    def head_forward(head):
        query, key_cols, scores = head_scores(head, all_keys)
        top = jnp.max(scores, -1, keepdims=True)
        total = jnp.sum(jnp.exp(scores - top), -1, keepdims=True)
        log_total = top + jnp.log(total)
        weights = jnp.exp(scores - log_total).astype(jnp.bfloat16)
        value_cols = lax.dynamic_slice_in_dim(all_values, head * head_dim, head_dim, 1)
        return (jnp.dot(weights, value_cols, preferred_element_type=jnp.float32), log_total[:, 0])

    mixed, log_totals = lax.map(head_forward, jnp.arange(HEADS))
    attended = jnp.transpose(mixed, (1, 0, 2)).reshape(rows, width).astype(jnp.bfloat16)
    expanded = jnp.dot(
        normed_two, expand_full, preferred_element_type=jnp.float32
    ) + expand_shift.astype(jnp.float32)
    activated = jax.nn.gelu(expanded, approximate=False).astype(jnp.bfloat16)
    output = (
        inputs
        + jnp.dot(attended, dense_full, preferred_element_type=jnp.float32)
        + dense_shift.astype(jnp.float32)
    )
    output = (
        output
        + jnp.dot(activated, shrink_full, preferred_element_type=jnp.float32)
        + shrink_shift.astype(jnp.float32)
    )
    upstream = cotangent[0]
    upstream_float = upstream.astype(jnp.float32)
    column_sum = jnp.sum(upstream_float, 0)
    dense_grad = contract(attended, upstream, 0, 0)
    shrink_grad = contract(activated, upstream, 0, 0)
    act_grad = contract(upstream, shrink_full, 1, 1)
    _, gelu_pull = jax.vjp(lambda value: jax.nn.gelu(value, approximate=False), expanded)
    expand_delta = gelu_pull(act_grad)[0].astype(jnp.bfloat16)
    expand_grad = contract(normed_two, expand_delta, 0, 0)
    expand_bias_grad = jnp.sum(expand_delta.astype(jnp.float32), 0)
    normed_two_grad = contract(expand_delta, expand_full, 1, 1)
    _, pull_two = jax.vjp(normalize, inputs, gain_two, shift_two)
    input_two, gain_two_grad, shift_two_grad = pull_two(normed_two_grad)
    attended_grad = contract(upstream, dense_full, 1, 1).astype(jnp.bfloat16)
    key_source, value_source = (all_keys, all_values)

    def head_backward(items):
        head, log_total = items
        query, key_cols, scores = head_scores(head, key_source)
        probs = jnp.exp(scores - log_total[:, None])
        value_cols = lax.dynamic_slice_in_dim(value_source, head * head_dim, head_dim, 1)
        out_grad = lax.dynamic_slice_in_dim(attended_grad, head * head_dim, head_dim, 1)
        prob_grad = contract(out_grad, value_cols, 1, 1)
        inner = jnp.sum(probs * prob_grad, -1, keepdims=True)
        score_grad = (probs * (prob_grad - inner)).astype(jnp.bfloat16)
        query_grad = jnp.dot(score_grad, key_cols, preferred_element_type=jnp.float32) * scale
        key_grad = contract(score_grad, query, 0, 0) * scale
        value_grad = contract(probs.astype(jnp.bfloat16), out_grad, 0, 0)
        return (query_grad, key_grad, value_grad)

    query_grads, key_grads, value_grads = lax.map(head_backward, (jnp.arange(HEADS), log_totals))
    key_sums, value_sums = (
        lax.psum_scatter(
            key_grads.astype(jnp.bfloat16), "ctx", scatter_dimension=1, tiled=True
        ).astype(jnp.float32),
        lax.psum_scatter(
            value_grads.astype(jnp.bfloat16), "ctx", scatter_dimension=1, tiled=True
        ).astype(jnp.float32),
    )
    query_back = rotate(jnp.transpose(query_grads, (1, 0, 2)), cosine, -sine).reshape(rows, width)
    key_back = rotate(jnp.transpose(key_sums, (1, 0, 2)), cosine, -sine).reshape(rows, width)
    value_back = jnp.transpose(value_sums, (1, 0, 2)).reshape(rows, width)
    joint_delta = jnp.concatenate([query_back, key_back, value_back], 1).astype(jnp.bfloat16)
    joint_grad = contract(normed_one, joint_delta, 0, 0)
    joint_bias_grad = jnp.sum(joint_delta.astype(jnp.float32), 0)
    normed_one_grad = contract(joint_delta, joint_full, 1, 1)
    _, pull_one = jax.vjp(normalize, inputs, gain_one, shift_one)
    input_one, gain_one_grad, shift_one_grad = pull_one(normed_one_grad)
    tokens_grad = (upstream_float + input_one + input_two).astype(jnp.bfloat16)
    (
        gain_one_part,
        shift_one_part,
        gain_two_part,
        shift_two_part,
        joint_part,
        joint_bias_part,
        dense_part,
        column_part,
        expand_part,
        expand_bias_part,
        shrink_part,
    ) = (
        lax.psum_scatter(
            gain_one_grad.astype(jnp.bfloat16), "fsdp", scatter_dimension=0, tiled=True
        ).astype(jnp.float32),
        lax.psum_scatter(
            shift_one_grad.astype(jnp.bfloat16), "fsdp", scatter_dimension=0, tiled=True
        ).astype(jnp.float32),
        lax.psum_scatter(
            gain_two_grad.astype(jnp.bfloat16), "fsdp", scatter_dimension=0, tiled=True
        ).astype(jnp.float32),
        lax.psum_scatter(
            shift_two_grad.astype(jnp.bfloat16), "fsdp", scatter_dimension=0, tiled=True
        ).astype(jnp.float32),
        lax.psum_scatter(
            joint_grad.astype(jnp.bfloat16), "fsdp", scatter_dimension=0, tiled=True
        ).astype(jnp.float32),
        lax.psum_scatter(
            joint_bias_grad.astype(jnp.bfloat16), "fsdp", scatter_dimension=0, tiled=True
        ).astype(jnp.float32),
        lax.psum_scatter(
            dense_grad.astype(jnp.bfloat16), "fsdp", scatter_dimension=0, tiled=True
        ).astype(jnp.float32),
        lax.psum_scatter(
            column_sum.astype(jnp.bfloat16), "fsdp", scatter_dimension=0, tiled=True
        ).astype(jnp.float32),
        lax.psum_scatter(
            expand_grad.astype(jnp.bfloat16), "fsdp", scatter_dimension=0, tiled=True
        ).astype(jnp.float32),
        lax.psum_scatter(
            expand_bias_grad.astype(jnp.bfloat16), "fsdp", scatter_dimension=0, tiled=True
        ).astype(jnp.float32),
        lax.psum_scatter(
            shrink_grad.astype(jnp.bfloat16), "fsdp", scatter_dimension=0, tiled=True
        ).astype(jnp.float32),
    )
    (
        gain_one_total,
        shift_one_total,
        gain_two_total,
        shift_two_total,
        joint_total,
        joint_bias_total,
        dense_total,
        column_total,
        expand_total,
        expand_bias_total,
        shrink_total,
    ) = (
        lax.psum(gain_one_part.astype(jnp.bfloat16), "ctx").astype(jnp.float32),
        lax.psum(shift_one_part.astype(jnp.bfloat16), "ctx").astype(jnp.float32),
        lax.psum(gain_two_part.astype(jnp.bfloat16), "ctx").astype(jnp.float32),
        lax.psum(shift_two_part.astype(jnp.bfloat16), "ctx").astype(jnp.float32),
        lax.psum(joint_part.astype(jnp.bfloat16), "ctx").astype(jnp.float32),
        lax.psum(joint_bias_part.astype(jnp.bfloat16), "ctx").astype(jnp.float32),
        lax.psum(dense_part.astype(jnp.bfloat16), "ctx").astype(jnp.float32),
        lax.psum(column_part.astype(jnp.bfloat16), "ctx").astype(jnp.float32),
        lax.psum(expand_part.astype(jnp.bfloat16), "ctx").astype(jnp.float32),
        lax.psum(expand_bias_part.astype(jnp.bfloat16), "ctx").astype(jnp.float32),
        lax.psum(shrink_part.astype(jnp.bfloat16), "ctx").astype(jnp.float32),
    )
    return (
        output.astype(jnp.bfloat16)[None],
        tokens_grad[None],
        gain_one_total,
        shift_one_total,
        gain_two_total,
        shift_two_total,
        joint_total,
        joint_bias_total,
        dense_total,
        column_total,
        expand_total,
        expand_bias_total,
        shrink_total,
        column_total,
    )

CYCLE = (0, 2, 4, 6, 7, 5, 3, 1)
RING = tuple((2 * CYCLE[i], 2 * CYCLE[(i + 1) % 8]) for i in range(8)) + tuple(
    (2 * CYCLE[i] + 1, 2 * CYCLE[i - 1] + 1) for i in range(8)
)
SWAP = tuple((i, i ^ 1) for i in range(16))
TILE = 512
BLOCK = 128
MIB = 1024 * 1024


def hop(values):
    return lax.ppermute(values, "ctx", RING)


def swap(values):
    return lax.ppermute(values, "ctx", SWAP)


def other(values):
    return lax.ppermute(values, "fsdp", ((0, 1), (1, 0)))


def after(values, *others):
    return lax.optimization_barrier((values, *others))[0]


def cut(values, start, size, axis):
    return lax.dynamic_slice_in_dim(values, start, size, axis)


def gather_hop(held, step, *gates):
    if step == 4:
        held = held[: held.shape[0] // 2]
    return hop(after(held, *gates) if gates else held)


def piece_owners(me):
    core = me % 2
    piece = jnp.arange(16, dtype=jnp.int32)
    pair = piece // 2
    step = jnp.where(pair % 2 == 1, (pair + 1) // 2, -(pair // 2)) * (2 * core - 1)
    along = me // 4
    place = (jnp.where((me // 2) % 2 == 0, along, 7 - along) + step + 8) % 8
    chip = jnp.where(place < 4, 2 * place, 15 - 2 * place)
    other_first = (pair % 2 == 0) & (pair > 0)
    return 2 * chip + (piece + core + other_first) % 2


def scatter_term(values, weight, step, held=None):
    rows = values.shape[0] // 16
    f32, bf16 = jnp.float32, jnp.bfloat16

    def term(first, count):
        return nn(values[first * rows : (first + count) * rows], weight)

    if step == 4:
        return (term(14, 1) + swap(term(15, 1).astype(bf16)).astype(f32)).astype(bf16)
    mine = term(4 * step, 2) + swap(term(4 * step - 2, 2).astype(bf16)).astype(f32)
    if step == 3:
        held = jnp.pad(held, ((rows, 0), (0, 0)))
    return (mine + held.astype(f32)).astype(bf16)


def scatter_last(values, weight, held):
    rows = values.shape[0] // 16
    own = nn(values[:rows], weight) + held[rows:].astype(jnp.float32)
    sent = nn(values[rows : 2 * rows], weight) + held[:rows].astype(jnp.float32)
    return own + swap(sent.astype(jnp.bfloat16)).astype(jnp.float32)


def turn_back(values, lanes):
    ahead = pltpu.roll(values, 128 - ROT // 2, 1)
    behind = pltpu.roll(values, ROT // 2, 1)
    return jnp.where(lanes % 64 < ROT // 2, -ahead, behind)


def nt(left_side, right_side):
    return lax.dot_general(
        left_side, right_side, (((1,), (1,)), ((), ())), preferred_element_type=jnp.float32
    )


def nn(left_side, right_side):
    return jnp.dot(left_side, right_side, preferred_element_type=jnp.float32)


def tn(left_side, right_side):
    return lax.dot_general(
        left_side, right_side, (((0,), (0,)), ((), ())), preferred_element_type=jnp.float32
    )


VMEM = pl.BlockSpec(memory_space=pltpu.VMEM)
SMEM = pl.BlockSpec(memory_space=pltpu.SMEM)
ANY = pl.BlockSpec(memory_space=pl.ANY)


def shaped(shape, dtype):
    return jax.ShapeDtypeStruct(shape, dtype)


def pre_kernel(x, norms, joint_w, biases, expand_w, *refs):
    one, two, joint, active, slope, done = refs[-6:]
    done[...] = jnp.zeros_like(done)
    wide = x[...].astype(jnp.float32)
    center = wide - jnp.mean(wide, -1, keepdims=True)
    spread = jnp.mean(center * center, -1, keepdims=True)
    unit = center * lax.rsqrt(spread + epsilon)
    normed_one = (unit * norms[0:1, :] + norms[1:2, :]).astype(jnp.bfloat16)
    normed_two = (unit * norms[2:3, :] + norms[3:4, :]).astype(jnp.bfloat16)
    one[...] = normed_one
    two[...] = normed_two
    joint[...] = nn(normed_one, joint_w[...]) + biases[0:1, :]
    expanded = nn(normed_two, expand_w[...]) + biases[1:2, :]
    share = 0.5 + 0.5 * lax.erf(expanded * (0.5**0.5))
    active[...] = (expanded * share).astype(jnp.bfloat16)
    slope[...] = share + expanded * (jnp.exp(-0.5 * expanded * expanded) * 0.3989422804014327)


def pre(index, x, norms, joint_w, biases, expand_w, outs, count):
    rows, width = x.shape
    step = rows // 2
    fixed = lambda shape: pl.BlockSpec(shape, lambda i: (0, 0))
    place = lambda cols: pl.BlockSpec((step, cols), lambda i: (2 * index + i, 0))
    total = rows * count
    bf16, f32 = jnp.bfloat16, jnp.float32
    aliases = {} if outs is None else {5 + i: i for i in range(5)}
    return pl.pallas_call(
        pre_kernel,
        grid=(2,),
        in_specs=[pl.BlockSpec((step, width), lambda i: (i, 0))]
        + [fixed(v.shape) for v in (norms, joint_w, biases, expand_w)]
        + [ANY] * len(aliases),
        out_specs=[place(width), place(width), place(256), place(256), place(256), fixed((8, 128))],
        out_shape=[
            pltpu.HBM((total, width), bf16),
            pltpu.HBM((total, width), bf16),
            pltpu.HBM((total, 256), f32),
            pltpu.HBM((total, 256), bf16),
            pltpu.HBM((total, 256), f32),
            shaped((8, 128), f32),
        ],
        input_output_aliases=aliases,
        compiler_params=pltpu.CompilerParams(vmem_limit_bytes=40 * MIB),
        cost_estimate=pl.CostEstimate(
            flops=rows * width * 1024, bytes_accessed=rows * width * 10, transcendentals=rows * 512
        ),
        name="norms_joint_hidden",
    )(x, norms, joint_w, biases, expand_w, *(outs or ()))


def vector_kernel(*refs):
    vectors, (out, rows) = refs[:8], refs[8:]
    rows[...] = jnp.zeros_like(rows)
    row = 0
    for vector in vectors:
        for part in range(vector.shape[1] // 512):
            rows[row : row + 1, :] = vector[:, part * 512 : (part + 1) * 512].astype(
                jnp.float32
            )
            row += 1
    out[...] = rows[...].astype(jnp.bfloat16)


def stack_vectors(vectors):
    return pl.pallas_call(
        vector_kernel,
        in_specs=[VMEM] * 8,
        out_specs=VMEM,
        out_shape=shaped((16, 512), jnp.bfloat16),
        scratch_shapes=[pltpu.VMEM((16, 512), jnp.float32)],
        cost_estimate=pl.CostEstimate(flops=0, bytes_accessed=1 << 16, transcendentals=0),
        name="stack_vectors",
    )(*[v.reshape(1, -1) for v in vectors])


def slice_kernel(me, joint, expand, shrink, dense, tall, flat, pieces, sems):
    index = me[0]
    hidden = expand.shape[1] // 2
    width = joint.shape[1] // 3
    chip = pl.multiple_of((index // 2) * 128, 128)
    own = pl.multiple_of(index * 128, 128)
    copies = [
        pltpu.make_async_copy(
            joint.at[:, pl.ds(pl.multiple_of(i * width + chip, 128), 128)], pieces.at[i], sems.at[i]
        )
        for i in range(3)
    ]
    copies += [
        pltpu.make_async_copy(
            expand.at[:, pl.ds(pl.multiple_of(i * hidden + own, 128), 128)],
            tall.at[:, pl.ds(256 + 128 * i, 128)],
            sems.at[3 + i],
        )
        for i in range(2)
    ]
    copies.append(
        pltpu.make_async_copy(shrink.at[pl.ds(own, 128)], flat.at[pl.ds(0, 128)], sems.at[5])
    )
    start = pl.multiple_of(lax.rem(index, 8) * 64, 64)
    copies.append(
        pltpu.make_async_copy(dense.at[pl.ds(start, 64)], flat.at[pl.ds(128, 64)], sems.at[6])
    )
    for copy in copies:
        copy.start()
    for copy in copies:
        copy.wait()
    heads = [
        jnp.where(lax.rem(index, 2) == 0, pieces[i, :, 0:64], pieces[i, :, 64:128])
        for i in range(3)
    ]
    tall[:, 0:256] = jnp.concatenate(heads + [jnp.zeros_like(heads[0])], 1)


def slice_parameters(me, joint, expand, shrink, dense):
    rows = joint.shape[0]
    bf16 = jnp.bfloat16
    return pl.pallas_call(
        slice_kernel,
        in_specs=[SMEM] + [ANY] * 4,
        out_specs=[VMEM] * 2,
        out_shape=[shaped((rows, 512), bf16), shaped((192, 1024), bf16)],
        scratch_shapes=[
            pltpu.VMEM((3, rows, 128), bf16),
            pltpu.SemaphoreType.DMA((7,)),
        ],
        cost_estimate=pl.CostEstimate(flops=0, bytes_accessed=4 * MIB, transcendentals=0),
        name="slice_parameters",
    )(me, joint, expand, shrink, dense)


def join_kernel(at, tall, tall_other, vector, vector_other, *refs):
    joint_c, expand_c, tall_t, scaled, norms, shifts, biases, rows = refs
    head, group = at[0], at[1]
    size = tall.shape[0]
    for half in range(2):
        here = slice(half * size, (half + 1) * size)
        piece = jnp.where(group == half, tall[...], tall_other[...])
        joint_c[here, :] = piece[:, 0:256]
        expand_c[here, :] = piece[:, 256:512]
        tall_t[:, here] = piece.astype(jnp.float32).T.astype(jnp.bfloat16)
        rows[half] = jnp.where(group == half, vector[...], vector_other[...]).astype(jnp.float32)
        norms[0:4, here] = rows[half, 0:4, :]
        shifts[:, here] = rows[half, 4:5, :] + rows[half, 5:6, :]
    norms[4:8, :] = jnp.zeros((4, 2 * size), jnp.float32)
    scaled[0:256, :] = (tall_t[0:256, :].astype(jnp.float32) * norms[0:1, :]).astype(jnp.bfloat16)
    scaled[256:512, :] = (tall_t[256:512, :].astype(jnp.float32) * norms[2:3, :]).astype(
        jnp.bfloat16
    )
    numbers = lax.broadcasted_iota(jnp.int32, (16, 128), 0)

    def pick(half, row):
        block = jnp.where(half == 0, rows[0, :, lanes], rows[1, :, lanes])
        return jnp.sum(jnp.where(numbers == row, block, 0.0), 0, keepdims=True)

    parts = []
    lanes = pl.ds(pl.multiple_of((lax.rem(head, 8) // 2) * 128, 128), 128)
    for part in range(3):
        row = part * 2 + head // 8
        pair = pick(row // 3, 6 + lax.rem(row, 3))
        parts.append(jnp.where(lax.rem(head, 2) == 0, pair[:, 0:64], pair[:, 64:128]))
    lanes = pl.ds(pl.multiple_of(lax.rem(head, 4) * 128, 128), 128)
    biases[0:1, :] = jnp.concatenate(parts + [jnp.zeros_like(parts[0])], 1)
    for half in range(2):
        biases[1:2, half * 128 : (half + 1) * 128] = pick(half, 9 + head // 4)
    biases[2:8, :] = jnp.zeros((6, 256), jnp.float32)


def join_parameters(at, tall, tall_other, vector, vector_other):
    size = tall.shape[0]
    f32, bf16 = jnp.float32, jnp.bfloat16
    return pl.pallas_call(
        join_kernel,
        in_specs=[SMEM] + [VMEM] * 4,
        out_specs=[VMEM] * 7,
        out_shape=[
            shaped((2 * size, 256), bf16),
            shaped((2 * size, 256), bf16),
            shaped((512, 2 * size), bf16),
            shaped((512, 2 * size), bf16),
            shaped((8, 2 * size), f32),
            shaped((1, 2 * size), f32),
            shaped((8, 256), f32),
        ],
        scratch_shapes=[pltpu.VMEM((2, 16, 512), f32)],
        cost_estimate=pl.CostEstimate(flops=0, bytes_accessed=8 * MIB, transcendentals=0),
        name="join_parameters",
    )(at, tall, tall_other, vector, vector_other)


def tables(angle_rows):
    lanes = jnp.arange(128) % 64
    inverse = jnp.power(10000.0, -2.0 * (lanes % (ROT // 2)).astype(jnp.float32) / ROT)
    angles = angle_rows.astype(jnp.float32)[:, None] * jnp.where(lanes < ROT, inverse, 0.0)[None, :]
    return jnp.cos(angles), jnp.sin(angles)


def turn_kernel(blocks, joint, cos_far, sin_far, cos_near, sin_near, _, q_out, k_out, v_out):
    rows = joint.shape[0]
    lanes = lax.broadcasted_iota(jnp.int32, (BLOCK, 128), 1)

    def sort(s, _):
        p = blocks[s]
        source = pl.ds(pl.multiple_of(s * BLOCK, BLOCK), BLOCK)
        target = pl.ds(pl.multiple_of(p * BLOCK, BLOCK), BLOCK)
        far = pl.ds(p, 1)
        cosine = cos_far[far, :] * cos_near[...] - sin_far[far, :] * sin_near[...]
        sine = sin_far[far, :] * cos_near[...] + cos_far[far, :] * sin_near[...]
        pair = joint[source, 0:128]
        pair = pair * cosine + turn_back(pair, lanes) * sine
        q_out[target, :] = pair[:, 0:64].astype(jnp.bfloat16)
        k_out[target, :] = pair[:, 64:128].astype(jnp.bfloat16)
        v_out[target, :] = joint[source, 128:192].astype(jnp.bfloat16)
        return 0

    lax.fori_loop(0, rows // BLOCK, sort, 0, unroll=4)


def turn(blocks, joint, angles, gate):
    rows = joint.shape[0]
    head = shaped((rows, 64), jnp.bfloat16)
    return pl.pallas_call(
        turn_kernel,
        in_specs=[SMEM] + [VMEM] * 5 + [ANY],
        out_specs=[VMEM] * 3,
        out_shape=[head] * 3,
        compiler_params=pltpu.CompilerParams(vmem_limit_bytes=40 * MIB),
        cost_estimate=pl.CostEstimate(flops=0, bytes_accessed=rows * 2048, transcendentals=0),
        name="rotary_and_sort",
    )(blocks, joint, *angles, gate)


def below_diagonal():
    return lax.broadcasted_iota(jnp.int32, (TILE, TILE), 0) <= lax.broadcasted_iota(
        jnp.int32, (TILE, TILE), 1
    )


def forward_kernel(index, slots, q, k, v, *refs):
    mixed_out, out, lse = refs[-5:-2]
    buffer, sems = refs[-2:]
    tiles = q.shape[0] // TILE
    below = below_diagonal()
    parts = TILE // BLOCK
    copies = []
    for which, i in enumerate((index, tiles - 1 - index)):
        query = q[i * TILE : (i + 1) * TILE, :] * jnp.bfloat16(0.125)

        def step(j, carry, masked):
            top, total, acc = carry
            there = pl.ds(pl.multiple_of(j * TILE, TILE), TILE)
            scores = nt(k[there, :], query)
            if masked:
                scores = jnp.where(below, scores, negative)
            new_top = jnp.maximum(top, jnp.max(scores, 0, keepdims=True))
            weights = jnp.exp(scores - new_top)
            keep = jnp.exp(top - new_top)
            total = total * keep + jnp.sum(weights, 0, keepdims=True)
            return new_top, total, acc * keep + tn(v[there, :], weights.astype(jnp.bfloat16))

        carry = (
            jnp.full((1, TILE), negative, jnp.float32),
            jnp.zeros((1, TILE), jnp.float32),
            jnp.zeros((64, TILE), jnp.float32),
        )
        carry = lax.fori_loop(0, i, lambda j, c: step(j, c, False), carry)
        top, total, acc = step(i, carry, True)
        acc = acc / total
        here = slice(which * TILE, (which + 1) * TILE)
        out[:, here] = acc
        lse[:, here] = top + jnp.log(total)
        buffer[here, :] = acc.T.astype(jnp.bfloat16)
        for part in range(parts):
            slot = slots[i * parts + part]
            copies.append(
                pltpu.make_async_copy(
                    buffer.at[pl.ds(which * TILE + part * BLOCK, BLOCK)],
                    mixed_out.at[pl.ds(pl.multiple_of(slot * BLOCK, BLOCK), BLOCK)],
                    sems.at[which * parts + part],
                )
            )
            copies[-1].start()
    for copy in copies:
        copy.wait()


def attention_forward(index, slots, q, k, v, mixed, gate):
    rows = q.shape[0]
    extra = ([] if mixed is None else [mixed]) + ([] if gate is None else [gate])
    return pl.pallas_call(
        functools.partial(forward_kernel, index),
        in_specs=[SMEM] + [VMEM] * 3 + [ANY] * len(extra),
        out_specs=[ANY, VMEM, VMEM],
        out_shape=[
            shaped((rows, 64), jnp.bfloat16),
            shaped((64, 2 * TILE), jnp.float32),
            shaped((1, 2 * TILE), jnp.float32),
        ],
        scratch_shapes=[
            pltpu.VMEM((2 * TILE, 64), jnp.bfloat16),
            pltpu.SemaphoreType.DMA((2 * TILE // BLOCK,)),
        ],
        input_output_aliases={} if mixed is None else {4: 0},
        compiler_params=pltpu.CompilerParams(vmem_limit_bytes=40 * MIB),
        cost_estimate=pl.CostEstimate(
            flops=rows * rows * 256, bytes_accessed=rows * 1024, transcendentals=rows * rows // 8
        ),
        name="attention_forward",
    )(slots, q, k, v, *extra)


def fold(values):
    size = values.shape[0] // 4
    return jnp.concatenate([values[i * size : (i + 1) * size] for i in range(4)], 1)


def norm_rows(weight, grad, total, gain, shift):
    weight = weight.astype(jnp.float32)
    shift_grad = jnp.dot(total, weight, precision=lax.Precision.HIGHEST)
    gain_grad = (jnp.sum(weight * grad, 0, keepdims=True) - shift * shift_grad) / gain
    return jnp.concatenate([gain_grad, shift_grad], 0)


def post_kernel(pieces, last, group, *refs):
    blocks = refs[:pieces]
    slope, active, mixed, normed, shrink, dense, expand_t, norms = refs[pieces : pieces + 8]
    if last:
        before = refs[pieces + 10 : pieces + 15]
        kept, sent, norm_grads = refs[-4:-1]
        delta, mixed_grad, *sums = refs[-11:-4]
    else:
        delta, mixed_grad, *sums = refs[-8:-1]
    shrink_grad, dense_grad, expand_grad, column, delta_sum = sums
    held = refs[-1]
    step = pl.program_id(0)
    for n in range(pieces):

        @pl.when(step == n)
        def _(n=n):
            held[...] = blocks[n][...]

    @pl.when(step == 0)
    def _():
        for n, total in enumerate(sums):
            total[...] = before[n][...] if last else jnp.zeros_like(total)

    grad = held[...]
    column[...] += jnp.sum(grad.astype(jnp.float32), 0, keepdims=True)
    rounded = (nt(grad, shrink[...]) * slope[...]).astype(jnp.bfloat16)
    delta[...] = rounded
    delta_sum[...] += jnp.sum(rounded.astype(jnp.float32), 0, keepdims=True)
    mixed_grad[...] = nt(grad, dense[...]).astype(jnp.bfloat16)
    shrink_grad[...] += tn(active[...], grad)
    dense_grad[...] += tn(mixed[...], grad)
    expand_grad[...] += tn(rounded, normed[...])
    if not last:
        return

    @pl.when(step == pieces - 1)
    def _():
        half = expand_grad.shape[1] // 2
        this = group[0]
        across = expand_grad[...].T
        low, high = fold(across[:half]), fold(across[half:])
        kept[0:128, :] = shrink_grad[pl.ds(pl.multiple_of(this * 128, 128), 128), :]
        kept[128:192, :] = dense_grad[...]
        kept[192:320, :] = jnp.where(this == 0, low, high)
        other_rows = pl.ds(pl.multiple_of((1 - this) * 128, 128), 128)
        sent[0:128, :] = shrink_grad[other_rows, :].astype(jnp.bfloat16)
        sent[128:192, :] = dense_grad[...].astype(jnp.bfloat16)
        sent[192:320, :] = jnp.where(this == 0, high, low).astype(jnp.bfloat16)
        norm_grads[...] = norm_rows(
            expand_t[...], expand_grad[...], delta_sum[...], norms[2:3, :], norms[3:4, :]
        )


def post(group, blocks, first, before, slope, active, mixed, normed, shrink, dense, expand_t, norms):
    count = len(blocks)
    rows, width = blocks[0].shape
    total = slope.shape[0]
    last = before is not None
    row = lambda cols: pl.BlockSpec((rows, cols), lambda i: (first + i, 0))
    fixed = lambda shape: pl.BlockSpec(shape, lambda i: (0, 0))
    f32, bf16 = jnp.float32, jnp.bfloat16
    constants = (shrink, dense, expand_t, norms)
    sums = [(256, width), (64, width), (256, width), (1, width), (1, 256)]
    ends = [((320, width), f32), ((320, width), bf16), ((2, width), f32)] if last else []
    return pl.pallas_call(
        functools.partial(post_kernel, count, last),
        grid=(count,),
        in_specs=[SMEM]
        + [VMEM] * count
        + [row(256), row(256), row(64), row(width)]
        + [fixed(v.shape) for v in constants]
        + ([ANY] * 2 + [fixed(v) for v in sums] if last else []),
        out_specs=[row(256), row(64)]
        + [fixed(v) for v in sums]
        + [fixed(shape) for shape, _ in ends],
        out_shape=[shaped((total, 256), bf16), shaped((total, 64), bf16)]
        + [shaped(v, f32) for v in sums]
        + [shaped(*end) for end in ends],
        scratch_shapes=[pltpu.VMEM((rows, width), bf16)],
        input_output_aliases={count + 9: 0, count + 10: 1} if last else {},
        compiler_params=pltpu.CompilerParams(vmem_limit_bytes=44 * MIB),
        cost_estimate=pl.CostEstimate(
            flops=rows * count * width * 1800,
            bytes_accessed=rows * count * width * 6,
            transcendentals=0,
        ),
        name="cotangent_products",
    )(group, *blocks, slope, active, mixed, normed, *constants, *(before or ()))


def joint_products_kernel(group, normed, delta, joint_t, total, norms, kept, sent, norm_grads, acc):
    step = pl.program_id(0)

    @pl.when(step == 0)
    def _():
        acc[...] = jnp.zeros_like(acc)

    acc[...] += tn(delta[...], normed[...])

    @pl.when(step == pl.num_programs(0) - 1)
    def _():
        across = acc[...].T
        half = across.shape[0] // 2
        low, high = across[:half], across[half:]
        kept[...] = jnp.where(group[0] == 0, low, high)
        sent[...] = jnp.where(group[0] == 0, high, low).astype(jnp.bfloat16)
        norm_grads[...] = norm_rows(
            joint_t[...], acc[...], total[...], norms[0:1, :], norms[1:2, :]
        )


def joint_products(group, normed, delta, joint_t, total, norms):
    rows, width = normed.shape
    size = 1024
    row = lambda cols: pl.BlockSpec((size, cols), lambda i: (i, 0))
    fixed = lambda shape: pl.BlockSpec(shape, lambda i: (0, 0))
    f32, bf16 = jnp.float32, jnp.bfloat16
    return pl.pallas_call(
        joint_products_kernel,
        grid=(rows // size,),
        in_specs=[SMEM, row(width), row(256)] + [fixed(v.shape) for v in (joint_t, total, norms)],
        out_specs=[fixed((width // 2, 256)), fixed((width // 2, 256)), fixed((2, width))],
        out_shape=[
            shaped((width // 2, 256), f32),
            shaped((width // 2, 256), bf16),
            shaped((2, width), f32),
        ],
        scratch_shapes=[pltpu.VMEM((256, width), f32)],
        compiler_params=pltpu.CompilerParams(vmem_limit_bytes=40 * MIB),
        cost_estimate=pl.CostEstimate(
            flops=rows * width * 512, bytes_accessed=rows * width * 3, transcendentals=0
        ),
        name="joint_products",
    )(group, normed, delta, joint_t, total, norms)


def pair_kernel(core, mine, received, vectors, out):
    here = mine[pl.ds(pl.multiple_of(core[0] * 256, 256), 256), :]
    there = received[...]
    low = jnp.where(core[0] == 0, here, there)
    high = jnp.where(core[0] == 0, there, here)
    for part in range(3):
        lanes = slice(part * 64, part * 64 + 64)
        out[0:256, part * 128 : part * 128 + 128] = jnp.concatenate(
            [low[:, lanes], high[:, lanes]], 1
        )
    out[256:272, 0:256] = vectors[...]
    out[256:272, 256:384] = jnp.zeros((16, 128), out.dtype)


def pair_heads(core, mine, received, vectors):
    return pl.pallas_call(
        pair_kernel,
        in_specs=[SMEM] + [VMEM] * 3,
        out_specs=VMEM,
        out_shape=shaped((272, 384), jnp.bfloat16),
        cost_estimate=pl.CostEstimate(flops=0, bytes_accessed=1 << 20, transcendentals=0),
        name="pair_heads",
    )(core, mine, received, vectors)


def sort_grad_kernel(tiles, slots, mixed_grad, *refs):
    outs = refs[:tiles]
    grad, inner = refs[-2:]
    per_tile = TILE // BLOCK

    for p in range(slots.shape[0]):
        tile, part = divmod(p, per_tile)
        column = part * BLOCK
        if tile >= tiles:
            tile, column = 2 * tiles - 1 - tile, column + TILE
        source = pl.ds(pl.multiple_of(slots[p] * BLOCK, BLOCK), BLOCK)
        piece = mixed_grad[source, :]
        here = slice(p * BLOCK, (p + 1) * BLOCK)
        grad[here, :] = piece
        flat = piece.astype(jnp.float32).T
        inner[:, here] = jnp.sum(
            flat * outs[tile][:, column : column + BLOCK], 0, keepdims=True
        )


def sort_grad(slots, mixed_grad, outs):
    rows = mixed_grad.shape[0]
    return pl.pallas_call(
        functools.partial(sort_grad_kernel, len(outs)),
        in_specs=[SMEM] + [VMEM] * (1 + len(outs)),
        out_specs=[VMEM] * 2,
        out_shape=[shaped((rows, 64), jnp.bfloat16), shaped((1, rows), jnp.float32)],
        compiler_params=pltpu.CompilerParams(vmem_limit_bytes=40 * MIB),
        cost_estimate=pl.CostEstimate(flops=0, bytes_accessed=rows * 1024, transcendentals=0),
        name="sort_gradient",
    )(slots, mixed_grad, *outs)


def backward_kernel(index, first, q, k, v, grad, inner, lse, *refs):
    dq, dk, dv = refs[-3:]
    tiles = q.shape[0] // TILE
    below = below_diagonal()
    if first:
        dq[...] = jnp.zeros_like(dq)
    else:
        dq[...] = refs[0][...]
    for which, j in enumerate((index, tiles - 1 - index)):
        key = k[j * TILE : (j + 1) * TILE, :]
        value = v[j * TILE : (j + 1) * TILE, :]

        def step(i, carry, masked):
            key_grad, value_grad = carry
            here = pl.ds(pl.multiple_of(i * TILE, TILE), TILE)
            query = q[here, :] * jnp.bfloat16(0.125)
            out_grad = grad[here, :]
            probs = jnp.exp(nt(key, query) - lse[:, here])
            if masked:
                probs = jnp.where(below, probs, 0.0)
            score_grad = (probs * (nt(value, out_grad) - inner[:, here])).astype(jnp.bfloat16)
            value_grad = value_grad + nn(probs.astype(jnp.bfloat16), out_grad)
            key_grad = key_grad + nn(score_grad, query)
            dq[:, here] += tn(key, score_grad)
            return key_grad, value_grad

        zero = jnp.zeros((TILE, 64), jnp.float32)
        carry = step(j, (zero, zero), True)
        key_grad, value_grad = lax.fori_loop(
            j + 1, tiles, lambda i, c: step(i, c, False), carry
        )
        here = slice(which * TILE, (which + 1) * TILE)
        dk[here, :] = key_grad
        dv[here, :] = value_grad


def attention_backward(index, q, k, v, grad, inner, lse, dq, gate):
    rows = q.shape[0]
    extra = ([] if dq is None else [dq]) + ([] if gate is None else [gate])
    specs = ([] if dq is None else [VMEM]) + ([] if gate is None else [ANY])
    return pl.pallas_call(
        functools.partial(backward_kernel, index, dq is None),
        in_specs=[VMEM] * 6 + specs,
        out_specs=[VMEM] * 3,
        out_shape=[
            shaped((64, rows), jnp.float32),
            shaped((2 * TILE, 64), jnp.float32),
            shaped((2 * TILE, 64), jnp.float32),
        ],
        compiler_params=pltpu.CompilerParams(vmem_limit_bytes=40 * MIB),
        cost_estimate=pl.CostEstimate(
            flops=rows * rows * 640, bytes_accessed=rows * 2048, transcendentals=rows * rows // 8
        ),
        name="attention_backward",
    )(q, k, v, grad, inner, lse, *extra)


def finish_kernel(tiles, slots, dq, expand_delta, cos_far, sin_far, cos_near, sin_near, *refs):
    key_grads, value_grads = refs[:tiles], refs[tiles : 2 * tiles]
    delta, total = refs[-2:]
    delta[:, 256:512] = expand_delta[...]
    lanes = lax.broadcasted_iota(jnp.int32, (BLOCK, 128), 1)
    per_tile = TILE // BLOCK
    total[...] = jnp.zeros_like(total)
    for p in range(slots.shape[0]):
        tile, part = divmod(p, per_tile)
        row = part * BLOCK
        if tile >= tiles:
            tile, row = 2 * tiles - 1 - tile, row + TILE
        target = pl.ds(pl.multiple_of(slots[p] * BLOCK, BLOCK), BLOCK)
        cosine = cos_far[p : p + 1, :] * cos_near[...] - sin_far[p : p + 1, :] * sin_near[...]
        sine = sin_far[p : p + 1, :] * cos_near[...] + cos_far[p : p + 1, :] * sin_near[...]
        query = dq[:, p * BLOCK : (p + 1) * BLOCK].T * 0.125
        pair = jnp.concatenate([query, key_grads[tile][row : row + BLOCK, :]], 1)
        pair = (pair * cosine - turn_back(pair, lanes) * sine).astype(jnp.bfloat16)
        value = value_grads[tile][row : row + BLOCK, :]
        last = jnp.concatenate([value, jnp.zeros_like(value)], 1).astype(jnp.bfloat16)
        delta[target, 0:128] = pair
        delta[target, 128:256] = last
        total[:, 0:128] += jnp.sum(pair.astype(jnp.float32), 0, keepdims=True)
        total[:, 128:256] += jnp.sum(last.astype(jnp.float32), 0, keepdims=True)


def finish(slots, dq, expand_delta, angles, key_grads, value_grads):
    rows = dq.shape[1]
    return pl.pallas_call(
        functools.partial(finish_kernel, len(key_grads)),
        in_specs=[SMEM] + [VMEM] * (6 + 2 * len(key_grads)),
        out_specs=[VMEM] * 2,
        out_shape=[shaped((rows, 512), jnp.bfloat16), shaped((1, 256), jnp.float32)],
        compiler_params=pltpu.CompilerParams(vmem_limit_bytes=40 * MIB),
        cost_estimate=pl.CostEstimate(flops=0, bytes_accessed=rows * 2048, transcendentals=0),
        name="joint_delta",
    )(slots, dq, expand_delta, *angles, *key_grads, *value_grads)


def assemble_kernel(owners, blob, *refs):
    shrink, dense, expand, mark = refs[-7:-3]
    wide, tall, sems = refs[-3:]
    mark[...] = jnp.zeros_like(mark)
    group = owners[2]
    hidden = expand.shape[1] // 2
    size = blob.shape[0] // 2

    def dense_copy(n):
        return pltpu.make_async_copy(
            wide.at[n, pl.ds(128, 64)],
            dense.at[pl.ds(pl.multiple_of(lax.rem(owners[n], 8) * 64, 64), 64)],
            sems.at[n, 3],
        )

    copies = []
    for n in range(2):
        wide[n] = blob[n * size : n * size + 192, :].astype(jnp.float32)
        for quarter in range(4):
            tall[n, quarter * 128 : (quarter + 1) * 128, :] = blob[
                n * size + 192 : n * size + 320, quarter * 256 : (quarter + 1) * 256
            ].astype(jnp.float32)
        start = pl.multiple_of(owners[n] * 128, 128)
        copies += [
            pltpu.make_async_copy(
                wide.at[n, pl.ds(0, 128)], shrink.at[pl.ds(start, 128)], sems.at[n, 0]
            ),
            pltpu.make_async_copy(
                tall.at[n, :, pl.ds(0, 128)], expand.at[:, pl.ds(start, 128)], sems.at[n, 1]
            ),
            pltpu.make_async_copy(
                tall.at[n, :, pl.ds(128, 128)],
                expand.at[:, pl.ds(pl.multiple_of(hidden + start, 128), 128)],
                sems.at[n, 2],
            ),
        ]
        for copy in copies[-3:]:
            copy.start()

        @pl.when(owners[n] // 8 == group)
        def _(n=n):
            dense_copy(n).start()

    for copy in copies:
        copy.wait()
    for n in range(2):

        @pl.when(owners[n] // 8 == group)
        def _(n=n):
            dense_copy(n).wait()


def assemble(owners, blob, shapes, outs, gate):
    extra = [] if gate is None else [gate]
    return pl.pallas_call(
        assemble_kernel,
        in_specs=[SMEM, VMEM] + [ANY] * ((0 if outs is None else 3) + len(extra)),
        out_specs=[ANY] * 3 + [VMEM],
        out_shape=[shaped(s, jnp.float32) for s in (*shapes, (8, 128))],
        scratch_shapes=[
            pltpu.VMEM((2, 192, 1024), jnp.float32),
            pltpu.VMEM((2, 512, 256), jnp.float32),
            pltpu.SemaphoreType.DMA((2, 4)),
        ],
        input_output_aliases={} if outs is None else {2 + i: i for i in range(3)},
        compiler_params=pltpu.CompilerParams(vmem_limit_bytes=40 * MIB),
        cost_estimate=pl.CostEstimate(flops=0, bytes_accessed=640 * 6144, transcendentals=0),
        name="place_gradients",
    )(owners, blob, *(outs or ()), *extra)


def assemble_joint_kernel(count, owners, *refs):
    blobs = refs[:count]
    joint, mark, held, buffer, sems, arrivals = refs[count:]
    mark[...] = jnp.zeros_like(mark)
    width = joint.shape[1] // 3
    size = blobs[0].shape[0] // 2
    fetches = [
        pltpu.make_async_copy(blobs[n], held.at[n], arrivals.at[n]) for n in range(count)
    ]
    for fetch in fetches:
        fetch.start()
    copies = []
    for n in range(2 * count):
        owner = owners[n]
        first = (n % 2) * size
        if n % 2 == 0:
            fetches[n // 2].wait()
        buffer[n] = held[n // 2, first : first + 256, :].astype(jnp.float32)
        top = pl.multiple_of(lax.rem(owner, 2) * 256, 256)
        for part in range(3):
            start = pl.multiple_of(part * width + (owner // 2) * 128, 128)
            copies.append(
                pltpu.make_async_copy(
                    buffer.at[n, :, pl.ds(part * 128, 128)],
                    joint.at[pl.ds(top, 256), pl.ds(start, 128)],
                    sems.at[n, part],
                )
            )
            copies[-1].start()
    for copy in copies:
        copy.wait()


def assemble_joint(owners, blobs, shape):
    count = len(blobs)
    return pl.pallas_call(
        functools.partial(assemble_joint_kernel, count),
        in_specs=[SMEM] + [ANY] * count,
        out_specs=[ANY, VMEM],
        out_shape=[shaped(shape, jnp.float32), shaped((8, 128), jnp.float32)],
        scratch_shapes=[
            pltpu.VMEM((count, *blobs[0].shape), jnp.bfloat16),
            pltpu.VMEM((2 * count, 256, 384), jnp.float32),
            pltpu.SemaphoreType.DMA((2 * count, 3)),
            pltpu.SemaphoreType.DMA((count,)),
        ],
        compiler_params=pltpu.CompilerParams(vmem_limit_bytes=40 * MIB),
        cost_estimate=pl.CostEstimate(
            flops=0, bytes_accessed=count * 512 * 384 * 6, transcendentals=0
        ),
        name="place_joint_gradient",
    )(owners, *blobs)


def split_heads(
    tokens,
    cotangent,
    first_gain,
    first_shift,
    second_gain,
    second_shift,
    joint_weight,
    joint_bias,
    dense_weight,
    dense_bias,
    expand_weight,
    expand_bias,
    shrink_weight,
    shrink_bias,
    block_order,
):
    f32, bf16 = jnp.float32, jnp.bfloat16
    me = lax.axis_index("ctx")
    group = lax.axis_index("fsdp")
    core = me % 2
    rows, width = tokens.shape[1:]
    total_rows = rows * 16
    hidden = expand_weight.shape[1] // 2
    own_tokens, own_upstream = tokens[0], cotangent[0]

    token_pair = jnp.concatenate([own_tokens, swap(own_tokens)], 0)
    token_hops = [gather_hop(token_pair, 1)]

    at = after(me, token_pair)
    scalars = jnp.stack([at, group]).astype(jnp.int32)
    tall, flat = slice_parameters(
        scalars, joint_weight, expand_weight, shrink_weight, dense_weight
    )
    tall_other = other(tall)
    vector = stack_vectors(
        lax.optimization_barrier(
            (
                first_gain,
                first_shift,
                second_gain,
                second_shift,
                dense_bias,
                shrink_bias,
                joint_bias,
                expand_bias,
                tall,
            )
        )[:8]
    )
    joint_c, expand_c, tall_t, scaled, norms, shifts, biases = join_parameters(
        scalars, tall, tall_other, vector, other(vector)
    )
    flat_other = other(after(flat, tall_other))
    shrink_pair = [jnp.where(group == i, flat[:128], flat_other[:128]) for i in range(2)]
    shrink_c = jnp.concatenate(shrink_pair, 0)
    dense_c = jnp.where(group == me // 8, flat[128:], flat_other[128:])

    owners = piece_owners(at)
    blocks = after(block_order, token_pair).reshape(16, 2)[owners].reshape(32)
    count = jnp.arange(32, dtype=jnp.int32)
    slots = jnp.sum(jnp.where(blocks[None, :] == count[:, None], count[None, :], 0), 1)
    near = after(jnp.arange(BLOCK), token_pair)
    angles = tables(jnp.arange(total_rows // BLOCK) * BLOCK) + tables(near)

    normal, flags = None, []

    def take(block):
        nonlocal normal
        *normal, flag = pre(
            len(flags), block, norms, joint_c, biases, expand_c, normal, 8
        )
        flags.append(flag)

    def far_pair(far):
        return jnp.concatenate([far, swap(far)], 0)

    take(token_pair)
    token_hops.append(gather_hop(token_hops[0], 2, tall, vector))
    take(token_hops[0])
    take(swap(token_hops[0]))
    token_hops.append(gather_hop(token_hops[1], 3, flags[0]))
    take(token_hops[1])
    take(swap(token_hops[1]))
    token_hops.append(gather_hop(token_hops[2], 4, flags[3]))
    upstream_pair = jnp.concatenate([own_upstream, swap(after(own_upstream, flags[0]))], 0)
    upstream_hops = [gather_hop(upstream_pair, 1, token_hops[2], flags[3])]
    take(token_hops[2])
    take(swap(token_hops[2]))
    take(far_pair(token_hops[3]))
    normed_one, normed_two, joint, activated, slope = normal
    query, key, value = turn(blocks, joint, angles, upstream_hops[0])

    mixed, outs, sums = None, [], []

    def attend(index, gate):
        nonlocal mixed
        mixed, out, lse = attention_forward(index, slots, query, key, value, mixed, gate)
        outs.append(out)
        sums.append(lse)

    upstream_hops.append(gather_hop(upstream_hops[0], 2, flags[6]))
    attend(0, None)
    upstream_hops.append(gather_hop(upstream_hops[1], 3, query))
    attend(1, upstream_hops[1])
    attend(2, upstream_hops[1])
    upstream_hops.append(gather_hop(upstream_hops[2], 4, sums[0]))
    attend(3, upstream_hops[2])
    upstream_blocks = [upstream_pair]
    for held in upstream_hops[:3]:
        upstream_blocks += [held, swap(held)]
    upstream_blocks.append(far_pair(upstream_hops[3]))
    lse = jnp.concatenate(
        [s[:, :TILE] for s in sums] + [s[:, TILE:] for s in sums[::-1]], 1
    )

    branch = jnp.concatenate([activated, mixed], 1)
    back = jnp.concatenate([shrink_c, dense_c], 0)
    this = group[None].astype(jnp.int32)

    def products(blocks, first, before, normed):
        return post(
            this,
            blocks,
            first,
            before,
            slope,
            activated,
            mixed,
            normed,
            shrink_c,
            dense_c,
            tall_t[256:],
            norms,
        )

    early = products(upstream_blocks[:4], 0, None, normed_two)
    out_hops = [hop(after(scatter_term(branch, back, 4), upstream_hops[3]))]
    term = scatter_term(branch, back, 3, out_hops[0])
    out_hops.append(hop(term))
    expand_delta, mixed_grad, _, _, _, column_sum, expand_sum, kept, sent, norm_two = products(
        upstream_blocks[4:], 4, early, after(normed_two, term)
    )
    term = scatter_term(branch, back, 2, out_hops[1])
    out_hops.append(hop(after(term, expand_sum)))
    out_grad, inner = sort_grad(slots, after(mixed_grad, term), outs)
    blob_other = other(sent)

    dq, key_grads, value_grads = None, [], []

    def attend_back(index, gate):
        nonlocal dq
        dq, dk, dv = attention_backward(
            index, query, key, value, out_grad, inner, lse, dq, gate
        )
        key_grads.append(dk)
        value_grads.append(dv)

    attend_back(0, term)
    attend_back(1, term)
    term = scatter_term(branch, back, 1, out_hops[2])
    out_hops.append(hop(after(term, key_grads[0])))
    blob = (kept + after(blob_other, key_grads[0]).astype(f32)).astype(bf16)
    blob_pair = jnp.concatenate([blob, swap(blob)], 0)
    blob_hops = [gather_hop(blob_pair, 1, out_hops[2])]
    attend_back(2, term)
    out_sum = scatter_last(branch, back, out_hops[3])
    output = own_tokens.astype(f32) + out_sum + shifts
    attend_back(3, out_hops[3])
    blob_hops.append(gather_hop(blob_hops[0], 2))
    delta, joint_sum = finish(slots, dq, expand_delta, angles, key_grads, value_grads)

    far_term = scatter_term(delta, scaled, 4)
    in_hops = [hop(far_term)]
    in_hops.append(hop(scatter_term(delta, scaled, 3, in_hops[0])))
    joint_kept, joint_sent, norm_one = joint_products(
        this, after(normed_one, in_hops[0]), delta, tall_t[:256], joint_sum, norms
    )

    def rows_of(which):
        norm_part = jnp.concatenate([norm_one, norm_two], 0).reshape(4, 2, 2, 256)
        column_part = column_sum.reshape(2, 2, 256)
        return jnp.concatenate(
            [
                cut(norm_part, which, 1, 1).reshape(8, 256),
                cut(column_part, which, 1, 0).reshape(2, 256),
                joint_sum,
                expand_sum,
                jnp.zeros((4, 256), f32),
            ],
            0,
        )

    sent = jnp.concatenate([joint_sent, rows_of(1 - group).astype(bf16)], 0)
    received = other(sent).astype(f32)
    half = width // 2
    packed = rows_of(group) + received[half:]
    joint_half = (joint_kept + received[:half]).astype(bf16)
    exchanged = swap(cut(joint_half, (1 - core) * (half // 2), half // 2, 0))
    joint_blob = pair_heads(
        core[None].astype(jnp.int32), joint_half, exchanged, packed.astype(bf16)
    )
    joint_pair = jnp.concatenate([joint_blob, swap(joint_blob)], 0)

    placed, marks = None, []
    shapes = ((hidden, width), (half, width), (half, 2 * hidden))

    def place(block, gate):
        nonlocal placed
        some = owners[2 * len(marks) : 2 * len(marks) + 2]
        *placed, mark = assemble(
            jnp.concatenate([some, this]).astype(jnp.int32), block, shapes, placed, gate
        )
        marks.append(mark)

    blob_hops.append(gather_hop(blob_hops[1], 3))
    place(blob_pair, in_hops[0])
    place(blob_hops[0], in_hops[0])
    place(swap(blob_hops[0]), in_hops[0])
    joint_hops = [gather_hop(joint_pair, 1)]
    in_hops.append(hop(after(scatter_term(delta, scaled, 2, in_hops[1]), marks[2])))
    blob_hops.append(gather_hop(blob_hops[2], 4, in_hops[0]))
    joint_hops.append(gather_hop(joint_hops[0], 2, in_hops[0]))
    place(blob_hops[1], in_hops[1])
    place(swap(blob_hops[1]), in_hops[1])
    in_hops.append(hop(after(scatter_term(delta, scaled, 1, in_hops[2]), marks[4])))
    joint_hops.append(gather_hop(joint_hops[1], 3, in_hops[1]))
    joint_hops.append(gather_hop(joint_hops[2], 4, in_hops[2]))
    place(blob_hops[2], in_hops[2])
    place(swap(blob_hops[2]), in_hops[2])
    place(far_pair(blob_hops[3]), in_hops[2])
    shrink_total, dense_total, expand_total = placed
    joint_blocks = [joint_pair]
    for held in joint_hops[:3]:
        joint_blocks += [held, swap(held)]
    joint_blocks.append(far_pair(joint_hops[3]))
    joint_total, mark = assemble_joint(owners, joint_blocks, (half, 3 * width))
    in_sum = scatter_last(delta, scaled, after(in_hops[3], mark, marks[7]))
    mine = own_tokens.astype(f32)
    mine = mine - jnp.mean(mine, -1, keepdims=True)
    scale = lax.rsqrt(jnp.mean(mine * mine, -1, keepdims=True) + epsilon)
    mine = mine * scale
    term = scale * (
        in_sum
        - jnp.mean(in_sum, -1, keepdims=True)
        - mine * jnp.mean(in_sum * mine, -1, keepdims=True)
    )
    tokens_grad = (own_upstream.astype(f32) + term).astype(bf16)

    pieces = [b[i : i + 16, :256].astype(f32) for b in joint_blocks for i in (256, 528)]
    totals = sum(p[:8] for p in pieces).reshape(4, half)
    order = (owners[None, :] == jnp.arange(16, dtype=jnp.int32)[:, None]).astype(f32)
    sums = jnp.stack([p[10:12] for p in pieces])
    sums = jnp.sum(order[:, :, None, None] * sums[None], 1)
    joint_bias_total = jnp.transpose(sums[:, 0, :192].reshape(16, 3, 64), (1, 0, 2)).reshape(-1)
    expand_bias_total = jnp.transpose(sums[:, 1].reshape(16, 2, 128), (1, 0, 2)).reshape(-1)
    column_total = packed[8:10].reshape(-1)

    return (
        output.astype(bf16)[None],
        tokens_grad[None],
        totals[0],
        totals[1],
        totals[2],
        totals[3],
        joint_total,
        cut(joint_bias_total, group * 3 * half, 3 * half, 0),
        dense_total,
        column_total,
        expand_total,
        cut(expand_bias_total, group * hidden, hidden, 0),
        shrink_total,
        column_total,
    )


def solution(mesh):
    fits = mesh.shape["ctx"] == HEADS and mesh.shape["fsdp"] == 2
    return jax.shard_map(
        split_heads if fits else shards,
        mesh=mesh,
        in_specs=(
            P("fsdp", "ctx", None),
            P("fsdp", "ctx", None),
            P("fsdp"),
            P("fsdp"),
            P("fsdp"),
            P("fsdp"),
            P("fsdp", None),
            P("fsdp"),
            P("fsdp", None),
            P("fsdp"),
            P("fsdp", None),
            P("fsdp"),
            P("fsdp", None),
            P("fsdp"),
            P(),
        ),
        out_specs=(
            P("fsdp", "ctx", None),
            P("fsdp", "ctx", None),
            P("fsdp"),
            P("fsdp"),
            P("fsdp"),
            P("fsdp"),
            P("fsdp", None),
            P("fsdp"),
            P("fsdp", None),
            P("fsdp"),
            P("fsdp", None),
            P("fsdp"),
            P("fsdp", None),
            P("fsdp"),
        ),
        check_vma=False,
    )
```

```python
import functools

import jax
import jax.numpy as jnp
from jax import lax
from jax.experimental import pallas as pl
from jax.experimental.pallas import tpu as pltpu
from jax.sharding import PartitionSpec as P

HEADS = 16
ROT = 16


epsilon = 1e-05
negative = -1e30


def normalize(values, gain, shift):
    center = values - jnp.mean(values, -1, keepdims=True)
    spread = jnp.mean(center * center, -1, keepdims=True)
    return center * lax.rsqrt(spread + epsilon) * gain + shift


def turn_tables(positions):
    inverse = jnp.power(10000.0, -2.0 * jnp.arange(ROT // 2, dtype=jnp.float32) / ROT)
    angles = positions.astype(jnp.float32)[:, None] * inverse[None, :]
    angles = jnp.concatenate([angles, angles], -1)[:, None, :]
    return (jnp.cos(angles), jnp.sin(angles))


def rotate(values, cosine, sine):
    half = ROT // 2
    front = values[..., :ROT]
    turned = jnp.concatenate([-front[..., half:], front[..., :half]], -1)
    return jnp.concatenate([front * cosine + turned * sine, values[..., ROT:]], -1)


def contract(left, right, left_dim, right_dim):
    return lax.dot_general(
        left, right, (((left_dim,), (right_dim,)), ((), ())), preferred_element_type=jnp.float32
    )


def shards(
    tokens,
    cotangent,
    first_gain,
    first_shift,
    second_gain,
    second_shift,
    joint_weight,
    joint_bias,
    dense_weight,
    dense_bias,
    expand_weight,
    expand_bias,
    shrink_weight,
    shrink_bias,
    block_order,
):
    rows = tokens.shape[1]
    width = tokens.shape[2]
    head_dim = width // HEADS
    scale = head_dim ** (-0.5)
    groups = lax.axis_size("ctx")
    half_rows = rows // 2
    (
        gain_one,
        shift_one,
        gain_two,
        shift_two,
        joint_full,
        joint_shift,
        dense_full,
        dense_shift,
        expand_full,
        expand_shift,
        shrink_full,
        shrink_shift,
    ) = (
        lax.all_gather(first_gain, "fsdp", axis=0, tiled=True),
        lax.all_gather(first_shift, "fsdp", axis=0, tiled=True),
        lax.all_gather(second_gain, "fsdp", axis=0, tiled=True),
        lax.all_gather(second_shift, "fsdp", axis=0, tiled=True),
        lax.all_gather(joint_weight, "fsdp", axis=0, tiled=True),
        lax.all_gather(joint_bias, "fsdp", axis=0, tiled=True),
        lax.all_gather(dense_weight, "fsdp", axis=0, tiled=True),
        lax.all_gather(dense_bias, "fsdp", axis=0, tiled=True),
        lax.all_gather(expand_weight, "fsdp", axis=0, tiled=True),
        lax.all_gather(expand_bias, "fsdp", axis=0, tiled=True),
        lax.all_gather(shrink_weight, "fsdp", axis=0, tiled=True),
        lax.all_gather(shrink_bias, "fsdp", axis=0, tiled=True),
    )
    gain_one = gain_one.astype(jnp.float32)
    shift_one = shift_one.astype(jnp.float32)
    gain_two = gain_two.astype(jnp.float32)
    shift_two = shift_two.astype(jnp.float32)
    all_positions = (
        block_order[:, None] * half_rows + jnp.arange(half_rows, dtype=jnp.int32)[None, :]
    ).reshape(rows * groups)
    positions = lax.dynamic_slice_in_dim(all_positions, lax.axis_index("ctx") * rows, rows)
    cosine, sine = turn_tables(positions)
    visible = positions[:, None] >= all_positions[None, :]
    inputs = tokens[0].astype(jnp.float32)
    normed_one = normalize(inputs, gain_one, shift_one).astype(jnp.bfloat16)
    normed_two = normalize(inputs, gain_two, shift_two).astype(jnp.bfloat16)
    joint = jnp.dot(
        normed_one, joint_full, preferred_element_type=jnp.float32
    ) + joint_shift.astype(jnp.float32)
    queries = (
        rotate(joint[:, :width].reshape(rows, HEADS, head_dim), cosine, sine)
        .reshape(rows, width)
        .astype(jnp.bfloat16)
    )
    key_rows = (
        rotate(joint[:, width : 2 * width].reshape(rows, HEADS, head_dim), cosine, sine)
        .reshape(rows, width)
        .astype(jnp.bfloat16)
    )
    value_rows = joint[:, 2 * width :].astype(jnp.bfloat16)
    all_keys, all_values = (
        lax.all_gather(key_rows, "ctx", axis=0, tiled=True),
        lax.all_gather(value_rows, "ctx", axis=0, tiled=True),
    )

    def head_scores(head, key_source):
        query = lax.dynamic_slice_in_dim(queries, head * head_dim, head_dim, 1)
        key_cols = lax.dynamic_slice_in_dim(key_source, head * head_dim, head_dim, 1)
        scores = contract(query, key_cols, 1, 1) * scale
        return (query, key_cols, jnp.where(visible, scores, negative))

    def head_forward(head):
        query, key_cols, scores = head_scores(head, all_keys)
        top = jnp.max(scores, -1, keepdims=True)
        total = jnp.sum(jnp.exp(scores - top), -1, keepdims=True)
        log_total = top + jnp.log(total)
        weights = jnp.exp(scores - log_total).astype(jnp.bfloat16)
        value_cols = lax.dynamic_slice_in_dim(all_values, head * head_dim, head_dim, 1)
        return (jnp.dot(weights, value_cols, preferred_element_type=jnp.float32), log_total[:, 0])

    mixed, log_totals = lax.map(head_forward, jnp.arange(HEADS))
    attended = jnp.transpose(mixed, (1, 0, 2)).reshape(rows, width).astype(jnp.bfloat16)
    expanded = jnp.dot(
        normed_two, expand_full, preferred_element_type=jnp.float32
    ) + expand_shift.astype(jnp.float32)
    activated = jax.nn.gelu(expanded, approximate=False).astype(jnp.bfloat16)
    output = (
        inputs
        + jnp.dot(attended, dense_full, preferred_element_type=jnp.float32)
        + dense_shift.astype(jnp.float32)
    )
    output = (
        output
        + jnp.dot(activated, shrink_full, preferred_element_type=jnp.float32)
        + shrink_shift.astype(jnp.float32)
    )
    upstream = cotangent[0]
    upstream_float = upstream.astype(jnp.float32)
    column_sum = jnp.sum(upstream_float, 0)
    dense_grad = contract(attended, upstream, 0, 0)
    shrink_grad = contract(activated, upstream, 0, 0)
    act_grad = contract(upstream, shrink_full, 1, 1)
    _, gelu_pull = jax.vjp(lambda value: jax.nn.gelu(value, approximate=False), expanded)
    expand_delta = gelu_pull(act_grad)[0].astype(jnp.bfloat16)
    expand_grad = contract(normed_two, expand_delta, 0, 0)
    expand_bias_grad = jnp.sum(expand_delta.astype(jnp.float32), 0)
    normed_two_grad = contract(expand_delta, expand_full, 1, 1)
    _, pull_two = jax.vjp(normalize, inputs, gain_two, shift_two)
    input_two, gain_two_grad, shift_two_grad = pull_two(normed_two_grad)
    attended_grad = contract(upstream, dense_full, 1, 1).astype(jnp.bfloat16)
    key_source, value_source = (all_keys, all_values)

    def head_backward(items):
        head, log_total = items
        query, key_cols, scores = head_scores(head, key_source)
        probs = jnp.exp(scores - log_total[:, None])
        value_cols = lax.dynamic_slice_in_dim(value_source, head * head_dim, head_dim, 1)
        out_grad = lax.dynamic_slice_in_dim(attended_grad, head * head_dim, head_dim, 1)
        prob_grad = contract(out_grad, value_cols, 1, 1)
        inner = jnp.sum(probs * prob_grad, -1, keepdims=True)
        score_grad = (probs * (prob_grad - inner)).astype(jnp.bfloat16)
        query_grad = jnp.dot(score_grad, key_cols, preferred_element_type=jnp.float32) * scale
        key_grad = contract(score_grad, query, 0, 0) * scale
        value_grad = contract(probs.astype(jnp.bfloat16), out_grad, 0, 0)
        return (query_grad, key_grad, value_grad)

    query_grads, key_grads, value_grads = lax.map(head_backward, (jnp.arange(HEADS), log_totals))
    key_sums, value_sums = (
        lax.psum_scatter(
            key_grads.astype(jnp.bfloat16), "ctx", scatter_dimension=1, tiled=True
        ).astype(jnp.float32),
        lax.psum_scatter(
            value_grads.astype(jnp.bfloat16), "ctx", scatter_dimension=1, tiled=True
        ).astype(jnp.float32),
    )
    query_back = rotate(jnp.transpose(query_grads, (1, 0, 2)), cosine, -sine).reshape(rows, width)
    key_back = rotate(jnp.transpose(key_sums, (1, 0, 2)), cosine, -sine).reshape(rows, width)
    value_back = jnp.transpose(value_sums, (1, 0, 2)).reshape(rows, width)
    joint_delta = jnp.concatenate([query_back, key_back, value_back], 1).astype(jnp.bfloat16)
    joint_grad = contract(normed_one, joint_delta, 0, 0)
    joint_bias_grad = jnp.sum(joint_delta.astype(jnp.float32), 0)
    normed_one_grad = contract(joint_delta, joint_full, 1, 1)
    _, pull_one = jax.vjp(normalize, inputs, gain_one, shift_one)
    input_one, gain_one_grad, shift_one_grad = pull_one(normed_one_grad)
    tokens_grad = (upstream_float + input_one + input_two).astype(jnp.bfloat16)
    (
        gain_one_part,
        shift_one_part,
        gain_two_part,
        shift_two_part,
        joint_part,
        joint_bias_part,
        dense_part,
        column_part,
        expand_part,
        expand_bias_part,
        shrink_part,
    ) = (
        lax.psum_scatter(
            gain_one_grad.astype(jnp.bfloat16), "fsdp", scatter_dimension=0, tiled=True
        ).astype(jnp.float32),
        lax.psum_scatter(
            shift_one_grad.astype(jnp.bfloat16), "fsdp", scatter_dimension=0, tiled=True
        ).astype(jnp.float32),
        lax.psum_scatter(
            gain_two_grad.astype(jnp.bfloat16), "fsdp", scatter_dimension=0, tiled=True
        ).astype(jnp.float32),
        lax.psum_scatter(
            shift_two_grad.astype(jnp.bfloat16), "fsdp", scatter_dimension=0, tiled=True
        ).astype(jnp.float32),
        lax.psum_scatter(
            joint_grad.astype(jnp.bfloat16), "fsdp", scatter_dimension=0, tiled=True
        ).astype(jnp.float32),
        lax.psum_scatter(
            joint_bias_grad.astype(jnp.bfloat16), "fsdp", scatter_dimension=0, tiled=True
        ).astype(jnp.float32),
        lax.psum_scatter(
            dense_grad.astype(jnp.bfloat16), "fsdp", scatter_dimension=0, tiled=True
        ).astype(jnp.float32),
        lax.psum_scatter(
            column_sum.astype(jnp.bfloat16), "fsdp", scatter_dimension=0, tiled=True
        ).astype(jnp.float32),
        lax.psum_scatter(
            expand_grad.astype(jnp.bfloat16), "fsdp", scatter_dimension=0, tiled=True
        ).astype(jnp.float32),
        lax.psum_scatter(
            expand_bias_grad.astype(jnp.bfloat16), "fsdp", scatter_dimension=0, tiled=True
        ).astype(jnp.float32),
        lax.psum_scatter(
            shrink_grad.astype(jnp.bfloat16), "fsdp", scatter_dimension=0, tiled=True
        ).astype(jnp.float32),
    )
    (
        gain_one_total,
        shift_one_total,
        gain_two_total,
        shift_two_total,
        joint_total,
        joint_bias_total,
        dense_total,
        column_total,
        expand_total,
        expand_bias_total,
        shrink_total,
    ) = (
        lax.psum(gain_one_part.astype(jnp.bfloat16), "ctx").astype(jnp.float32),
        lax.psum(shift_one_part.astype(jnp.bfloat16), "ctx").astype(jnp.float32),
        lax.psum(gain_two_part.astype(jnp.bfloat16), "ctx").astype(jnp.float32),
        lax.psum(shift_two_part.astype(jnp.bfloat16), "ctx").astype(jnp.float32),
        lax.psum(joint_part.astype(jnp.bfloat16), "ctx").astype(jnp.float32),
        lax.psum(joint_bias_part.astype(jnp.bfloat16), "ctx").astype(jnp.float32),
        lax.psum(dense_part.astype(jnp.bfloat16), "ctx").astype(jnp.float32),
        lax.psum(column_part.astype(jnp.bfloat16), "ctx").astype(jnp.float32),
        lax.psum(expand_part.astype(jnp.bfloat16), "ctx").astype(jnp.float32),
        lax.psum(expand_bias_part.astype(jnp.bfloat16), "ctx").astype(jnp.float32),
        lax.psum(shrink_part.astype(jnp.bfloat16), "ctx").astype(jnp.float32),
    )
    return (
        output.astype(jnp.bfloat16)[None],
        tokens_grad[None],
        gain_one_total,
        shift_one_total,
        gain_two_total,
        shift_two_total,
        joint_total,
        joint_bias_total,
        dense_total,
        column_total,
        expand_total,
        expand_bias_total,
        shrink_total,
        column_total,
    )

CYCLE = (0, 2, 4, 6, 7, 5, 3, 1)
RING = tuple((2 * CYCLE[i], 2 * CYCLE[(i + 1) % 8]) for i in range(8)) + tuple(
    (2 * CYCLE[i] + 1, 2 * CYCLE[i - 1] + 1) for i in range(8)
)
SWAP = tuple((i, i ^ 1) for i in range(16))
TILE = 512
BLOCK = 128
MIB = 1024 * 1024


def hop(values):
    return lax.ppermute(values, "ctx", RING)


def swap(values):
    return lax.ppermute(values, "ctx", SWAP)


def other(values):
    return lax.ppermute(values, "fsdp", ((0, 1), (1, 0)))


def after(values, *others):
    return lax.optimization_barrier((values, *others))[0]


def cut(values, start, size, axis):
    return lax.dynamic_slice_in_dim(values, start, size, axis)


def gather_hop(held, step, *gates):
    if step == 4:
        held = held[: held.shape[0] // 2]
    return hop(after(held, *gates) if gates else held)


def piece_owners(me):
    core = me % 2
    piece = jnp.arange(16, dtype=jnp.int32)
    pair = piece // 2
    step = jnp.where(pair % 2 == 1, (pair + 1) // 2, -(pair // 2)) * (2 * core - 1)
    along = me // 4
    place = (jnp.where((me // 2) % 2 == 0, along, 7 - along) + step + 8) % 8
    chip = jnp.where(place < 4, 2 * place, 15 - 2 * place)
    other_first = (pair % 2 == 0) & (pair > 0)
    return 2 * chip + (piece + core + other_first) % 2


def scatter_term(values, weight, step, held=None):
    rows = values.shape[0] // 16
    f32, bf16 = jnp.float32, jnp.bfloat16

    def term(first, count):
        return nn(values[first * rows : (first + count) * rows], weight)

    if step == 4:
        return (term(14, 1) + swap(term(15, 1).astype(bf16)).astype(f32)).astype(bf16)
    mine = term(4 * step, 2) + swap(term(4 * step - 2, 2).astype(bf16)).astype(f32)
    if step == 3:
        held = jnp.pad(held, ((rows, 0), (0, 0)))
    return (mine + held.astype(f32)).astype(bf16)


def turn_back(values, lanes):
    ahead = pltpu.roll(values, 128 - ROT // 2, 1)
    behind = pltpu.roll(values, ROT // 2, 1)
    return jnp.where(lanes % 64 < ROT // 2, -ahead, behind)


def nt(left_side, right_side):
    return lax.dot_general(
        left_side, right_side, (((1,), (1,)), ((), ())), preferred_element_type=jnp.float32
    )


def nn(left_side, right_side):
    return jnp.dot(left_side, right_side, preferred_element_type=jnp.float32)


def tn(left_side, right_side):
    return lax.dot_general(
        left_side, right_side, (((0,), (0,)), ((), ())), preferred_element_type=jnp.float32
    )


VMEM = pl.BlockSpec(memory_space=pltpu.VMEM)
SMEM = pl.BlockSpec(memory_space=pltpu.SMEM)
ANY = pl.BlockSpec(memory_space=pl.ANY)


def cost(flops, bytes_accessed, transcendentals, share=1):
    return pl.CostEstimate(
        flops=int(flops * share),
        bytes_accessed=int(bytes_accessed * share),
        transcendentals=int(transcendentals * share),
    )


def shaped(shape, dtype):
    return jax.ShapeDtypeStruct(shape, dtype)


def pre_kernel(x, norms, joint_w, biases, expand_w, *refs):
    one, two, joint, active, slope, done = refs[-6:]
    done[...] = jnp.zeros_like(done)
    wide = x[...].astype(jnp.float32)
    center = wide - jnp.mean(wide, -1, keepdims=True)
    spread = jnp.mean(center * center, -1, keepdims=True)
    unit = center * lax.rsqrt(spread + epsilon)
    normed_one = (unit * norms[0:1, :] + norms[1:2, :]).astype(jnp.bfloat16)
    normed_two = (unit * norms[2:3, :] + norms[3:4, :]).astype(jnp.bfloat16)
    one[...] = normed_one
    two[...] = normed_two
    joint[...] = nn(normed_one, joint_w[...]) + biases[0:1, :]
    expanded = nn(normed_two, expand_w[...]) + biases[1:2, :]
    share = 0.5 + 0.5 * lax.erf(expanded * (0.5**0.5))
    active[...] = (expanded * share).astype(jnp.bfloat16)
    slope[...] = share + expanded * (jnp.exp(-0.5 * expanded * expanded) * 0.3989422804014327)


def pre(index, x, norms, joint_w, biases, expand_w, outs, count):
    rows, width = x.shape
    step = rows // 2
    fixed = lambda shape: pl.BlockSpec(shape, lambda i: (0, 0))
    place = lambda cols: pl.BlockSpec((step, cols), lambda i: (2 * index + i, 0))
    total = rows * count
    bf16, f32 = jnp.bfloat16, jnp.float32
    aliases = {} if outs is None else {5 + i: i for i in range(5)}
    return pl.pallas_call(
        pre_kernel,
        grid=(2,),
        in_specs=[pl.BlockSpec((step, width), lambda i: (i, 0))]
        + [fixed(v.shape) for v in (norms, joint_w, biases, expand_w)]
        + [ANY] * len(aliases),
        out_specs=[place(width), place(width), place(256), place(256), place(256), fixed((8, 128))],
        out_shape=[
            pltpu.HBM((total, width), bf16),
            pltpu.HBM((total, width), bf16),
            pltpu.HBM((total, 256), f32),
            pltpu.HBM((total, 256), bf16),
            pltpu.HBM((total, 256), f32),
            shaped((8, 128), f32),
        ],
        input_output_aliases=aliases,
        compiler_params=pltpu.CompilerParams(vmem_limit_bytes=40 * MIB),
        cost_estimate=cost(
            flops=rows * width * 1024,
            bytes_accessed=rows * width * 10,
            transcendentals=rows * 512,
            share=1,
        ),
        name="norms_joint_hidden",
    )(x, norms, joint_w, biases, expand_w, *(outs or ()))


def vector_kernel(*refs):
    vectors, (out, rows) = refs[:8], refs[8:]
    rows[...] = jnp.zeros_like(rows)
    row = 0
    for vector in vectors:
        for part in range(vector.shape[1] // 512):
            rows[row : row + 1, :] = vector[:, part * 512 : (part + 1) * 512].astype(
                jnp.float32
            )
            row += 1
    out[...] = rows[...].astype(jnp.bfloat16)


def stack_vectors(vectors):
    return pl.pallas_call(
        vector_kernel,
        in_specs=[VMEM] * 8,
        out_specs=VMEM,
        out_shape=shaped((16, 512), jnp.bfloat16),
        scratch_shapes=[pltpu.VMEM((16, 512), jnp.float32)],
        cost_estimate=cost(flops=0, bytes_accessed=1 << 16, transcendentals=0),
        name="stack_vectors",
    )(*[v.reshape(1, -1) for v in vectors])


def slice_kernel(me, joint, expand, shrink, dense, tall, flat, pieces, sems):
    index = me[0]
    hidden = expand.shape[1] // 2
    width = joint.shape[1] // 3
    chip = pl.multiple_of((index // 2) * 128, 128)
    own = pl.multiple_of(index * 128, 128)
    copies = [
        pltpu.make_async_copy(
            joint.at[:, pl.ds(pl.multiple_of(i * width + chip, 128), 128)], pieces.at[i], sems.at[i]
        )
        for i in range(3)
    ]
    copies += [
        pltpu.make_async_copy(
            expand.at[:, pl.ds(pl.multiple_of(i * hidden + own, 128), 128)],
            tall.at[:, pl.ds(256 + 128 * i, 128)],
            sems.at[3 + i],
        )
        for i in range(2)
    ]
    copies.append(
        pltpu.make_async_copy(shrink.at[pl.ds(own, 128)], flat.at[pl.ds(0, 128)], sems.at[5])
    )
    start = pl.multiple_of(lax.rem(index, 8) * 64, 64)
    copies.append(
        pltpu.make_async_copy(dense.at[pl.ds(start, 64)], flat.at[pl.ds(128, 64)], sems.at[6])
    )
    for copy in copies:
        copy.start()
    for copy in copies:
        copy.wait()
    heads = [
        jnp.where(lax.rem(index, 2) == 0, pieces[i, :, 0:64], pieces[i, :, 64:128])
        for i in range(3)
    ]
    tall[:, 0:256] = jnp.concatenate(heads + [jnp.zeros_like(heads[0])], 1)


def slice_parameters(me, joint, expand, shrink, dense):
    rows = joint.shape[0]
    bf16 = jnp.bfloat16
    return pl.pallas_call(
        slice_kernel,
        in_specs=[SMEM] + [ANY] * 4,
        out_specs=[VMEM] * 2,
        out_shape=[shaped((rows, 512), bf16), shaped((192, 1024), bf16)],
        scratch_shapes=[
            pltpu.VMEM((3, rows, 128), bf16),
            pltpu.SemaphoreType.DMA((7,)),
        ],
        cost_estimate=cost(flops=0, bytes_accessed=4 * MIB, transcendentals=0),
        name="slice_parameters",
    )(me, joint, expand, shrink, dense)


def join_kernel(at, tall, tall_other, vector, vector_other, *refs):
    joint_c, expand_c, tall_t, scaled, norms, shifts, biases, rows = refs
    head, group = at[0], at[1]
    size = tall.shape[0]
    for half in range(2):
        here = slice(half * size, (half + 1) * size)
        piece = jnp.where(group == half, tall[...], tall_other[...])
        joint_c[here, :] = piece[:, 0:256]
        expand_c[here, :] = piece[:, 256:512]
        tall_t[:, here] = piece.astype(jnp.float32).T.astype(jnp.bfloat16)
        rows[half] = jnp.where(group == half, vector[...], vector_other[...]).astype(jnp.float32)
        norms[0:4, here] = rows[half, 0:4, :]
        shifts[:, here] = rows[half, 4:5, :] + rows[half, 5:6, :]
    norms[4:8, :] = jnp.zeros((4, 2 * size), jnp.float32)
    scaled[0:256, :] = (tall_t[0:256, :].astype(jnp.float32) * norms[0:1, :]).astype(jnp.bfloat16)
    scaled[256:512, :] = (tall_t[256:512, :].astype(jnp.float32) * norms[2:3, :]).astype(
        jnp.bfloat16
    )
    numbers = lax.broadcasted_iota(jnp.int32, (16, 128), 0)

    def pick(half, row):
        block = jnp.where(half == 0, rows[0, :, lanes], rows[1, :, lanes])
        return jnp.sum(jnp.where(numbers == row, block, 0.0), 0, keepdims=True)

    parts = []
    lanes = pl.ds(pl.multiple_of((lax.rem(head, 8) // 2) * 128, 128), 128)
    for part in range(3):
        row = part * 2 + head // 8
        pair = pick(row // 3, 6 + lax.rem(row, 3))
        parts.append(jnp.where(lax.rem(head, 2) == 0, pair[:, 0:64], pair[:, 64:128]))
    lanes = pl.ds(pl.multiple_of(lax.rem(head, 4) * 128, 128), 128)
    biases[0:1, :] = jnp.concatenate(parts + [jnp.zeros_like(parts[0])], 1)
    for half in range(2):
        biases[1:2, half * 128 : (half + 1) * 128] = pick(half, 9 + head // 4)
    biases[2:8, :] = jnp.zeros((6, 256), jnp.float32)


def join_parameters(at, tall, tall_other, vector, vector_other):
    size = tall.shape[0]
    f32, bf16 = jnp.float32, jnp.bfloat16
    return pl.pallas_call(
        join_kernel,
        in_specs=[SMEM] + [VMEM] * 4,
        out_specs=[VMEM] * 7,
        out_shape=[
            shaped((2 * size, 256), bf16),
            shaped((2 * size, 256), bf16),
            shaped((512, 2 * size), bf16),
            shaped((512, 2 * size), bf16),
            shaped((8, 2 * size), f32),
            shaped((1, 2 * size), f32),
            shaped((8, 256), f32),
        ],
        scratch_shapes=[pltpu.VMEM((2, 16, 512), f32)],
        cost_estimate=cost(flops=0, bytes_accessed=8 * MIB, transcendentals=0),
        name="join_parameters",
    )(at, tall, tall_other, vector, vector_other)


def tables(angle_rows):
    lanes = jnp.arange(128) % 64
    inverse = jnp.power(10000.0, -2.0 * (lanes % (ROT // 2)).astype(jnp.float32) / ROT)
    angles = angle_rows.astype(jnp.float32)[:, None] * jnp.where(lanes < ROT, inverse, 0.0)[None, :]
    return jnp.cos(angles), jnp.sin(angles)


def turn_kernel(blocks, joint, cos_far, sin_far, cos_near, sin_near, _, q_out, k_out, v_out):
    rows = joint.shape[0]
    lanes = lax.broadcasted_iota(jnp.int32, (BLOCK, 128), 1)

    def sort(s, _):
        p = blocks[s]
        source = pl.ds(pl.multiple_of(s * BLOCK, BLOCK), BLOCK)
        target = pl.ds(pl.multiple_of(p * BLOCK, BLOCK), BLOCK)
        far = pl.ds(p, 1)
        cosine = cos_far[far, :] * cos_near[...] - sin_far[far, :] * sin_near[...]
        sine = sin_far[far, :] * cos_near[...] + cos_far[far, :] * sin_near[...]
        pair = joint[source, 0:128]
        pair = pair * cosine + turn_back(pair, lanes) * sine
        q_out[target, :] = pair[:, 0:64].astype(jnp.bfloat16)
        k_out[target, :] = pair[:, 64:128].astype(jnp.bfloat16)
        v_out[target, :] = joint[source, 128:192].astype(jnp.bfloat16)
        return 0

    lax.fori_loop(0, rows // BLOCK, sort, 0, unroll=4)


def turn(blocks, joint, angles, gate):
    rows = joint.shape[0]
    head = shaped((rows, 64), jnp.bfloat16)
    return pl.pallas_call(
        turn_kernel,
        in_specs=[SMEM] + [VMEM] * 5 + [ANY],
        out_specs=[VMEM] * 3,
        out_shape=[head] * 3,
        compiler_params=pltpu.CompilerParams(vmem_limit_bytes=40 * MIB),
        cost_estimate=cost(flops=0, bytes_accessed=rows * 2048, transcendentals=0),
        name="rotary_and_sort",
    )(blocks, joint, *angles, gate)


def below_diagonal():
    return lax.broadcasted_iota(jnp.int32, (TILE, TILE), 0) <= lax.broadcasted_iota(
        jnp.int32, (TILE, TILE), 1
    )


def forward_kernel(index, slots, q, k, v, *refs):
    mixed_out, out, lse = refs[-5:-2]
    buffer, sems = refs[-2:]
    tiles = q.shape[0] // TILE
    below = below_diagonal()
    parts = TILE // BLOCK
    copies = []
    for which, i in enumerate((index, tiles - 1 - index)):
        query = q[i * TILE : (i + 1) * TILE, :] * jnp.bfloat16(0.125)

        def step(j, carry, masked):
            top, total, acc = carry
            there = pl.ds(pl.multiple_of(j * TILE, TILE), TILE)
            scores = nt(k[there, :], query)
            if masked:
                scores = jnp.where(below, scores, negative)
            new_top = jnp.maximum(top, jnp.max(scores, 0, keepdims=True))
            weights = jnp.exp(scores - new_top)
            keep = jnp.exp(top - new_top)
            total = total * keep + jnp.sum(weights, 0, keepdims=True)
            return new_top, total, acc * keep + tn(v[there, :], weights.astype(jnp.bfloat16))

        carry = (
            jnp.full((1, TILE), negative, jnp.float32),
            jnp.zeros((1, TILE), jnp.float32),
            jnp.zeros((64, TILE), jnp.float32),
        )
        carry = lax.fori_loop(0, i, lambda j, c: step(j, c, False), carry, unroll=True)
        top, total, acc = step(i, carry, True)
        acc = acc / total
        here = slice(which * TILE, (which + 1) * TILE)
        out[:, here] = acc
        lse[:, here] = top + jnp.log(total)
        buffer[here, :] = acc.T.astype(jnp.bfloat16)
        for part in range(parts):
            slot = slots[i * parts + part]
            copies.append(
                pltpu.make_async_copy(
                    buffer.at[pl.ds(which * TILE + part * BLOCK, BLOCK)],
                    mixed_out.at[pl.ds(pl.multiple_of(slot * BLOCK, BLOCK), BLOCK)],
                    sems.at[which * parts + part],
                )
            )
            copies[-1].start()
    for copy in copies:
        copy.wait()


def attention_forward(index, slots, q, k, v, mixed, gate):
    rows = q.shape[0]
    extra = ([] if mixed is None else [mixed]) + ([] if gate is None else [gate])
    return pl.pallas_call(
        functools.partial(forward_kernel, index),
        in_specs=[SMEM] + [VMEM] * 3 + [ANY] * len(extra),
        out_specs=[ANY, VMEM, VMEM],
        out_shape=[
            shaped((rows, 64), jnp.bfloat16),
            shaped((64, 2 * TILE), jnp.float32),
            shaped((1, 2 * TILE), jnp.float32),
        ],
        scratch_shapes=[
            pltpu.VMEM((2 * TILE, 64), jnp.bfloat16),
            pltpu.SemaphoreType.DMA((2 * TILE // BLOCK,)),
        ],
        input_output_aliases={} if mixed is None else {4: 0},
        compiler_params=pltpu.CompilerParams(vmem_limit_bytes=40 * MIB),
        cost_estimate=cost(
            flops=rows * rows * 256, bytes_accessed=rows * 1024, transcendentals=rows * rows // 8
        ),
        name="attention_forward",
    )(slots, q, k, v, *extra)


def fold(values):
    size = values.shape[0] // 4
    return jnp.concatenate([values[i * size : (i + 1) * size] for i in range(4)], 1)


def norm_rows(weight, grad, total, gain, shift):
    weight = weight.astype(jnp.float32)
    shift_grad = jnp.dot(total, weight, precision=lax.Precision.HIGHEST)
    gain_grad = (jnp.sum(weight * grad, 0, keepdims=True) - shift * shift_grad) / gain
    return jnp.concatenate([gain_grad, shift_grad], 0)


def post_kernel(pieces, last, group, *refs):
    blocks = refs[:pieces]
    slope, active, mixed, normed, shrink, dense, expand_t, norms = refs[pieces : pieces + 8]
    if last:
        before = refs[pieces + 10 : pieces + 15]
        kept, sent, norm_grads = refs[-4:-1]
        delta, mixed_grad, *sums = refs[-11:-4]
    else:
        delta, mixed_grad, *sums = refs[-8:-1]
    shrink_grad, dense_grad, expand_grad, column, delta_sum = sums
    held = refs[-1]
    step = pl.program_id(0)
    for n in range(pieces):

        @pl.when(step == n)
        def _(n=n):
            held[...] = blocks[n][...]

    @pl.when(step == 0)
    def _():
        for n, total in enumerate(sums):
            total[...] = before[n][...] if last else jnp.zeros_like(total)

    grad = held[...]
    column[...] += jnp.sum(grad.astype(jnp.float32), 0, keepdims=True)
    rounded = (nt(grad, shrink[...]) * slope[...]).astype(jnp.bfloat16)
    delta[...] = rounded
    delta_sum[...] += jnp.sum(rounded.astype(jnp.float32), 0, keepdims=True)
    mixed_grad[...] = nt(grad, dense[...]).astype(jnp.bfloat16)
    shrink_grad[...] += tn(active[...], grad)
    dense_grad[...] += tn(mixed[...], grad)
    expand_grad[...] += tn(rounded, normed[...])
    if not last:
        return

    @pl.when(step == pieces - 1)
    def _():
        half = expand_grad.shape[1] // 2
        this = group[0]
        across = expand_grad[...].T
        low, high = fold(across[:half]), fold(across[half:])
        kept[0:128, :] = shrink_grad[pl.ds(pl.multiple_of(this * 128, 128), 128), :]
        kept[128:192, :] = dense_grad[...]
        kept[192:320, :] = jnp.where(this == 0, low, high)
        other_rows = pl.ds(pl.multiple_of((1 - this) * 128, 128), 128)
        sent[0:128, :] = shrink_grad[other_rows, :].astype(jnp.bfloat16)
        sent[128:192, :] = dense_grad[...].astype(jnp.bfloat16)
        sent[192:320, :] = jnp.where(this == 0, high, low).astype(jnp.bfloat16)
        norm_grads[...] = norm_rows(
            expand_t[...], expand_grad[...], delta_sum[...], norms[2:3, :], norms[3:4, :]
        )


def post(group, blocks, first, before, slope, active, mixed, normed, shrink, dense, expand_t, norms):
    count = len(blocks)
    rows, width = blocks[0].shape
    total = slope.shape[0]
    last = before is not None
    row = lambda cols: pl.BlockSpec((rows, cols), lambda i: (first + i, 0))
    fixed = lambda shape: pl.BlockSpec(shape, lambda i: (0, 0))
    f32, bf16 = jnp.float32, jnp.bfloat16
    constants = (shrink, dense, expand_t, norms)
    sums = [(256, width), (64, width), (256, width), (1, width), (1, 256)]
    ends = [((320, width), f32), ((320, width), bf16), ((2, width), f32)] if last else []
    return pl.pallas_call(
        functools.partial(post_kernel, count, last),
        grid=(count,),
        in_specs=[SMEM]
        + [VMEM] * count
        + [row(256), row(256), row(64), row(width)]
        + [fixed(v.shape) for v in constants]
        + ([ANY] * 2 + [fixed(v) for v in sums] if last else []),
        out_specs=[row(256), row(64)]
        + [fixed(v) for v in sums]
        + [fixed(shape) for shape, _ in ends],
        out_shape=[shaped((total, 256), bf16), shaped((total, 64), bf16)]
        + [shaped(v, f32) for v in sums]
        + [shaped(*end) for end in ends],
        scratch_shapes=[pltpu.VMEM((rows, width), bf16)],
        input_output_aliases={count + 9: 0, count + 10: 1} if last else {},
        compiler_params=pltpu.CompilerParams(vmem_limit_bytes=44 * MIB),
        cost_estimate=cost(
            flops=rows * count * width * 1800,
            bytes_accessed=rows * count * width * 6,
            transcendentals=0,
        ),
        name="cotangent_products",
    )(group, *blocks, slope, active, mixed, normed, *constants, *(before or ()))


def joint_products_kernel(group, normed, delta, joint_t, total, norms, kept, sent, norm_grads, acc):
    step = pl.program_id(0)

    @pl.when(step == 0)
    def _():
        acc[...] = jnp.zeros_like(acc)

    acc[...] += tn(delta[...], normed[...])

    @pl.when(step == pl.num_programs(0) - 1)
    def _():
        across = acc[...].T
        half = across.shape[0] // 2
        low, high = across[:half], across[half:]
        kept[...] = jnp.where(group[0] == 0, low, high)
        sent[...] = jnp.where(group[0] == 0, high, low).astype(jnp.bfloat16)
        norm_grads[...] = norm_rows(
            joint_t[...], acc[...], total[...], norms[0:1, :], norms[1:2, :]
        )


def joint_products(group, normed, delta, joint_t, total, norms):
    rows, width = normed.shape
    size = 1024
    row = lambda cols: pl.BlockSpec((size, cols), lambda i: (i, 0))
    fixed = lambda shape: pl.BlockSpec(shape, lambda i: (0, 0))
    f32, bf16 = jnp.float32, jnp.bfloat16
    return pl.pallas_call(
        joint_products_kernel,
        grid=(rows // size,),
        in_specs=[SMEM, row(width), row(256)] + [fixed(v.shape) for v in (joint_t, total, norms)],
        out_specs=[fixed((width // 2, 256)), fixed((width // 2, 256)), fixed((2, width))],
        out_shape=[
            shaped((width // 2, 256), f32),
            shaped((width // 2, 256), bf16),
            shaped((2, width), f32),
        ],
        scratch_shapes=[pltpu.VMEM((256, width), f32)],
        compiler_params=pltpu.CompilerParams(vmem_limit_bytes=40 * MIB),
        cost_estimate=cost(
            flops=rows * width * 512, bytes_accessed=rows * width * 3, transcendentals=0
        ),
        name="joint_products",
    )(group, normed, delta, joint_t, total, norms)


def pair_kernel(core, mine, received, vectors, out):
    here = mine[pl.ds(pl.multiple_of(core[0] * 256, 256), 256), :]
    there = received[...]
    low = jnp.where(core[0] == 0, here, there)
    high = jnp.where(core[0] == 0, there, here)
    for part in range(3):
        lanes = slice(part * 64, part * 64 + 64)
        out[0:256, part * 128 : part * 128 + 128] = jnp.concatenate(
            [low[:, lanes], high[:, lanes]], 1
        )
    out[256:272, 0:256] = vectors[...]
    out[256:272, 256:384] = jnp.zeros((16, 128), out.dtype)


def pair_heads(core, mine, received, vectors):
    return pl.pallas_call(
        pair_kernel,
        in_specs=[SMEM] + [VMEM] * 3,
        out_specs=VMEM,
        out_shape=shaped((272, 384), jnp.bfloat16),
        cost_estimate=cost(flops=0, bytes_accessed=1 << 20, transcendentals=0),
        name="pair_heads",
    )(core, mine, received, vectors)


def sort_grad_kernel(tiles, slots, mixed_grad, *refs):
    outs = refs[:tiles]
    grad, inner = refs[-2:]
    per_tile = TILE // BLOCK

    for p in range(slots.shape[0]):
        tile, part = divmod(p, per_tile)
        column = part * BLOCK
        if tile >= tiles:
            tile, column = 2 * tiles - 1 - tile, column + TILE
        source = pl.ds(pl.multiple_of(slots[p] * BLOCK, BLOCK), BLOCK)
        piece = mixed_grad[source, :]
        here = slice(p * BLOCK, (p + 1) * BLOCK)
        grad[here, :] = piece
        flat = piece.astype(jnp.float32).T
        inner[:, here] = jnp.sum(
            flat * outs[tile][:, column : column + BLOCK], 0, keepdims=True
        )


def sort_grad(slots, mixed_grad, outs):
    rows = mixed_grad.shape[0]
    return pl.pallas_call(
        functools.partial(sort_grad_kernel, len(outs)),
        in_specs=[SMEM] + [VMEM] * (1 + len(outs)),
        out_specs=[VMEM] * 2,
        out_shape=[shaped((rows, 64), jnp.bfloat16), shaped((1, rows), jnp.float32)],
        compiler_params=pltpu.CompilerParams(vmem_limit_bytes=40 * MIB),
        cost_estimate=cost(flops=0, bytes_accessed=rows * 1024, transcendentals=0),
        name="sort_gradient",
    )(slots, mixed_grad, *outs)


def backward_kernel(index, first, q, k, v, grad, inner, lse, *refs):
    dq, dk, dv = refs[-3:]
    tiles = q.shape[0] // TILE
    below = below_diagonal()
    if first:
        dq[...] = jnp.zeros_like(dq)
    else:
        dq[...] = refs[0][...]
    for which, j in enumerate((index, tiles - 1 - index)):
        key = k[j * TILE : (j + 1) * TILE, :]
        value = v[j * TILE : (j + 1) * TILE, :]

        def step(i, carry, masked):
            key_grad, value_grad = carry
            here = pl.ds(pl.multiple_of(i * TILE, TILE), TILE)
            query = q[here, :] * jnp.bfloat16(0.125)
            out_grad = grad[here, :]
            probs = jnp.exp(nt(key, query) - lse[:, here])
            if masked:
                probs = jnp.where(below, probs, 0.0)
            score_grad = (probs * (nt(value, out_grad) - inner[:, here])).astype(jnp.bfloat16)
            value_grad = value_grad + nn(probs.astype(jnp.bfloat16), out_grad)
            key_grad = key_grad + nn(score_grad, query)
            dq[:, here] += tn(key, score_grad)
            return key_grad, value_grad

        zero = jnp.zeros((TILE, 64), jnp.float32)
        carry = step(j, (zero, zero), True)
        key_grad, value_grad = lax.fori_loop(
            j + 1, tiles, lambda i, c: step(i, c, False), carry, unroll=True
        )
        here = slice(which * TILE, (which + 1) * TILE)
        dk[here, :] = key_grad
        dv[here, :] = value_grad


def attention_backward(index, q, k, v, grad, inner, lse, dq, gate):
    rows = q.shape[0]
    extra = ([] if dq is None else [dq]) + ([] if gate is None else [gate])
    specs = ([] if dq is None else [VMEM]) + ([] if gate is None else [ANY])
    return pl.pallas_call(
        functools.partial(backward_kernel, index, dq is None),
        in_specs=[VMEM] * 6 + specs,
        out_specs=[VMEM] * 3,
        out_shape=[
            shaped((64, rows), jnp.float32),
            shaped((2 * TILE, 64), jnp.float32),
            shaped((2 * TILE, 64), jnp.float32),
        ],
        compiler_params=pltpu.CompilerParams(vmem_limit_bytes=40 * MIB),
        cost_estimate=cost(
            flops=rows * rows * 640, bytes_accessed=rows * 2048, transcendentals=rows * rows // 8
        ),
        name="attention_backward",
    )(q, k, v, grad, inner, lse, *extra)


def finish_kernel(tiles, slots, dq, expand_delta, cos_far, sin_far, cos_near, sin_near, *refs):
    key_grads, value_grads = refs[:tiles], refs[tiles : 2 * tiles]
    delta, total = refs[-2:]
    delta[:, 256:512] = expand_delta[...]
    lanes = lax.broadcasted_iota(jnp.int32, (BLOCK, 128), 1)
    per_tile = TILE // BLOCK
    total[...] = jnp.zeros_like(total)
    for p in range(slots.shape[0]):
        tile, part = divmod(p, per_tile)
        row = part * BLOCK
        if tile >= tiles:
            tile, row = 2 * tiles - 1 - tile, row + TILE
        target = pl.ds(pl.multiple_of(slots[p] * BLOCK, BLOCK), BLOCK)
        cosine = cos_far[p : p + 1, :] * cos_near[...] - sin_far[p : p + 1, :] * sin_near[...]
        sine = sin_far[p : p + 1, :] * cos_near[...] + cos_far[p : p + 1, :] * sin_near[...]
        query = dq[:, p * BLOCK : (p + 1) * BLOCK].T * 0.125
        pair = jnp.concatenate([query, key_grads[tile][row : row + BLOCK, :]], 1)
        pair = (pair * cosine - turn_back(pair, lanes) * sine).astype(jnp.bfloat16)
        value = value_grads[tile][row : row + BLOCK, :]
        last = jnp.concatenate([value, jnp.zeros_like(value)], 1).astype(jnp.bfloat16)
        delta[target, 0:128] = pair
        delta[target, 128:256] = last
        total[:, 0:128] += jnp.sum(pair.astype(jnp.float32), 0, keepdims=True)
        total[:, 128:256] += jnp.sum(last.astype(jnp.float32), 0, keepdims=True)


def finish(slots, dq, expand_delta, angles, key_grads, value_grads):
    rows = dq.shape[1]
    return pl.pallas_call(
        functools.partial(finish_kernel, len(key_grads)),
        in_specs=[SMEM] + [VMEM] * (6 + 2 * len(key_grads)),
        out_specs=[VMEM] * 2,
        out_shape=[shaped((rows, 512), jnp.bfloat16), shaped((1, 256), jnp.float32)],
        compiler_params=pltpu.CompilerParams(vmem_limit_bytes=40 * MIB),
        cost_estimate=cost(flops=0, bytes_accessed=rows * 2048, transcendentals=0),
        name="joint_delta",
    )(slots, dq, expand_delta, *angles, *key_grads, *value_grads)


def pair_kernel_rows(own, partner, _, out):
    size = own.shape[0]
    out[:size, :] = own[...]
    out[size:, :] = partner[...]


def pair_up(own, partner, gate):
    rows, width = own.shape
    return pl.pallas_call(
        pair_kernel_rows,
        in_specs=[VMEM, VMEM, ANY],
        out_specs=VMEM,
        out_shape=shaped((2 * rows, width), own.dtype),
        cost_estimate=cost(flops=0, bytes_accessed=rows * width * 8, transcendentals=0),
        name="pair_of_pieces",
    )(own, partner, gate)


def first_kernel(pair, *refs):
    refs[-1][...] = pair[...]


def first_piece(pair, *gates):
    rows, width = pair.shape[0] // 2, pair.shape[1]
    block = pl.BlockSpec((rows, width), lambda i: (0, 0))
    return pl.pallas_call(
        first_kernel,
        grid=(1,),
        in_specs=[block] + [ANY] * len(gates),
        out_specs=block,
        out_shape=shaped((rows, width), pair.dtype),
        cost_estimate=cost(flops=0, bytes_accessed=rows * width * 4, transcendentals=0),
        name="first_piece",
    )(pair, *gates)


def sum_kernel(kept, received, _, out):
    out[...] = (kept[...] + received[...].astype(jnp.float32)).astype(out.dtype)


def sum_pieces(kept, received, gate):
    rows, width = kept.shape
    return pl.pallas_call(
        sum_kernel,
        in_specs=[VMEM, VMEM, ANY],
        out_specs=VMEM,
        out_shape=shaped((rows, width), jnp.bfloat16),
        cost_estimate=cost(flops=0, bytes_accessed=rows * width * 8, transcendentals=0),
        name="sum_of_pieces",
    )(kept, received, gate)


def last_kernel(values, weight, held, *refs):
    own, sent = refs[-2:]
    rows = own.shape[0]
    own[...] = nn(values[:rows, :], weight[...]) + held[rows:, :].astype(jnp.float32)
    term = nn(values[rows:, :], weight[...]) + held[:rows, :].astype(jnp.float32)
    sent[...] = term.astype(jnp.bfloat16)


def scatter_last(values, weight, held, *gates):
    rows, width = held.shape[0] // 2, held.shape[1]
    depth = values.shape[1]
    fixed = lambda shape: pl.BlockSpec(shape, lambda i: (0, 0))
    return pl.pallas_call(
        last_kernel,
        grid=(1,),
        in_specs=[fixed((2 * rows, depth)), fixed(weight.shape), fixed(held.shape)]
        + [ANY] * len(gates),
        out_specs=[fixed((rows, width))] * 2,
        out_shape=[shaped((rows, width), jnp.float32), shaped((rows, width), jnp.bfloat16)],
        cost_estimate=cost(
            flops=4 * rows * depth * width, bytes_accessed=rows * width * 10, transcendentals=0
        ),
        name="last_sums",
    )(values, weight, held, *gates)


def input_grad_kernel(tokens, upstream, own, received, out):
    x = tokens[...].astype(jnp.float32)
    x = x - jnp.mean(x, -1, keepdims=True)
    scale = lax.rsqrt(jnp.mean(x * x, -1, keepdims=True) + epsilon)
    x = x * scale
    grad = own[...] + received[...].astype(jnp.float32)
    term = grad - jnp.mean(grad, -1, keepdims=True) - x * jnp.mean(grad * x, -1, keepdims=True)
    out[...] = (upstream[...].astype(jnp.float32) + scale * term).astype(out.dtype)


def input_grad(tokens, upstream, own, received):
    rows, width = tokens.shape
    return pl.pallas_call(
        input_grad_kernel,
        in_specs=[VMEM] * 4,
        out_specs=VMEM,
        out_shape=shaped((rows, width), jnp.bfloat16),
        cost_estimate=cost(flops=0, bytes_accessed=rows * width * 12, transcendentals=0),
        name="input_gradient",
    )(tokens, upstream, own, received)


def assemble_kernel(owners, first, second, *refs):
    shrink, dense, expand, mark = refs[-7:-3]
    wide, tall, sems = refs[-3:]
    mark[...] = jnp.zeros_like(mark)
    group = owners[4]
    hidden = expand.shape[1] // 2
    size = first.shape[0] // 2

    def dense_copy(n):
        return pltpu.make_async_copy(
            wide.at[n, pl.ds(128, 64)],
            dense.at[pl.ds(pl.multiple_of(lax.rem(owners[n], 8) * 64, 64), 64)],
            sems.at[n, 3],
        )

    copies = []
    for n in range(4):
        blob = (first, second)[n // 2]
        top = (n % 2) * size
        wide[n] = blob[top : top + 192, :].astype(jnp.float32)
        start = pl.multiple_of(owners[n] * 128, 128)
        copies.append(
            pltpu.make_async_copy(
                wide.at[n, pl.ds(0, 128)], shrink.at[pl.ds(start, 128)], sems.at[n, 0]
            )
        )
        copies[-1].start()

        @pl.when(owners[n] // 8 == group)
        def _(n=n):
            dense_copy(n).start()

        for quarter in range(4):
            tall[n, quarter * 128 : (quarter + 1) * 128, :] = blob[
                top + 192 : top + 320, quarter * 256 : (quarter + 1) * 256
            ].astype(jnp.float32)
        copies += [
            pltpu.make_async_copy(
                tall.at[n, :, pl.ds(0, 128)], expand.at[:, pl.ds(start, 128)], sems.at[n, 1]
            ),
            pltpu.make_async_copy(
                tall.at[n, :, pl.ds(128, 128)],
                expand.at[:, pl.ds(pl.multiple_of(hidden + start, 128), 128)],
                sems.at[n, 2],
            ),
        ]
        for copy in copies[-2:]:
            copy.start()
    for copy in copies:
        copy.wait()
    for n in range(4):

        @pl.when(owners[n] // 8 == group)
        def _(n=n):
            dense_copy(n).wait()


def assemble(owners, first, second, shapes, outs, *gates):
    return pl.pallas_call(
        assemble_kernel,
        in_specs=[SMEM, VMEM, VMEM] + [ANY] * ((0 if outs is None else 3) + len(gates)),
        out_specs=[ANY] * 3 + [VMEM],
        out_shape=[shaped(s, jnp.float32) for s in (*shapes, (8, 128))],
        scratch_shapes=[
            pltpu.VMEM((4, 192, 1024), jnp.float32),
            pltpu.VMEM((4, 512, 256), jnp.float32),
            pltpu.SemaphoreType.DMA((4, 4)),
        ],
        input_output_aliases={} if outs is None else {3 + i: i for i in range(3)},
        compiler_params=pltpu.CompilerParams(vmem_limit_bytes=24 * MIB),
        cost_estimate=cost(flops=0, bytes_accessed=1280 * 6144, transcendentals=0),
        name="place_gradients",
    )(owners, first, second, *(outs or ()), *gates)


def assemble_joint_kernel(count, owners, *refs):
    blobs = refs[:count]
    joint, norm_sums, joint_bias, expand_bias, held, buffer, sems, arrivals = refs[count:]
    group = owners[2 * count]
    norm_sums[...] = jnp.zeros_like(norm_sums)
    width = joint.shape[1] // 3
    size = blobs[0].shape[0] // 2
    fetches = [
        pltpu.make_async_copy(blobs[n], held.at[n], arrivals.at[n]) for n in range(count)
    ]
    for fetch in fetches:
        fetch.start()
    copies = []
    for n in range(2 * count):
        owner = owners[n]
        first = (n % 2) * size
        if n % 2 == 0:
            fetches[n // 2].wait()
        buffer[n] = held[n // 2, first : first + 256, :].astype(jnp.float32)
        top = pl.multiple_of(lax.rem(owner, 2) * 256, 256)
        for part in range(3):
            start = pl.multiple_of(part * width + (owner // 2) * 128, 128)
            copies.append(
                pltpu.make_async_copy(
                    buffer.at[n, :, pl.ds(part * 128, 128)],
                    joint.at[pl.ds(top, 256), pl.ds(start, 128)],
                    sems.at[n, part],
                )
            )
            copies[-1].start()
    for n in range(count):
        first = held[n, 256:272, 0:256].astype(jnp.float32)
        second = held[n, size + 256 : size + 272, 0:256].astype(jnp.float32)
        norm_sums[...] += first[0:8, :] + second[0:8, :]
        low_first = lax.rem(owners[2 * n], 2) == 0
        low = jnp.where(low_first, first[10:11, :], second[10:11, :])
        high = jnp.where(low_first, second[10:11, :], first[10:11, :])
        for part in range(3):
            lanes = slice(part * 64, part * 64 + 64)
            joint_bias[pl.ds(part * 8 + owners[2 * n] // 2, 1), :] = jnp.concatenate(
                [low[:, lanes], high[:, lanes]], 1
            )
        for piece, row in enumerate((first[11:12, :], second[11:12, :])):
            expand_bias[pl.ds(owners[2 * n + piece], 1), :] = jnp.where(
                group == 0, row[:, 0:128], row[:, 128:256]
            )
    for copy in copies:
        copy.wait()


def assemble_joint(owners, blobs, shape):
    count = len(blobs)
    return pl.pallas_call(
        functools.partial(assemble_joint_kernel, count),
        in_specs=[SMEM] + [ANY] * count,
        out_specs=[ANY] + [VMEM] * 3,
        out_shape=[
            shaped(shape, jnp.float32),
            shaped((8, 256), jnp.float32),
            shaped((24, 128), jnp.float32),
            shaped((16, 128), jnp.float32),
        ],
        scratch_shapes=[
            pltpu.VMEM((count, *blobs[0].shape), jnp.bfloat16),
            pltpu.VMEM((2 * count, 256, 384), jnp.float32),
            pltpu.SemaphoreType.DMA((2 * count, 3)),
            pltpu.SemaphoreType.DMA((count,)),
        ],
        compiler_params=pltpu.CompilerParams(vmem_limit_bytes=40 * MIB),
        cost_estimate=cost(
            flops=0, bytes_accessed=count * 512 * 384 * 6, transcendentals=0
        ),
        name="place_joint_gradient",
    )(owners, *blobs)


def split_heads(
    tokens,
    cotangent,
    first_gain,
    first_shift,
    second_gain,
    second_shift,
    joint_weight,
    joint_bias,
    dense_weight,
    dense_bias,
    expand_weight,
    expand_bias,
    shrink_weight,
    shrink_bias,
    block_order,
):
    f32, bf16 = jnp.float32, jnp.bfloat16
    me = lax.axis_index("ctx")
    group = lax.axis_index("fsdp")
    core = me % 2
    rows, width = tokens.shape[1:]
    total_rows = rows * 16
    hidden = expand_weight.shape[1] // 2
    own_tokens, own_upstream = tokens[0], cotangent[0]


    token_pair = jnp.concatenate([own_tokens, swap(own_tokens)], 0)
    token_hops = [gather_hop(token_pair, 1)]
    at = after(me, token_pair)
    scalars = jnp.stack([at, group]).astype(jnp.int32)
    tall, flat = slice_parameters(
        scalars, joint_weight, expand_weight, shrink_weight, dense_weight
    )
    tall_other = other(tall)
    vector = stack_vectors(
        lax.optimization_barrier(
            (
                first_gain,
                first_shift,
                second_gain,
                second_shift,
                dense_bias,
                shrink_bias,
                joint_bias,
                expand_bias,
                tall,
            )
        )[:8]
    )
    joint_c, expand_c, tall_t, scaled, norms, shifts, biases = join_parameters(
        scalars, tall, tall_other, vector, other(vector)
    )
    flat_other = other(after(flat, tall_other))
    shrink_pair = [jnp.where(group == i, flat[:128], flat_other[:128]) for i in range(2)]
    shrink_c = jnp.concatenate(shrink_pair, 0)
    dense_c = jnp.where(group == me // 8, flat[128:], flat_other[128:])

    owners = piece_owners(at)
    blocks = after(block_order, token_pair).reshape(16, 2)[owners].reshape(32)
    count = jnp.arange(32, dtype=jnp.int32)
    slots = jnp.sum(jnp.where(blocks[None, :] == count[:, None], count[None, :], 0), 1)
    near = after(jnp.arange(BLOCK), token_pair)
    angles = tables(jnp.arange(total_rows // BLOCK) * BLOCK) + tables(near)

    normal, flags = None, []

    def take(block):
        nonlocal normal
        *normal, flag = pre(
            len(flags), block, norms, joint_c, biases, expand_c, normal, 8
        )
        flags.append(flag)

    def far_pair(far):
        return jnp.concatenate([far, swap(far)], 0)

    take(token_pair)
    token_hops.append(gather_hop(token_hops[0], 2, tall, vector))
    take(token_hops[0])
    take(swap(token_hops[0]))
    token_hops.append(gather_hop(token_hops[1], 3, flags[0]))
    take(token_hops[1])
    take(swap(token_hops[1]))
    token_hops.append(gather_hop(token_hops[2], 4, flags[3]))
    upstream_pair = jnp.concatenate([own_upstream, swap(after(own_upstream, flags[0]))], 0)
    upstream_hops = [gather_hop(upstream_pair, 1, token_hops[2], flags[3])]
    take(token_hops[2])
    take(swap(token_hops[2]))
    take(far_pair(token_hops[3]))
    normed_one, normed_two, joint, activated, slope = normal
    query, key, value = turn(blocks, joint, angles, upstream_hops[0])

    mixed, outs, sums = None, [], []

    def attend(index, gate):
        nonlocal mixed
        mixed, out, lse = attention_forward(index, slots, query, key, value, mixed, gate)
        outs.append(out)
        sums.append(lse)

    upstream_hops.append(gather_hop(upstream_hops[0], 2, flags[6]))
    attend(0, None)
    upstream_hops.append(gather_hop(upstream_hops[1], 3, query))
    attend(1, upstream_hops[1])
    attend(2, upstream_hops[1])
    upstream_hops.append(gather_hop(upstream_hops[2], 4, sums[0]))
    attend(3, upstream_hops[2])
    upstream_blocks = [upstream_pair]
    for held in upstream_hops[:3]:
        upstream_blocks += [held, swap(held)]
    upstream_blocks.append(far_pair(upstream_hops[3]))
    lse = jnp.concatenate(
        [s[:, :TILE] for s in sums] + [s[:, TILE:] for s in sums[::-1]], 1
    )

    branch = jnp.concatenate([activated, mixed], 1)
    back = jnp.concatenate([shrink_c, dense_c], 0)
    this = group[None].astype(jnp.int32)

    def products(blocks, first, before, normed):
        return post(
            this,
            blocks,
            first,
            before,
            slope,
            activated,
            mixed,
            normed,
            shrink_c,
            dense_c,
            tall_t[256:],
            norms,
        )

    early = products(upstream_blocks[:4], 0, None, normed_two)
    out_hops = [hop(after(scatter_term(branch, back, 4), upstream_hops[3]))]
    term = scatter_term(branch, back, 3, out_hops[0])
    out_hops.append(hop(term))
    expand_delta, mixed_grad, _, _, _, column_sum, expand_sum, kept, sent, norm_two = products(
        upstream_blocks[4:], 4, early, after(normed_two, term)
    )
    term = scatter_term(branch, back, 2, out_hops[1])
    out_hops.append(hop(after(term, expand_sum)))
    out_grad, inner = sort_grad(slots, after(mixed_grad, term), outs)
    blob_other = other(sent)

    dq, key_grads, value_grads = None, [], []

    def attend_back(index, gate):
        nonlocal dq
        dq, dk, dv = attention_backward(
            index, query, key, value, out_grad, inner, lse, dq, gate
        )
        key_grads.append(dk)
        value_grads.append(dv)

    attend_back(0, term)
    attend_back(1, term)
    term = scatter_term(branch, back, 1, out_hops[2])
    out_hops.append(hop(after(term, key_grads[0])))
    blob = (kept + after(blob_other, key_grads[0]).astype(f32)).astype(bf16)
    blob_pair = jnp.concatenate([blob, swap(blob)], 0)
    blob_hops = [gather_hop(blob_pair, 1, out_hops[2])]
    attend_back(2, term)
    out_rows = nn(branch[: 2 * rows], back)
    out_sent = out_rows[rows:] + out_hops[3][:rows].astype(f32)
    out_sum = out_rows[:rows] + out_hops[3][rows:].astype(f32)
    out_sum = out_sum + swap(out_sent.astype(bf16)).astype(f32)
    output = own_tokens.astype(f32) + out_sum + shifts
    attend_back(3, out_hops[3])
    blob_hops.append(gather_hop(blob_hops[0], 2))
    delta, joint_sum = finish(slots, dq, expand_delta, angles, key_grads, value_grads)

    far_term = scatter_term(delta, scaled, 4)
    in_hops = [hop(far_term)]
    in_hops.append(hop(scatter_term(delta, scaled, 3, in_hops[0])))
    joint_kept, joint_sent, norm_one = joint_products(
        this, after(normed_one, in_hops[0]), delta, tall_t[:256], joint_sum, norms
    )

    def rows_of(which):
        norm_part = jnp.concatenate([norm_one, norm_two], 0).reshape(4, 2, 2, 256)
        column_part = column_sum.reshape(2, 2, 256)
        return jnp.concatenate(
            [
                cut(norm_part, which, 1, 1).reshape(8, 256),
                cut(column_part, which, 1, 0).reshape(2, 256),
                joint_sum,
                expand_sum,
                jnp.zeros((4, 256), f32),
            ],
            0,
        )

    sent = jnp.concatenate([joint_sent, rows_of(1 - group).astype(bf16)], 0)
    received = other(sent).astype(f32)
    half = width // 2
    packed = rows_of(group) + received[half:]
    joint_half = (joint_kept + received[:half]).astype(bf16)
    exchanged = swap(cut(joint_half, (1 - core) * (half // 2), half // 2, 0))
    joint_blob = pair_heads(
        core[None].astype(jnp.int32), joint_half, exchanged, packed.astype(bf16)
    )
    joint_pair = jnp.concatenate([joint_blob, swap(joint_blob)], 0)

    placed, marks = None, []
    shapes = ((hidden, width), (half, width), (half, 2 * hidden))

    def place(first, second, *gates):
        nonlocal placed
        some = owners[4 * len(marks) : 4 * len(marks) + 4]
        *placed, mark = assemble(
            jnp.concatenate([some, this]).astype(jnp.int32), first, second, shapes, placed, *gates
        )
        marks.append(mark)

    blob_hops.append(gather_hop(blob_hops[1], 3))
    place(blob_pair, blob_hops[0], in_hops[0])
    place(swap(blob_hops[0]), blob_hops[1], in_hops[0])
    joint_hops = [gather_hop(joint_pair, 1)]
    in_hops.append(hop(scatter_term(delta, scaled, 2, in_hops[1])))
    blob_hops.append(hop(first_piece(blob_hops[2], marks[1])))
    joint_hops.append(gather_hop(joint_hops[0], 2))
    place(swap(blob_hops[1]), blob_hops[2])
    in_hops.append(hop(scatter_term(delta, scaled, 1, in_hops[2])))
    joint_hops.append(gather_hop(joint_hops[1], 3))
    joint_hops.append(hop(first_piece(joint_hops[2], marks[1])))
    place(swap(blob_hops[2]), far_pair(blob_hops[3]))
    shrink_total, dense_total, expand_total = placed
    joint_blocks = [joint_pair]
    for held in joint_hops[:3]:
        joint_blocks += [held, swap(held)]
    joint_blocks.append(far_pair(joint_hops[3]))
    joint_total, norm_sums, joint_bias_sums, expand_bias_sums = assemble_joint(
        jnp.concatenate([owners, this]).astype(jnp.int32), joint_blocks, (half, 3 * width)
    )
    in_own, in_sent = scatter_last(delta, scaled, in_hops[3], norm_sums, marks[3])
    tokens_grad = input_grad(own_tokens, own_upstream, in_own, swap(in_sent))
    totals = norm_sums.reshape(4, half)
    column_total = packed[8:10].reshape(-1)

    return (
        output.astype(bf16)[None],
        tokens_grad[None],
        totals[0],
        totals[1],
        totals[2],
        totals[3],
        joint_total,
        cut(joint_bias_sums, group * 12, 12, 0).reshape(-1),
        dense_total,
        column_total,
        expand_total,
        expand_bias_sums.reshape(-1),
        shrink_total,
        column_total,
    )


def solution(mesh):
    fits = mesh.shape["ctx"] == HEADS and mesh.shape["fsdp"] == 2
    return jax.shard_map(
        split_heads if fits else shards,
        mesh=mesh,
        in_specs=(
            P("fsdp", "ctx", None),
            P("fsdp", "ctx", None),
            P("fsdp"),
            P("fsdp"),
            P("fsdp"),
            P("fsdp"),
            P("fsdp", None),
            P("fsdp"),
            P("fsdp", None),
            P("fsdp"),
            P("fsdp", None),
            P("fsdp"),
            P("fsdp", None),
            P("fsdp"),
            P(),
        ),
        out_specs=(
            P("fsdp", "ctx", None),
            P("fsdp", "ctx", None),
            P("fsdp"),
            P("fsdp"),
            P("fsdp"),
            P("fsdp"),
            P("fsdp", None),
            P("fsdp"),
            P("fsdp", None),
            P("fsdp"),
            P("fsdp", None),
            P("fsdp"),
            P("fsdp", None),
            P("fsdp"),
        ),
        check_vma=False,
    )
```

```python
import functools

import jax
import jax.numpy as jnp
from jax import lax
from jax.experimental import pallas as pl
from jax.experimental.pallas import tpu as pltpu
from jax.sharding import PartitionSpec as P

HEADS = 16
ROT = 16


epsilon = 1e-05
negative = -1e30


def normalize(values, gain, shift):
    center = values - jnp.mean(values, -1, keepdims=True)
    spread = jnp.mean(center * center, -1, keepdims=True)
    return center * lax.rsqrt(spread + epsilon) * gain + shift


def turn_tables(positions):
    inverse = jnp.power(10000.0, -2.0 * jnp.arange(ROT // 2, dtype=jnp.float32) / ROT)
    angles = positions.astype(jnp.float32)[:, None] * inverse[None, :]
    angles = jnp.concatenate([angles, angles], -1)[:, None, :]
    return (jnp.cos(angles), jnp.sin(angles))


def rotate(values, cosine, sine):
    half = ROT // 2
    front = values[..., :ROT]
    turned = jnp.concatenate([-front[..., half:], front[..., :half]], -1)
    return jnp.concatenate([front * cosine + turned * sine, values[..., ROT:]], -1)


def contract(left, right, left_dim, right_dim):
    return lax.dot_general(
        left, right, (((left_dim,), (right_dim,)), ((), ())), preferred_element_type=jnp.float32
    )


def shards(
    tokens,
    cotangent,
    first_gain,
    first_shift,
    second_gain,
    second_shift,
    joint_weight,
    joint_bias,
    dense_weight,
    dense_bias,
    expand_weight,
    expand_bias,
    shrink_weight,
    shrink_bias,
    block_order,
):
    rows = tokens.shape[1]
    width = tokens.shape[2]
    head_dim = width // HEADS
    scale = head_dim ** (-0.5)
    groups = lax.axis_size("ctx")
    half_rows = rows // 2
    (
        gain_one,
        shift_one,
        gain_two,
        shift_two,
        joint_full,
        joint_shift,
        dense_full,
        dense_shift,
        expand_full,
        expand_shift,
        shrink_full,
        shrink_shift,
    ) = (
        lax.all_gather(first_gain, "fsdp", axis=0, tiled=True),
        lax.all_gather(first_shift, "fsdp", axis=0, tiled=True),
        lax.all_gather(second_gain, "fsdp", axis=0, tiled=True),
        lax.all_gather(second_shift, "fsdp", axis=0, tiled=True),
        lax.all_gather(joint_weight, "fsdp", axis=0, tiled=True),
        lax.all_gather(joint_bias, "fsdp", axis=0, tiled=True),
        lax.all_gather(dense_weight, "fsdp", axis=0, tiled=True),
        lax.all_gather(dense_bias, "fsdp", axis=0, tiled=True),
        lax.all_gather(expand_weight, "fsdp", axis=0, tiled=True),
        lax.all_gather(expand_bias, "fsdp", axis=0, tiled=True),
        lax.all_gather(shrink_weight, "fsdp", axis=0, tiled=True),
        lax.all_gather(shrink_bias, "fsdp", axis=0, tiled=True),
    )
    gain_one = gain_one.astype(jnp.float32)
    shift_one = shift_one.astype(jnp.float32)
    gain_two = gain_two.astype(jnp.float32)
    shift_two = shift_two.astype(jnp.float32)
    all_positions = (
        block_order[:, None] * half_rows + jnp.arange(half_rows, dtype=jnp.int32)[None, :]
    ).reshape(rows * groups)
    positions = lax.dynamic_slice_in_dim(all_positions, lax.axis_index("ctx") * rows, rows)
    cosine, sine = turn_tables(positions)
    visible = positions[:, None] >= all_positions[None, :]
    inputs = tokens[0].astype(jnp.float32)
    normed_one = normalize(inputs, gain_one, shift_one).astype(jnp.bfloat16)
    normed_two = normalize(inputs, gain_two, shift_two).astype(jnp.bfloat16)
    joint = jnp.dot(
        normed_one, joint_full, preferred_element_type=jnp.float32
    ) + joint_shift.astype(jnp.float32)
    queries = (
        rotate(joint[:, :width].reshape(rows, HEADS, head_dim), cosine, sine)
        .reshape(rows, width)
        .astype(jnp.bfloat16)
    )
    key_rows = (
        rotate(joint[:, width : 2 * width].reshape(rows, HEADS, head_dim), cosine, sine)
        .reshape(rows, width)
        .astype(jnp.bfloat16)
    )
    value_rows = joint[:, 2 * width :].astype(jnp.bfloat16)
    all_keys, all_values = (
        lax.all_gather(key_rows, "ctx", axis=0, tiled=True),
        lax.all_gather(value_rows, "ctx", axis=0, tiled=True),
    )

    def head_scores(head, key_source):
        query = lax.dynamic_slice_in_dim(queries, head * head_dim, head_dim, 1)
        key_cols = lax.dynamic_slice_in_dim(key_source, head * head_dim, head_dim, 1)
        scores = contract(query, key_cols, 1, 1) * scale
        return (query, key_cols, jnp.where(visible, scores, negative))

    def head_forward(head):
        query, key_cols, scores = head_scores(head, all_keys)
        top = jnp.max(scores, -1, keepdims=True)
        total = jnp.sum(jnp.exp(scores - top), -1, keepdims=True)
        log_total = top + jnp.log(total)
        weights = jnp.exp(scores - log_total).astype(jnp.bfloat16)
        value_cols = lax.dynamic_slice_in_dim(all_values, head * head_dim, head_dim, 1)
        return (jnp.dot(weights, value_cols, preferred_element_type=jnp.float32), log_total[:, 0])

    mixed, log_totals = lax.map(head_forward, jnp.arange(HEADS))
    attended = jnp.transpose(mixed, (1, 0, 2)).reshape(rows, width).astype(jnp.bfloat16)
    expanded = jnp.dot(
        normed_two, expand_full, preferred_element_type=jnp.float32
    ) + expand_shift.astype(jnp.float32)
    activated = jax.nn.gelu(expanded, approximate=False).astype(jnp.bfloat16)
    output = (
        inputs
        + jnp.dot(attended, dense_full, preferred_element_type=jnp.float32)
        + dense_shift.astype(jnp.float32)
    )
    output = (
        output
        + jnp.dot(activated, shrink_full, preferred_element_type=jnp.float32)
        + shrink_shift.astype(jnp.float32)
    )
    upstream = cotangent[0]
    upstream_float = upstream.astype(jnp.float32)
    column_sum = jnp.sum(upstream_float, 0)
    dense_grad = contract(attended, upstream, 0, 0)
    shrink_grad = contract(activated, upstream, 0, 0)
    act_grad = contract(upstream, shrink_full, 1, 1)
    _, gelu_pull = jax.vjp(lambda value: jax.nn.gelu(value, approximate=False), expanded)
    expand_delta = gelu_pull(act_grad)[0].astype(jnp.bfloat16)
    expand_grad = contract(normed_two, expand_delta, 0, 0)
    expand_bias_grad = jnp.sum(expand_delta.astype(jnp.float32), 0)
    normed_two_grad = contract(expand_delta, expand_full, 1, 1)
    _, pull_two = jax.vjp(normalize, inputs, gain_two, shift_two)
    input_two, gain_two_grad, shift_two_grad = pull_two(normed_two_grad)
    attended_grad = contract(upstream, dense_full, 1, 1).astype(jnp.bfloat16)
    key_source, value_source = (all_keys, all_values)

    def head_backward(items):
        head, log_total = items
        query, key_cols, scores = head_scores(head, key_source)
        probs = jnp.exp(scores - log_total[:, None])
        value_cols = lax.dynamic_slice_in_dim(value_source, head * head_dim, head_dim, 1)
        out_grad = lax.dynamic_slice_in_dim(attended_grad, head * head_dim, head_dim, 1)
        prob_grad = contract(out_grad, value_cols, 1, 1)
        inner = jnp.sum(probs * prob_grad, -1, keepdims=True)
        score_grad = (probs * (prob_grad - inner)).astype(jnp.bfloat16)
        query_grad = jnp.dot(score_grad, key_cols, preferred_element_type=jnp.float32) * scale
        key_grad = contract(score_grad, query, 0, 0) * scale
        value_grad = contract(probs.astype(jnp.bfloat16), out_grad, 0, 0)
        return (query_grad, key_grad, value_grad)

    query_grads, key_grads, value_grads = lax.map(head_backward, (jnp.arange(HEADS), log_totals))
    key_sums, value_sums = (
        lax.psum_scatter(
            key_grads.astype(jnp.bfloat16), "ctx", scatter_dimension=1, tiled=True
        ).astype(jnp.float32),
        lax.psum_scatter(
            value_grads.astype(jnp.bfloat16), "ctx", scatter_dimension=1, tiled=True
        ).astype(jnp.float32),
    )
    query_back = rotate(jnp.transpose(query_grads, (1, 0, 2)), cosine, -sine).reshape(rows, width)
    key_back = rotate(jnp.transpose(key_sums, (1, 0, 2)), cosine, -sine).reshape(rows, width)
    value_back = jnp.transpose(value_sums, (1, 0, 2)).reshape(rows, width)
    joint_delta = jnp.concatenate([query_back, key_back, value_back], 1).astype(jnp.bfloat16)
    joint_grad = contract(normed_one, joint_delta, 0, 0)
    joint_bias_grad = jnp.sum(joint_delta.astype(jnp.float32), 0)
    normed_one_grad = contract(joint_delta, joint_full, 1, 1)
    _, pull_one = jax.vjp(normalize, inputs, gain_one, shift_one)
    input_one, gain_one_grad, shift_one_grad = pull_one(normed_one_grad)
    tokens_grad = (upstream_float + input_one + input_two).astype(jnp.bfloat16)
    (
        gain_one_part,
        shift_one_part,
        gain_two_part,
        shift_two_part,
        joint_part,
        joint_bias_part,
        dense_part,
        column_part,
        expand_part,
        expand_bias_part,
        shrink_part,
    ) = (
        lax.psum_scatter(
            gain_one_grad.astype(jnp.bfloat16), "fsdp", scatter_dimension=0, tiled=True
        ).astype(jnp.float32),
        lax.psum_scatter(
            shift_one_grad.astype(jnp.bfloat16), "fsdp", scatter_dimension=0, tiled=True
        ).astype(jnp.float32),
        lax.psum_scatter(
            gain_two_grad.astype(jnp.bfloat16), "fsdp", scatter_dimension=0, tiled=True
        ).astype(jnp.float32),
        lax.psum_scatter(
            shift_two_grad.astype(jnp.bfloat16), "fsdp", scatter_dimension=0, tiled=True
        ).astype(jnp.float32),
        lax.psum_scatter(
            joint_grad.astype(jnp.bfloat16), "fsdp", scatter_dimension=0, tiled=True
        ).astype(jnp.float32),
        lax.psum_scatter(
            joint_bias_grad.astype(jnp.bfloat16), "fsdp", scatter_dimension=0, tiled=True
        ).astype(jnp.float32),
        lax.psum_scatter(
            dense_grad.astype(jnp.bfloat16), "fsdp", scatter_dimension=0, tiled=True
        ).astype(jnp.float32),
        lax.psum_scatter(
            column_sum.astype(jnp.bfloat16), "fsdp", scatter_dimension=0, tiled=True
        ).astype(jnp.float32),
        lax.psum_scatter(
            expand_grad.astype(jnp.bfloat16), "fsdp", scatter_dimension=0, tiled=True
        ).astype(jnp.float32),
        lax.psum_scatter(
            expand_bias_grad.astype(jnp.bfloat16), "fsdp", scatter_dimension=0, tiled=True
        ).astype(jnp.float32),
        lax.psum_scatter(
            shrink_grad.astype(jnp.bfloat16), "fsdp", scatter_dimension=0, tiled=True
        ).astype(jnp.float32),
    )
    (
        gain_one_total,
        shift_one_total,
        gain_two_total,
        shift_two_total,
        joint_total,
        joint_bias_total,
        dense_total,
        column_total,
        expand_total,
        expand_bias_total,
        shrink_total,
    ) = (
        lax.psum(gain_one_part.astype(jnp.bfloat16), "ctx").astype(jnp.float32),
        lax.psum(shift_one_part.astype(jnp.bfloat16), "ctx").astype(jnp.float32),
        lax.psum(gain_two_part.astype(jnp.bfloat16), "ctx").astype(jnp.float32),
        lax.psum(shift_two_part.astype(jnp.bfloat16), "ctx").astype(jnp.float32),
        lax.psum(joint_part.astype(jnp.bfloat16), "ctx").astype(jnp.float32),
        lax.psum(joint_bias_part.astype(jnp.bfloat16), "ctx").astype(jnp.float32),
        lax.psum(dense_part.astype(jnp.bfloat16), "ctx").astype(jnp.float32),
        lax.psum(column_part.astype(jnp.bfloat16), "ctx").astype(jnp.float32),
        lax.psum(expand_part.astype(jnp.bfloat16), "ctx").astype(jnp.float32),
        lax.psum(expand_bias_part.astype(jnp.bfloat16), "ctx").astype(jnp.float32),
        lax.psum(shrink_part.astype(jnp.bfloat16), "ctx").astype(jnp.float32),
    )
    return (
        output.astype(jnp.bfloat16)[None],
        tokens_grad[None],
        gain_one_total,
        shift_one_total,
        gain_two_total,
        shift_two_total,
        joint_total,
        joint_bias_total,
        dense_total,
        column_total,
        expand_total,
        expand_bias_total,
        shrink_total,
        column_total,
    )

CYCLE = (0, 2, 4, 6, 7, 5, 3, 1)
RING = tuple((2 * CYCLE[i], 2 * CYCLE[(i + 1) % 8]) for i in range(8)) + tuple(
    (2 * CYCLE[i] + 1, 2 * CYCLE[i - 1] + 1) for i in range(8)
)
SWAP = tuple((i, i ^ 1) for i in range(16))
TILE = 512
BLOCK = 128
MIB = 1024 * 1024


def hop(values):
    return lax.ppermute(values, "ctx", RING)


def swap(values):
    return lax.ppermute(values, "ctx", SWAP)


def other(values):
    return lax.ppermute(values, "fsdp", ((0, 1), (1, 0)))


def after(values, *others):
    return lax.optimization_barrier((values, *others))[0]


def cut(values, start, size, axis):
    return lax.dynamic_slice_in_dim(values, start, size, axis)


def gather_hop(held, step, *gates):
    if step == 4:
        held = held[: held.shape[0] // 2]
    return hop(after(held, *gates) if gates else held)


def piece_owners(me):
    core = me % 2
    piece = jnp.arange(16, dtype=jnp.int32)
    pair = piece // 2
    step = jnp.where(pair % 2 == 1, (pair + 1) // 2, -(pair // 2)) * (2 * core - 1)
    along = me // 4
    place = (jnp.where((me // 2) % 2 == 0, along, 7 - along) + step + 8) % 8
    chip = jnp.where(place < 4, 2 * place, 15 - 2 * place)
    other_first = (pair % 2 == 0) & (pair > 0)
    return 2 * chip + (piece + core + other_first) % 2


def scatter_term(values, weight, step, held=None):
    rows = values.shape[0] // 16
    f32, bf16 = jnp.float32, jnp.bfloat16

    def term(first, count):
        return nn(values[first * rows : (first + count) * rows], weight)

    if step == 4:
        return (term(14, 1) + swap(term(15, 1).astype(bf16)).astype(f32)).astype(bf16)
    mine = term(4 * step, 2) + swap(term(4 * step - 2, 2).astype(bf16)).astype(f32)
    if step == 3:
        held = jnp.pad(held, ((rows, 0), (0, 0)))
    return (mine + held.astype(f32)).astype(bf16)


def turn_back(values, lanes):
    ahead = pltpu.roll(values, 128 - ROT // 2, 1)
    behind = pltpu.roll(values, ROT // 2, 1)
    return jnp.where(lanes % 64 < ROT // 2, -ahead, behind)


def nt(left_side, right_side):
    return lax.dot_general(
        left_side, right_side, (((1,), (1,)), ((), ())), preferred_element_type=jnp.float32
    )


def nn(left_side, right_side):
    return jnp.dot(left_side, right_side, preferred_element_type=jnp.float32)


def tn(left_side, right_side):
    return lax.dot_general(
        left_side, right_side, (((0,), (0,)), ((), ())), preferred_element_type=jnp.float32
    )


VMEM = pl.BlockSpec(memory_space=pltpu.VMEM)
SMEM = pl.BlockSpec(memory_space=pltpu.SMEM)
ANY = pl.BlockSpec(memory_space=pl.ANY)


def cost(flops, bytes_accessed, transcendentals, share=1):
    return pl.CostEstimate(
        flops=int(flops * share),
        bytes_accessed=int(bytes_accessed * share),
        transcendentals=int(transcendentals * share),
    )


def shaped(shape, dtype):
    return jax.ShapeDtypeStruct(shape, dtype)


def pre_kernel(x, norms, joint_w, biases, expand_w, *refs):
    one, two, joint, active, slope, done = refs[-6:]
    done[...] = jnp.zeros_like(done)
    wide = x[...].astype(jnp.float32)
    center = wide - jnp.mean(wide, -1, keepdims=True)
    spread = jnp.mean(center * center, -1, keepdims=True)
    unit = center * lax.rsqrt(spread + epsilon)
    normed_one = (unit * norms[0:1, :] + norms[1:2, :]).astype(jnp.bfloat16)
    normed_two = (unit * norms[2:3, :] + norms[3:4, :]).astype(jnp.bfloat16)
    one[...] = normed_one
    two[...] = normed_two
    joint[...] = nn(normed_one, joint_w[...]) + biases[0:1, :]
    expanded = nn(normed_two, expand_w[...]) + biases[1:2, :]
    share = 0.5 + 0.5 * lax.erf(expanded * (0.5**0.5))
    active[...] = (expanded * share).astype(jnp.bfloat16)
    slope[...] = share + expanded * (jnp.exp(-0.5 * expanded * expanded) * 0.3989422804014327)


def pre(index, x, norms, joint_w, biases, expand_w, outs, count):
    rows, width = x.shape
    step = rows // 2
    fixed = lambda shape: pl.BlockSpec(shape, lambda i: (0, 0))
    place = lambda cols: pl.BlockSpec((step, cols), lambda i: (2 * index + i, 0))
    total = rows * count
    bf16, f32 = jnp.bfloat16, jnp.float32
    aliases = {} if outs is None else {5 + i: i for i in range(5)}
    return pl.pallas_call(
        pre_kernel,
        grid=(2,),
        in_specs=[pl.BlockSpec((step, width), lambda i: (i, 0))]
        + [fixed(v.shape) for v in (norms, joint_w, biases, expand_w)]
        + [ANY] * len(aliases),
        out_specs=[place(width), place(width), place(256), place(256), place(256), fixed((8, 128))],
        out_shape=[
            pltpu.HBM((total, width), bf16),
            pltpu.HBM((total, width), bf16),
            pltpu.HBM((total, 256), f32),
            pltpu.HBM((total, 256), bf16),
            pltpu.HBM((total, 256), f32),
            shaped((8, 128), f32),
        ],
        input_output_aliases=aliases,
        compiler_params=pltpu.CompilerParams(vmem_limit_bytes=40 * MIB),
        cost_estimate=cost(
            flops=rows * width * 1024,
            bytes_accessed=rows * width * 10,
            transcendentals=rows * 512,
            share=1,
        ),
        name="norms_joint_hidden",
    )(x, norms, joint_w, biases, expand_w, *(outs or ()))


def vector_kernel(*refs):
    vectors, (out, rows) = refs[:8], refs[8:]
    rows[...] = jnp.zeros_like(rows)
    row = 0
    for vector in vectors:
        for part in range(vector.shape[1] // 512):
            rows[row : row + 1, :] = vector[:, part * 512 : (part + 1) * 512].astype(
                jnp.float32
            )
            row += 1
    out[...] = rows[...].astype(jnp.bfloat16)


def stack_vectors(vectors):
    return pl.pallas_call(
        vector_kernel,
        in_specs=[VMEM] * 8,
        out_specs=VMEM,
        out_shape=shaped((16, 512), jnp.bfloat16),
        scratch_shapes=[pltpu.VMEM((16, 512), jnp.float32)],
        cost_estimate=cost(flops=0, bytes_accessed=1 << 16, transcendentals=0),
        name="stack_vectors",
    )(*[v.reshape(1, -1) for v in vectors])


def slice_kernel(me, joint, expand, shrink, dense, tall, flat, pieces, sems):
    index = me[0]
    hidden = expand.shape[1] // 2
    width = joint.shape[1] // 3
    chip = pl.multiple_of((index // 2) * 128, 128)
    own = pl.multiple_of(index * 128, 128)
    copies = [
        pltpu.make_async_copy(
            joint.at[:, pl.ds(pl.multiple_of(i * width + chip, 128), 128)], pieces.at[i], sems.at[i]
        )
        for i in range(3)
    ]
    copies += [
        pltpu.make_async_copy(
            expand.at[:, pl.ds(pl.multiple_of(i * hidden + own, 128), 128)],
            tall.at[:, pl.ds(256 + 128 * i, 128)],
            sems.at[3 + i],
        )
        for i in range(2)
    ]
    copies.append(
        pltpu.make_async_copy(shrink.at[pl.ds(own, 128)], flat.at[pl.ds(0, 128)], sems.at[5])
    )
    start = pl.multiple_of(lax.rem(index, 8) * 64, 64)
    copies.append(
        pltpu.make_async_copy(dense.at[pl.ds(start, 64)], flat.at[pl.ds(128, 64)], sems.at[6])
    )
    for copy in copies:
        copy.start()
    for copy in copies:
        copy.wait()
    heads = [
        jnp.where(lax.rem(index, 2) == 0, pieces[i, :, 0:64], pieces[i, :, 64:128])
        for i in range(3)
    ]
    tall[:, 0:256] = jnp.concatenate(heads + [jnp.zeros_like(heads[0])], 1)


def slice_parameters(me, joint, expand, shrink, dense):
    rows = joint.shape[0]
    bf16 = jnp.bfloat16
    return pl.pallas_call(
        slice_kernel,
        in_specs=[SMEM] + [ANY] * 4,
        out_specs=[VMEM] * 2,
        out_shape=[shaped((rows, 512), bf16), shaped((192, 1024), bf16)],
        scratch_shapes=[
            pltpu.VMEM((3, rows, 128), bf16),
            pltpu.SemaphoreType.DMA((7,)),
        ],
        cost_estimate=cost(flops=0, bytes_accessed=4 * MIB, transcendentals=0),
        name="slice_parameters",
    )(me, joint, expand, shrink, dense)


def join_kernel(at, tall, tall_other, vector, vector_other, *refs):
    joint_c, expand_c, tall_t, scaled, norms, shifts, biases, rows = refs
    head, group = at[0], at[1]
    size = tall.shape[0]
    for half in range(2):
        here = slice(half * size, (half + 1) * size)
        piece = jnp.where(group == half, tall[...], tall_other[...])
        joint_c[here, :] = piece[:, 0:256]
        expand_c[here, :] = piece[:, 256:512]
        tall_t[:, here] = piece.astype(jnp.float32).T.astype(jnp.bfloat16)
        rows[half] = jnp.where(group == half, vector[...], vector_other[...]).astype(jnp.float32)
        norms[0:4, here] = rows[half, 0:4, :]
        shifts[:, here] = rows[half, 4:5, :] + rows[half, 5:6, :]
    norms[4:8, :] = jnp.zeros((4, 2 * size), jnp.float32)
    scaled[0:256, :] = (tall_t[0:256, :].astype(jnp.float32) * norms[0:1, :]).astype(jnp.bfloat16)
    scaled[256:512, :] = (tall_t[256:512, :].astype(jnp.float32) * norms[2:3, :]).astype(
        jnp.bfloat16
    )
    numbers = lax.broadcasted_iota(jnp.int32, (16, 128), 0)

    def pick(half, row):
        block = jnp.where(half == 0, rows[0, :, lanes], rows[1, :, lanes])
        return jnp.sum(jnp.where(numbers == row, block, 0.0), 0, keepdims=True)

    parts = []
    lanes = pl.ds(pl.multiple_of((lax.rem(head, 8) // 2) * 128, 128), 128)
    for part in range(3):
        row = part * 2 + head // 8
        pair = pick(row // 3, 6 + lax.rem(row, 3))
        parts.append(jnp.where(lax.rem(head, 2) == 0, pair[:, 0:64], pair[:, 64:128]))
    lanes = pl.ds(pl.multiple_of(lax.rem(head, 4) * 128, 128), 128)
    biases[0:1, :] = jnp.concatenate(parts + [jnp.zeros_like(parts[0])], 1)
    for half in range(2):
        biases[1:2, half * 128 : (half + 1) * 128] = pick(half, 9 + head // 4)
    biases[2:8, :] = jnp.zeros((6, 256), jnp.float32)


def join_parameters(at, tall, tall_other, vector, vector_other):
    size = tall.shape[0]
    f32, bf16 = jnp.float32, jnp.bfloat16
    return pl.pallas_call(
        join_kernel,
        in_specs=[SMEM] + [VMEM] * 4,
        out_specs=[VMEM] * 7,
        out_shape=[
            shaped((2 * size, 256), bf16),
            shaped((2 * size, 256), bf16),
            shaped((512, 2 * size), bf16),
            shaped((512, 2 * size), bf16),
            shaped((8, 2 * size), f32),
            shaped((1, 2 * size), f32),
            shaped((8, 256), f32),
        ],
        scratch_shapes=[pltpu.VMEM((2, 16, 512), f32)],
        cost_estimate=cost(flops=0, bytes_accessed=8 * MIB, transcendentals=0),
        name="join_parameters",
    )(at, tall, tall_other, vector, vector_other)


def tables(angle_rows):
    lanes = jnp.arange(128) % 64
    inverse = jnp.power(10000.0, -2.0 * (lanes % (ROT // 2)).astype(jnp.float32) / ROT)
    angles = angle_rows.astype(jnp.float32)[:, None] * jnp.where(lanes < ROT, inverse, 0.0)[None, :]
    return jnp.cos(angles), jnp.sin(angles)


def turn_kernel(blocks, joint, cos_far, sin_far, cos_near, sin_near, _, q_out, k_out, v_out):
    rows = joint.shape[0]
    lanes = lax.broadcasted_iota(jnp.int32, (BLOCK, 128), 1)

    def sort(s, _):
        p = blocks[s]
        source = pl.ds(pl.multiple_of(s * BLOCK, BLOCK), BLOCK)
        target = pl.ds(pl.multiple_of(p * BLOCK, BLOCK), BLOCK)
        far = pl.ds(p, 1)
        cosine = cos_far[far, :] * cos_near[...] - sin_far[far, :] * sin_near[...]
        sine = sin_far[far, :] * cos_near[...] + cos_far[far, :] * sin_near[...]
        pair = joint[source, 0:128]
        pair = pair * cosine + turn_back(pair, lanes) * sine
        q_out[target, :] = pair[:, 0:64].astype(jnp.bfloat16)
        k_out[target, :] = pair[:, 64:128].astype(jnp.bfloat16)
        v_out[target, :] = joint[source, 128:192].astype(jnp.bfloat16)
        return 0

    lax.fori_loop(0, rows // BLOCK, sort, 0, unroll=4)


def turn(blocks, joint, angles, gate):
    rows = joint.shape[0]
    head = shaped((rows, 64), jnp.bfloat16)
    return pl.pallas_call(
        turn_kernel,
        in_specs=[SMEM] + [VMEM] * 5 + [ANY],
        out_specs=[VMEM] * 3,
        out_shape=[head] * 3,
        compiler_params=pltpu.CompilerParams(vmem_limit_bytes=40 * MIB),
        cost_estimate=cost(flops=0, bytes_accessed=rows * 2048, transcendentals=0),
        name="rotary_and_sort",
    )(blocks, joint, *angles, gate)


def below_diagonal():
    return lax.broadcasted_iota(jnp.int32, (TILE, TILE), 0) <= lax.broadcasted_iota(
        jnp.int32, (TILE, TILE), 1
    )


def forward_kernel(index, slots, q, k, v, *refs):
    mixed_out, out, lse = refs[-5:-2]
    buffer, sems = refs[-2:]
    tiles = q.shape[0] // TILE
    below = below_diagonal()
    parts = TILE // BLOCK
    copies = []
    for which, i in enumerate((index, tiles - 1 - index)):
        query = q[i * TILE : (i + 1) * TILE, :] * jnp.bfloat16(0.125)

        def step(j, carry, masked):
            top, total, acc = carry
            there = pl.ds(pl.multiple_of(j * TILE, TILE), TILE)
            scores = nt(k[there, :], query)
            if masked:
                scores = jnp.where(below, scores, negative)
            new_top = jnp.maximum(top, jnp.max(scores, 0, keepdims=True))
            weights = jnp.exp(scores - new_top)
            keep = jnp.exp(top - new_top)
            total = total * keep + jnp.sum(weights, 0, keepdims=True)
            return new_top, total, acc * keep + tn(v[there, :], weights.astype(jnp.bfloat16))

        carry = (
            jnp.full((1, TILE), negative, jnp.float32),
            jnp.zeros((1, TILE), jnp.float32),
            jnp.zeros((64, TILE), jnp.float32),
        )
        carry = lax.fori_loop(0, i, lambda j, c: step(j, c, False), carry, unroll=True)
        top, total, acc = step(i, carry, True)
        acc = acc / total
        here = slice(which * TILE, (which + 1) * TILE)
        out[:, here] = acc
        lse[:, here] = top + jnp.log(total)
        buffer[here, :] = acc.T.astype(jnp.bfloat16)
        for part in range(parts):
            slot = slots[i * parts + part]
            copies.append(
                pltpu.make_async_copy(
                    buffer.at[pl.ds(which * TILE + part * BLOCK, BLOCK)],
                    mixed_out.at[pl.ds(pl.multiple_of(slot * BLOCK, BLOCK), BLOCK)],
                    sems.at[which * parts + part],
                )
            )
            copies[-1].start()
    for copy in copies:
        copy.wait()


def attention_forward(index, slots, q, k, v, mixed, gate):
    rows = q.shape[0]
    extra = ([] if mixed is None else [mixed]) + ([] if gate is None else [gate])
    return pl.pallas_call(
        functools.partial(forward_kernel, index),
        in_specs=[SMEM] + [VMEM] * 3 + [ANY] * len(extra),
        out_specs=[ANY, VMEM, VMEM],
        out_shape=[
            shaped((rows, 64), jnp.bfloat16),
            shaped((64, 2 * TILE), jnp.float32),
            shaped((1, 2 * TILE), jnp.float32),
        ],
        scratch_shapes=[
            pltpu.VMEM((2 * TILE, 64), jnp.bfloat16),
            pltpu.SemaphoreType.DMA((2 * TILE // BLOCK,)),
        ],
        input_output_aliases={} if mixed is None else {4: 0},
        compiler_params=pltpu.CompilerParams(vmem_limit_bytes=40 * MIB),
        cost_estimate=cost(
            flops=rows * rows * 256, bytes_accessed=rows * 1024, transcendentals=rows * rows // 8
        ),
        name="attention_forward",
    )(slots, q, k, v, *extra)


def fold(values):
    size = values.shape[0] // 4
    return jnp.concatenate([values[i * size : (i + 1) * size] for i in range(4)], 1)


def norm_rows(weight, grad, total, gain, shift):
    weight = weight.astype(jnp.float32)
    shift_grad = jnp.dot(total, weight, precision=lax.Precision.HIGHEST)
    gain_grad = (jnp.sum(weight * grad, 0, keepdims=True) - shift * shift_grad) / gain
    return jnp.concatenate([gain_grad, shift_grad], 0)


def post_kernel(pieces, last, group, *refs):
    blocks = refs[:pieces]
    slope, active, mixed, normed, shrink, dense, expand_t, norms = refs[pieces : pieces + 8]
    if last:
        before = refs[pieces + 10 : pieces + 15]
        kept, sent, norm_grads = refs[-4:-1]
        delta, mixed_grad, *sums = refs[-11:-4]
    else:
        delta, mixed_grad, *sums = refs[-8:-1]
    shrink_grad, dense_grad, expand_grad, column, delta_sum = sums
    held = refs[-1]
    step = pl.program_id(0)
    for n in range(pieces):

        @pl.when(step == n)
        def _(n=n):
            held[...] = blocks[n][...]

    @pl.when(step == 0)
    def _():
        for n, total in enumerate(sums):
            total[...] = before[n][...] if last else jnp.zeros_like(total)

    grad = held[...]
    column[...] += jnp.sum(grad.astype(jnp.float32), 0, keepdims=True)
    rounded = (nt(grad, shrink[...]) * slope[...]).astype(jnp.bfloat16)
    delta[...] = rounded
    delta_sum[...] += jnp.sum(rounded.astype(jnp.float32), 0, keepdims=True)
    mixed_grad[...] = nt(grad, dense[...]).astype(jnp.bfloat16)
    shrink_grad[...] += tn(active[...], grad)
    dense_grad[...] += tn(mixed[...], grad)
    expand_grad[...] += tn(rounded, normed[...])
    if not last:
        return

    @pl.when(step == pieces - 1)
    def _():
        half = expand_grad.shape[1] // 2
        this = group[0]
        across = expand_grad[...].T
        low, high = fold(across[:half]), fold(across[half:])
        kept[0:128, :] = shrink_grad[pl.ds(pl.multiple_of(this * 128, 128), 128), :]
        kept[128:192, :] = dense_grad[...]
        kept[192:320, :] = jnp.where(this == 0, low, high)
        other_rows = pl.ds(pl.multiple_of((1 - this) * 128, 128), 128)
        sent[0:128, :] = shrink_grad[other_rows, :].astype(jnp.bfloat16)
        sent[128:192, :] = dense_grad[...].astype(jnp.bfloat16)
        sent[192:320, :] = jnp.where(this == 0, high, low).astype(jnp.bfloat16)
        norm_grads[...] = norm_rows(
            expand_t[...], expand_grad[...], delta_sum[...], norms[2:3, :], norms[3:4, :]
        )


def post(group, blocks, first, before, slope, active, mixed, normed, shrink, dense, expand_t, norms):
    count = len(blocks)
    rows, width = blocks[0].shape
    total = slope.shape[0]
    last = before is not None
    row = lambda cols: pl.BlockSpec((rows, cols), lambda i: (first + i, 0))
    fixed = lambda shape: pl.BlockSpec(shape, lambda i: (0, 0))
    f32, bf16 = jnp.float32, jnp.bfloat16
    constants = (shrink, dense, expand_t, norms)
    sums = [(256, width), (64, width), (256, width), (1, width), (1, 256)]
    ends = [((320, width), f32), ((320, width), bf16), ((2, width), f32)] if last else []
    return pl.pallas_call(
        functools.partial(post_kernel, count, last),
        grid=(count,),
        in_specs=[SMEM]
        + [VMEM] * count
        + [row(256), row(256), row(64), row(width)]
        + [fixed(v.shape) for v in constants]
        + ([ANY] * 2 + [fixed(v) for v in sums] if last else []),
        out_specs=[row(256), row(64)]
        + [fixed(v) for v in sums]
        + [fixed(shape) for shape, _ in ends],
        out_shape=[shaped((total, 256), bf16), shaped((total, 64), bf16)]
        + [shaped(v, f32) for v in sums]
        + [shaped(*end) for end in ends],
        scratch_shapes=[pltpu.VMEM((rows, width), bf16)],
        input_output_aliases={count + 9: 0, count + 10: 1} if last else {},
        compiler_params=pltpu.CompilerParams(vmem_limit_bytes=44 * MIB),
        cost_estimate=cost(
            flops=rows * count * width * 1800,
            bytes_accessed=rows * count * width * 6,
            transcendentals=0,
        ),
        name="cotangent_products",
    )(group, *blocks, slope, active, mixed, normed, *constants, *(before or ()))


def joint_products_kernel(group, normed, delta, joint_t, total, norms, kept, sent, norm_grads, acc):
    step = pl.program_id(0)

    @pl.when(step == 0)
    def _():
        acc[...] = jnp.zeros_like(acc)

    acc[...] += tn(delta[...], normed[...])

    @pl.when(step == pl.num_programs(0) - 1)
    def _():
        across = acc[...].T
        half = across.shape[0] // 2
        low, high = across[:half], across[half:]
        kept[...] = jnp.where(group[0] == 0, low, high)
        sent[...] = jnp.where(group[0] == 0, high, low).astype(jnp.bfloat16)
        norm_grads[...] = norm_rows(
            joint_t[...], acc[...], total[...], norms[0:1, :], norms[1:2, :]
        )


def joint_products(group, normed, delta, joint_t, total, norms):
    rows, width = normed.shape
    size = 1024
    row = lambda cols: pl.BlockSpec((size, cols), lambda i: (i, 0))
    fixed = lambda shape: pl.BlockSpec(shape, lambda i: (0, 0))
    f32, bf16 = jnp.float32, jnp.bfloat16
    return pl.pallas_call(
        joint_products_kernel,
        grid=(rows // size,),
        in_specs=[SMEM, row(width), row(256)] + [fixed(v.shape) for v in (joint_t, total, norms)],
        out_specs=[fixed((width // 2, 256)), fixed((width // 2, 256)), fixed((2, width))],
        out_shape=[
            shaped((width // 2, 256), f32),
            shaped((width // 2, 256), bf16),
            shaped((2, width), f32),
        ],
        scratch_shapes=[pltpu.VMEM((256, width), f32)],
        compiler_params=pltpu.CompilerParams(vmem_limit_bytes=40 * MIB),
        cost_estimate=cost(
            flops=rows * width * 512, bytes_accessed=rows * width * 3, transcendentals=0
        ),
        name="joint_products",
    )(group, normed, delta, joint_t, total, norms)


def pair_kernel(core, mine, received, vectors, out):
    here = mine[pl.ds(pl.multiple_of(core[0] * 256, 256), 256), :]
    there = received[...]
    low = jnp.where(core[0] == 0, here, there)
    high = jnp.where(core[0] == 0, there, here)
    for part in range(3):
        lanes = slice(part * 64, part * 64 + 64)
        out[0:256, part * 128 : part * 128 + 128] = jnp.concatenate(
            [low[:, lanes], high[:, lanes]], 1
        )
    out[256:272, 0:256] = vectors[...]
    out[256:272, 256:384] = jnp.zeros((16, 128), out.dtype)


def pair_heads(core, mine, received, vectors):
    return pl.pallas_call(
        pair_kernel,
        in_specs=[SMEM] + [VMEM] * 3,
        out_specs=VMEM,
        out_shape=shaped((272, 384), jnp.bfloat16),
        cost_estimate=cost(flops=0, bytes_accessed=1 << 20, transcendentals=0),
        name="pair_heads",
    )(core, mine, received, vectors)


def sort_grad_kernel(tiles, slots, mixed_grad, *refs):
    outs = refs[:tiles]
    grad, inner = refs[-2:]
    per_tile = TILE // BLOCK

    for p in range(slots.shape[0]):
        tile, part = divmod(p, per_tile)
        column = part * BLOCK
        if tile >= tiles:
            tile, column = 2 * tiles - 1 - tile, column + TILE
        source = pl.ds(pl.multiple_of(slots[p] * BLOCK, BLOCK), BLOCK)
        piece = mixed_grad[source, :]
        here = slice(p * BLOCK, (p + 1) * BLOCK)
        grad[here, :] = piece
        flat = piece.astype(jnp.float32).T
        inner[:, here] = jnp.sum(
            flat * outs[tile][:, column : column + BLOCK], 0, keepdims=True
        )


def sort_grad(slots, mixed_grad, outs):
    rows = mixed_grad.shape[0]
    return pl.pallas_call(
        functools.partial(sort_grad_kernel, len(outs)),
        in_specs=[SMEM] + [VMEM] * (1 + len(outs)),
        out_specs=[VMEM] * 2,
        out_shape=[shaped((rows, 64), jnp.bfloat16), shaped((1, rows), jnp.float32)],
        compiler_params=pltpu.CompilerParams(vmem_limit_bytes=40 * MIB),
        cost_estimate=cost(flops=0, bytes_accessed=rows * 1024, transcendentals=0),
        name="sort_gradient",
    )(slots, mixed_grad, *outs)


def backward_kernel(index, first, q, k, v, grad, inner, lse, *refs):
    dq, dk, dv = refs[-3:]
    tiles = q.shape[0] // TILE
    below = below_diagonal()
    if first:
        dq[...] = jnp.zeros_like(dq)
    else:
        dq[...] = refs[0][...]
    for which, j in enumerate((index, tiles - 1 - index)):
        key = k[j * TILE : (j + 1) * TILE, :]
        value = v[j * TILE : (j + 1) * TILE, :]

        def step(i, carry, masked):
            key_grad, value_grad = carry
            here = pl.ds(pl.multiple_of(i * TILE, TILE), TILE)
            query = q[here, :] * jnp.bfloat16(0.125)
            out_grad = grad[here, :]
            probs = jnp.exp(nt(key, query) - lse[:, here])
            if masked:
                probs = jnp.where(below, probs, 0.0)
            score_grad = (probs * (nt(value, out_grad) - inner[:, here])).astype(jnp.bfloat16)
            value_grad = value_grad + nn(probs.astype(jnp.bfloat16), out_grad)
            key_grad = key_grad + nn(score_grad, query)
            dq[:, here] += tn(key, score_grad)
            return key_grad, value_grad

        zero = jnp.zeros((TILE, 64), jnp.float32)
        carry = step(j, (zero, zero), True)
        key_grad, value_grad = lax.fori_loop(
            j + 1, tiles, lambda i, c: step(i, c, False), carry, unroll=True
        )
        here = slice(which * TILE, (which + 1) * TILE)
        dk[here, :] = key_grad
        dv[here, :] = value_grad


def attention_backward(index, q, k, v, grad, inner, lse, dq, gate):
    rows = q.shape[0]
    extra = ([] if dq is None else [dq]) + ([] if gate is None else [gate])
    specs = ([] if dq is None else [VMEM]) + ([] if gate is None else [ANY])
    return pl.pallas_call(
        functools.partial(backward_kernel, index, dq is None),
        in_specs=[VMEM] * 6 + specs,
        out_specs=[VMEM] * 3,
        out_shape=[
            shaped((64, rows), jnp.float32),
            shaped((2 * TILE, 64), jnp.float32),
            shaped((2 * TILE, 64), jnp.float32),
        ],
        compiler_params=pltpu.CompilerParams(vmem_limit_bytes=40 * MIB),
        cost_estimate=cost(
            flops=rows * rows * 640, bytes_accessed=rows * 2048, transcendentals=rows * rows // 8
        ),
        name="attention_backward",
    )(q, k, v, grad, inner, lse, *extra)


def finish_kernel(tiles, slots, dq, expand_delta, cos_far, sin_far, cos_near, sin_near, *refs):
    key_grads, value_grads = refs[:tiles], refs[tiles : 2 * tiles]
    delta, total = refs[-2:]
    delta[:, 256:512] = expand_delta[...]
    lanes = lax.broadcasted_iota(jnp.int32, (BLOCK, 128), 1)
    per_tile = TILE // BLOCK
    total[...] = jnp.zeros_like(total)
    for p in range(slots.shape[0]):
        tile, part = divmod(p, per_tile)
        row = part * BLOCK
        if tile >= tiles:
            tile, row = 2 * tiles - 1 - tile, row + TILE
        target = pl.ds(pl.multiple_of(slots[p] * BLOCK, BLOCK), BLOCK)
        cosine = cos_far[p : p + 1, :] * cos_near[...] - sin_far[p : p + 1, :] * sin_near[...]
        sine = sin_far[p : p + 1, :] * cos_near[...] + cos_far[p : p + 1, :] * sin_near[...]
        query = dq[:, p * BLOCK : (p + 1) * BLOCK].T * 0.125
        pair = jnp.concatenate([query, key_grads[tile][row : row + BLOCK, :]], 1)
        pair = (pair * cosine - turn_back(pair, lanes) * sine).astype(jnp.bfloat16)
        value = value_grads[tile][row : row + BLOCK, :]
        last = jnp.concatenate([value, jnp.zeros_like(value)], 1).astype(jnp.bfloat16)
        delta[target, 0:128] = pair
        delta[target, 128:256] = last
        total[:, 0:128] += jnp.sum(pair.astype(jnp.float32), 0, keepdims=True)
        total[:, 128:256] += jnp.sum(last.astype(jnp.float32), 0, keepdims=True)


def finish(slots, dq, expand_delta, angles, key_grads, value_grads):
    rows = dq.shape[1]
    return pl.pallas_call(
        functools.partial(finish_kernel, len(key_grads)),
        in_specs=[SMEM] + [VMEM] * (6 + 2 * len(key_grads)),
        out_specs=[VMEM] * 2,
        out_shape=[shaped((rows, 512), jnp.bfloat16), shaped((1, 256), jnp.float32)],
        compiler_params=pltpu.CompilerParams(vmem_limit_bytes=40 * MIB),
        cost_estimate=cost(flops=0, bytes_accessed=rows * 2048, transcendentals=0),
        name="joint_delta",
    )(slots, dq, expand_delta, *angles, *key_grads, *value_grads)


def pair_kernel_rows(own, partner, _, out):
    size = own.shape[0]
    out[:size, :] = own[...]
    out[size:, :] = partner[...]


def pair_up(own, partner, gate):
    rows, width = own.shape
    return pl.pallas_call(
        pair_kernel_rows,
        in_specs=[VMEM, VMEM, ANY],
        out_specs=VMEM,
        out_shape=shaped((2 * rows, width), own.dtype),
        cost_estimate=cost(flops=0, bytes_accessed=rows * width * 8, transcendentals=0),
        name="pair_of_pieces",
    )(own, partner, gate)


def first_kernel(pair, *refs):
    refs[-1][...] = pair[...]


def first_piece(pair, *gates):
    rows, width = pair.shape[0] // 2, pair.shape[1]
    block = pl.BlockSpec((rows, width), lambda i: (0, 0))
    return pl.pallas_call(
        first_kernel,
        grid=(1,),
        in_specs=[block] + [ANY] * len(gates),
        out_specs=block,
        out_shape=shaped((rows, width), pair.dtype),
        cost_estimate=cost(flops=0, bytes_accessed=rows * width * 4, transcendentals=0),
        name="first_piece",
    )(pair, *gates)


def sum_kernel(kept, received, _, out):
    out[...] = (kept[...] + received[...].astype(jnp.float32)).astype(out.dtype)


def sum_pieces(kept, received, gate):
    rows, width = kept.shape
    return pl.pallas_call(
        sum_kernel,
        in_specs=[VMEM, VMEM, ANY],
        out_specs=VMEM,
        out_shape=shaped((rows, width), jnp.bfloat16),
        cost_estimate=cost(flops=0, bytes_accessed=rows * width * 8, transcendentals=0),
        name="sum_of_pieces",
    )(kept, received, gate)


def last_kernel(values, weight, held, *refs):
    own, sent = refs[-2:]
    rows = own.shape[0]
    own[...] = nn(values[:rows, :], weight[...]) + held[rows:, :].astype(jnp.float32)
    term = nn(values[rows:, :], weight[...]) + held[:rows, :].astype(jnp.float32)
    sent[...] = term.astype(jnp.bfloat16)


def scatter_last(values, weight, held, *gates):
    rows, width = held.shape[0] // 2, held.shape[1]
    depth = values.shape[1]
    fixed = lambda shape: pl.BlockSpec(shape, lambda i: (0, 0))
    return pl.pallas_call(
        last_kernel,
        grid=(1,),
        in_specs=[fixed((2 * rows, depth)), fixed(weight.shape), fixed(held.shape)]
        + [ANY] * len(gates),
        out_specs=[fixed((rows, width))] * 2,
        out_shape=[shaped((rows, width), jnp.float32), shaped((rows, width), jnp.bfloat16)],
        cost_estimate=cost(
            flops=4 * rows * depth * width, bytes_accessed=rows * width * 10, transcendentals=0
        ),
        name="last_sums",
    )(values, weight, held, *gates)


def input_grad_kernel(tokens, upstream, own, received, *refs):
    out = refs[-1]
    x = tokens[...].astype(jnp.float32)
    x = x - jnp.mean(x, -1, keepdims=True)
    scale = lax.rsqrt(jnp.mean(x * x, -1, keepdims=True) + epsilon)
    x = x * scale
    grad = own[...] + received[...].astype(jnp.float32)
    term = grad - jnp.mean(grad, -1, keepdims=True) - x * jnp.mean(grad * x, -1, keepdims=True)
    out[...] = (upstream[...].astype(jnp.float32) + scale * term).astype(out.dtype)


def input_grad(tokens, upstream, own, received, *gates):
    rows, width = tokens.shape
    return pl.pallas_call(
        input_grad_kernel,
        in_specs=[VMEM] * 4 + [ANY] * len(gates),
        out_specs=VMEM,
        out_shape=shaped((rows, width), jnp.bfloat16),
        cost_estimate=cost(flops=0, bytes_accessed=rows * width * 12, transcendentals=0),
        name="input_gradient",
    )(tokens, upstream, own, received, *gates)


def assemble_kernel(owners, first, second, *refs):
    shrink, dense, expand, mark = refs[-7:-3]
    wide, tall, sems = refs[-3:]
    mark[...] = jnp.zeros_like(mark)
    group = owners[4]
    hidden = expand.shape[1] // 2
    size = first.shape[0] // 2

    def dense_copy(n):
        return pltpu.make_async_copy(
            wide.at[n, pl.ds(128, 64)],
            dense.at[pl.ds(pl.multiple_of(lax.rem(owners[n], 8) * 64, 64), 64)],
            sems.at[n, 3],
        )

    copies = []
    for n in range(4):
        blob = (first, second)[n // 2]
        top = (n % 2) * size
        wide[n] = blob[top : top + 192, :].astype(jnp.float32)
        start = pl.multiple_of(owners[n] * 128, 128)
        copies.append(
            pltpu.make_async_copy(
                wide.at[n, pl.ds(0, 128)], shrink.at[pl.ds(start, 128)], sems.at[n, 0]
            )
        )
        copies[-1].start()

        @pl.when(owners[n] // 8 == group)
        def _(n=n):
            dense_copy(n).start()

        for quarter in range(4):
            tall[n, quarter * 128 : (quarter + 1) * 128, :] = blob[
                top + 192 : top + 320, quarter * 256 : (quarter + 1) * 256
            ].astype(jnp.float32)
        copies += [
            pltpu.make_async_copy(
                tall.at[n, :, pl.ds(0, 128)], expand.at[:, pl.ds(start, 128)], sems.at[n, 1]
            ),
            pltpu.make_async_copy(
                tall.at[n, :, pl.ds(128, 128)],
                expand.at[:, pl.ds(pl.multiple_of(hidden + start, 128), 128)],
                sems.at[n, 2],
            ),
        ]
        for copy in copies[-2:]:
            copy.start()
    for copy in copies:
        copy.wait()
    for n in range(4):

        @pl.when(owners[n] // 8 == group)
        def _(n=n):
            dense_copy(n).wait()


def assemble(owners, first, second, shapes, outs, *gates):
    return pl.pallas_call(
        assemble_kernel,
        in_specs=[SMEM, VMEM, VMEM] + [ANY] * ((0 if outs is None else 3) + len(gates)),
        out_specs=[ANY] * 3 + [VMEM],
        out_shape=[shaped(s, jnp.float32) for s in (*shapes, (8, 128))],
        scratch_shapes=[
            pltpu.VMEM((4, 192, 1024), jnp.float32),
            pltpu.VMEM((4, 512, 256), jnp.float32),
            pltpu.SemaphoreType.DMA((4, 4)),
        ],
        input_output_aliases={} if outs is None else {3 + i: i for i in range(3)},
        compiler_params=pltpu.CompilerParams(vmem_limit_bytes=24 * MIB),
        cost_estimate=cost(flops=0, bytes_accessed=1280 * 6144, transcendentals=0),
        name="place_gradients",
    )(owners, first, second, *(outs or ()), *gates)


def assemble_joint_kernel(count, owners, *refs):
    blobs = refs[:count]
    joint, norm_sums, joint_bias, expand_bias, held, buffer, sems, arrivals = refs[count:]
    group = owners[2 * count]
    norm_sums[...] = jnp.zeros_like(norm_sums)
    width = joint.shape[1] // 3
    size = blobs[0].shape[0] // 2
    fetches = [
        pltpu.make_async_copy(blobs[n], held.at[n], arrivals.at[n]) for n in range(count)
    ]
    for fetch in fetches:
        fetch.start()
    copies = []
    for n in range(2 * count):
        owner = owners[n]
        first = (n % 2) * size
        if n % 2 == 0:
            fetches[n // 2].wait()
        buffer[n] = held[n // 2, first : first + 256, :].astype(jnp.float32)
        top = pl.multiple_of(lax.rem(owner, 2) * 256, 256)
        for part in range(3):
            start = pl.multiple_of(part * width + (owner // 2) * 128, 128)
            copies.append(
                pltpu.make_async_copy(
                    buffer.at[n, :, pl.ds(part * 128, 128)],
                    joint.at[pl.ds(top, 256), pl.ds(start, 128)],
                    sems.at[n, part],
                )
            )
            copies[-1].start()
    for n in range(count):
        first = held[n, 256:272, 0:256].astype(jnp.float32)
        second = held[n, size + 256 : size + 272, 0:256].astype(jnp.float32)
        norm_sums[...] += first[0:8, :] + second[0:8, :]
        low_first = lax.rem(owners[2 * n], 2) == 0
        low = jnp.where(low_first, first[10:11, :], second[10:11, :])
        high = jnp.where(low_first, second[10:11, :], first[10:11, :])
        for part in range(3):
            lanes = slice(part * 64, part * 64 + 64)
            joint_bias[pl.ds(part * 8 + owners[2 * n] // 2, 1), :] = jnp.concatenate(
                [low[:, lanes], high[:, lanes]], 1
            )
        for piece, row in enumerate((first[11:12, :], second[11:12, :])):
            expand_bias[pl.ds(owners[2 * n + piece], 1), :] = jnp.where(
                group == 0, row[:, 0:128], row[:, 128:256]
            )
    for copy in copies:
        copy.wait()


def assemble_joint(owners, blobs, shape):
    count = len(blobs)
    return pl.pallas_call(
        functools.partial(assemble_joint_kernel, count),
        in_specs=[SMEM] + [ANY] * count,
        out_specs=[ANY] + [VMEM] * 3,
        out_shape=[
            shaped(shape, jnp.float32),
            shaped((8, 256), jnp.float32),
            shaped((24, 128), jnp.float32),
            shaped((16, 128), jnp.float32),
        ],
        scratch_shapes=[
            pltpu.VMEM((count, *blobs[0].shape), jnp.bfloat16),
            pltpu.VMEM((2 * count, 256, 384), jnp.float32),
            pltpu.SemaphoreType.DMA((2 * count, 3)),
            pltpu.SemaphoreType.DMA((count,)),
        ],
        compiler_params=pltpu.CompilerParams(vmem_limit_bytes=40 * MIB),
        cost_estimate=cost(
            flops=0, bytes_accessed=count * 512 * 384 * 6, transcendentals=0
        ),
        name="place_joint_gradient",
    )(owners, *blobs)


def split_heads(
    tokens,
    cotangent,
    first_gain,
    first_shift,
    second_gain,
    second_shift,
    joint_weight,
    joint_bias,
    dense_weight,
    dense_bias,
    expand_weight,
    expand_bias,
    shrink_weight,
    shrink_bias,
    block_order,
):
    f32, bf16 = jnp.float32, jnp.bfloat16
    me = lax.axis_index("ctx")
    group = lax.axis_index("fsdp")
    core = me % 2
    rows, width = tokens.shape[1:]
    total_rows = rows * 16
    hidden = expand_weight.shape[1] // 2
    own_tokens, own_upstream = tokens[0], cotangent[0]


    token_pair = jnp.concatenate([own_tokens, swap(own_tokens)], 0)
    token_hops = [gather_hop(token_pair, 1)]
    at = after(me, token_pair)
    scalars = jnp.stack([at, group]).astype(jnp.int32)
    tall, flat = slice_parameters(
        scalars, joint_weight, expand_weight, shrink_weight, dense_weight
    )
    tall_other = other(tall)
    vector = stack_vectors(
        lax.optimization_barrier(
            (
                first_gain,
                first_shift,
                second_gain,
                second_shift,
                dense_bias,
                shrink_bias,
                joint_bias,
                expand_bias,
                tall,
            )
        )[:8]
    )
    joint_c, expand_c, tall_t, scaled, norms, shifts, biases = join_parameters(
        scalars, tall, tall_other, vector, other(vector)
    )
    flat_other = other(after(flat, tall_other))
    shrink_pair = [jnp.where(group == i, flat[:128], flat_other[:128]) for i in range(2)]
    shrink_c = jnp.concatenate(shrink_pair, 0)
    dense_c = jnp.where(group == me // 8, flat[128:], flat_other[128:])

    owners = piece_owners(at)
    blocks = after(block_order, token_pair).reshape(16, 2)[owners].reshape(32)
    count = jnp.arange(32, dtype=jnp.int32)
    slots = jnp.sum(jnp.where(blocks[None, :] == count[:, None], count[None, :], 0), 1)
    near = after(jnp.arange(BLOCK), token_pair)
    angles = tables(jnp.arange(total_rows // BLOCK) * BLOCK) + tables(near)

    normal, flags = None, []

    def take(block):
        nonlocal normal
        *normal, flag = pre(
            len(flags), block, norms, joint_c, biases, expand_c, normal, 8
        )
        flags.append(flag)

    def far_pair(far):
        return jnp.concatenate([far, swap(far)], 0)

    take(token_pair)
    token_hops.append(gather_hop(token_hops[0], 2, tall, vector))
    take(token_hops[0])
    take(swap(token_hops[0]))
    token_hops.append(gather_hop(token_hops[1], 3, flags[0]))
    take(token_hops[1])
    take(swap(token_hops[1]))
    token_hops.append(gather_hop(token_hops[2], 4, flags[3]))
    upstream_pair = jnp.concatenate([own_upstream, swap(after(own_upstream, flags[0]))], 0)
    upstream_hops = [gather_hop(upstream_pair, 1, token_hops[2], flags[3])]
    take(token_hops[2])
    take(swap(token_hops[2]))
    take(far_pair(token_hops[3]))
    normed_one, normed_two, joint, activated, slope = normal
    query, key, value = turn(blocks, joint, angles, upstream_hops[0])

    mixed, outs, sums = None, [], []

    def attend(index, gate):
        nonlocal mixed
        mixed, out, lse = attention_forward(index, slots, query, key, value, mixed, gate)
        outs.append(out)
        sums.append(lse)

    upstream_hops.append(gather_hop(upstream_hops[0], 2, flags[6]))
    attend(0, None)
    upstream_hops.append(gather_hop(upstream_hops[1], 3, query))
    attend(1, upstream_hops[1])
    attend(2, upstream_hops[1])
    upstream_hops.append(gather_hop(upstream_hops[2], 4, sums[0]))
    attend(3, upstream_hops[2])
    upstream_blocks = [upstream_pair]
    for held in upstream_hops[:3]:
        upstream_blocks += [held, swap(held)]
    upstream_blocks.append(far_pair(upstream_hops[3]))
    lse = jnp.concatenate(
        [s[:, :TILE] for s in sums] + [s[:, TILE:] for s in sums[::-1]], 1
    )

    branch = jnp.concatenate([activated, mixed], 1)
    back = jnp.concatenate([shrink_c, dense_c], 0)
    this = group[None].astype(jnp.int32)

    def products(blocks, first, before, normed):
        return post(
            this,
            blocks,
            first,
            before,
            slope,
            activated,
            mixed,
            normed,
            shrink_c,
            dense_c,
            tall_t[256:],
            norms,
        )

    early = products(upstream_blocks[:4], 0, None, normed_two)
    out_hops = [hop(after(scatter_term(branch, back, 4), upstream_hops[3]))]
    term = scatter_term(branch, back, 3, out_hops[0])
    out_hops.append(hop(term))
    expand_delta, mixed_grad, _, _, _, column_sum, expand_sum, kept, sent, norm_two = products(
        upstream_blocks[4:], 4, early, after(normed_two, term)
    )
    term = scatter_term(branch, back, 2, out_hops[1])
    out_hops.append(hop(after(term, expand_sum)))
    out_grad, inner = sort_grad(slots, after(mixed_grad, term), outs)
    blob_other = other(sent)

    dq, key_grads, value_grads = None, [], []

    def attend_back(index, gate):
        nonlocal dq
        dq, dk, dv = attention_backward(
            index, query, key, value, out_grad, inner, lse, dq, gate
        )
        key_grads.append(dk)
        value_grads.append(dv)

    attend_back(0, term)
    attend_back(1, term)
    term = scatter_term(branch, back, 1, out_hops[2])
    out_hops.append(hop(after(term, key_grads[0])))
    blob = (kept + after(blob_other, key_grads[0]).astype(f32)).astype(bf16)
    blob_pair = jnp.concatenate([blob, swap(blob)], 0)
    blob_hops = [gather_hop(blob_pair, 1, out_hops[2])]
    attend_back(2, term)
    out_rows = nn(branch[: 2 * rows], back)
    out_sent = out_rows[rows:] + out_hops[3][:rows].astype(f32)
    out_sum = out_rows[:rows] + out_hops[3][rows:].astype(f32)
    out_sum = out_sum + swap(out_sent.astype(bf16)).astype(f32)
    output = own_tokens.astype(f32) + out_sum + shifts
    attend_back(3, out_hops[3])
    blob_hops.append(gather_hop(blob_hops[0], 2))
    delta, joint_sum = finish(slots, dq, expand_delta, angles, key_grads, value_grads)

    far_term = scatter_term(delta, scaled, 4)
    in_hops = [hop(far_term)]
    in_hops.append(hop(scatter_term(delta, scaled, 3, in_hops[0])))
    joint_kept, joint_sent, norm_one = joint_products(
        this, after(normed_one, in_hops[0]), delta, tall_t[:256], joint_sum, norms
    )

    def rows_of(which):
        norm_part = jnp.concatenate([norm_one, norm_two], 0).reshape(4, 2, 2, 256)
        column_part = column_sum.reshape(2, 2, 256)
        return jnp.concatenate(
            [
                cut(norm_part, which, 1, 1).reshape(8, 256),
                cut(column_part, which, 1, 0).reshape(2, 256),
                joint_sum,
                expand_sum,
                jnp.zeros((4, 256), f32),
            ],
            0,
        )

    sent = jnp.concatenate([joint_sent, rows_of(1 - group).astype(bf16)], 0)
    received = other(sent).astype(f32)
    half = width // 2
    packed = rows_of(group) + received[half:]
    joint_half = (joint_kept + received[:half]).astype(bf16)
    exchanged = swap(cut(joint_half, (1 - core) * (half // 2), half // 2, 0))
    joint_blob = pair_heads(
        core[None].astype(jnp.int32), joint_half, exchanged, packed.astype(bf16)
    )
    joint_pair = jnp.concatenate([joint_blob, swap(joint_blob)], 0)

    placed, marks = None, []
    shapes = ((hidden, width), (half, width), (half, 2 * hidden))

    def place(first, second, *gates):
        nonlocal placed
        some = owners[4 * len(marks) : 4 * len(marks) + 4]
        *placed, mark = assemble(
            jnp.concatenate([some, this]).astype(jnp.int32), first, second, shapes, placed, *gates
        )
        marks.append(mark)

    blob_hops.append(gather_hop(blob_hops[1], 3))
    place(blob_pair, blob_hops[0], in_hops[0])
    place(swap(blob_hops[0]), blob_hops[1], in_hops[0])
    joint_hops = [gather_hop(joint_pair, 1)]
    in_hops.append(hop(scatter_term(delta, scaled, 2, in_hops[1])))
    blob_hops.append(hop(first_piece(blob_hops[2], marks[1])))
    joint_hops.append(gather_hop(joint_hops[0], 2))
    place(swap(blob_hops[1]), blob_hops[2])
    in_hops.append(hop(scatter_term(delta, scaled, 1, in_hops[2])))
    joint_hops.append(gather_hop(joint_hops[1], 3))
    joint_hops.append(hop(first_piece(joint_hops[2], marks[1])))
    place(swap(blob_hops[2]), far_pair(blob_hops[3]))
    shrink_total, dense_total, expand_total = placed
    joint_blocks = [joint_pair]
    for held in joint_hops[:3]:
        joint_blocks += [held, swap(held)]
    joint_blocks.append(far_pair(joint_hops[3]))
    joint_total, norm_sums, joint_bias_sums, expand_bias_sums = assemble_joint(
        jnp.concatenate([owners, this]).astype(jnp.int32), joint_blocks, (half, 3 * width)
    )
    in_own, in_sent = scatter_last(delta, scaled, in_hops[3])
    tokens_grad = input_grad(
        own_tokens, own_upstream, in_own, swap(in_sent), norm_sums, marks[3]
    )
    totals = norm_sums.reshape(4, half)
    column_total = packed[8:10].reshape(-1)

    return (
        output.astype(bf16)[None],
        tokens_grad[None],
        totals[0],
        totals[1],
        totals[2],
        totals[3],
        joint_total,
        cut(joint_bias_sums, group * 12, 12, 0).reshape(-1),
        dense_total,
        column_total,
        expand_total,
        expand_bias_sums.reshape(-1),
        shrink_total,
        column_total,
    )


def solution(mesh):
    fits = mesh.shape["ctx"] == HEADS and mesh.shape["fsdp"] == 2
    return jax.shard_map(
        split_heads if fits else shards,
        mesh=mesh,
        in_specs=(
            P("fsdp", "ctx", None),
            P("fsdp", "ctx", None),
            P("fsdp"),
            P("fsdp"),
            P("fsdp"),
            P("fsdp"),
            P("fsdp", None),
            P("fsdp"),
            P("fsdp", None),
            P("fsdp"),
            P("fsdp", None),
            P("fsdp"),
            P("fsdp", None),
            P("fsdp"),
            P(),
        ),
        out_specs=(
            P("fsdp", "ctx", None),
            P("fsdp", "ctx", None),
            P("fsdp"),
            P("fsdp"),
            P("fsdp"),
            P("fsdp"),
            P("fsdp", None),
            P("fsdp"),
            P("fsdp", None),
            P("fsdp"),
            P("fsdp", None),
            P("fsdp"),
            P("fsdp", None),
            P("fsdp"),
        ),
        check_vma=False,
    )
```
